32 devices in a mesh: gx: 8 (over y, x, core), gy: 4 (over z).
Axes of the slice: x: 2, y: 2, z: 4, core: 2. Of those that a mesh axis runs over, the one named last changes fastest.
Arguments:
- node_latents: bfloat16 [8192, 128], P(('gx', 'gy')), may hold values from -6 to 6
- edge_latents: bfloat16 [8192, 64, 128], P(('gx', 'gy')), may hold values from -6 to 6
- node_cotangent: bfloat16 [8192, 128], P(('gx', 'gy')), may hold values from -6 to 6
- edge_cotangent: bfloat16 [8192, 64, 128], P(('gx', 'gy')), may hold values from -6 to 6
- neighbours: int32 [8192, 64], P(('gx', 'gy')), may hold values from 0 to 831, as said below
- edge_mask: int32 [8192, 64], P(('gx', 'gy')), may hold values from 0 to 1, as said below
- send_table: int32 [32, 64], P(('gx', 'gy')), may hold values from 0 to 255, as said below
- counts: int32 [32], P(('gx', 'gy')), may hold values from 85 to 256, as said below
- weights: float32 [9, 128, 128], replicated, may hold values from -0.375 to 0.375
- vectors: float32 [10, 128], replicated, may hold values from 0.1 to 1.9
- weights_m: float32 [9, 128, 128], replicated, may hold values from -0.010416667 to 0.010416667
- vectors_m: float32 [10, 128], replicated, may hold values from -0.041666668 to 0.041666668
- weights_v: float32 [9, 128, 128], replicated, may hold values from 6.781684e-06 to 2.7126736e-05
- vectors_v: float32 [10, 128], replicated, may hold values from 0.000108506945 to 0.00043402778
- weights_ema: float32 [9, 128, 128], replicated, may hold values from -0.375 to 0.375
- vectors_ema: float32 [10, 128], replicated, may hold values from 0.1 to 1.9
Outputs:
- nodes_out: bfloat16 [8192, 128], P(('gx', 'gy'))
- edges_out: bfloat16 [8192, 64, 128], P(('gx', 'gy'))
- nodes_grad: bfloat16 [8192, 128], P(('gx', 'gy'))
- edges_grad: bfloat16 [8192, 64, 128], P(('gx', 'gy'))
- grad_norm: float32 [], replicated
- weights_m_new: float32 [9, 128, 128], replicated
- vectors_m_new: float32 [10, 128], replicated
- weights_v_new: float32 [9, 128, 128], replicated
- vectors_v_new: float32 [10, 128], replicated
- weights_new: float32 [9, 128, 128], replicated
- vectors_new: float32 [10, 128], replicated
- weights_copy: bfloat16 [9, 128, 128], replicated
- vectors_copy: bfloat16 [10, 128], replicated
- weights_ema_new: float32 [9, 128, 128], replicated
- vectors_ema_new: float32 [10, 128], replicated
The draws below stay inside these ranges and needn't reach their ends.
Inputs may be any that keep to these rules, and one draw needn't show every extreme that they name: `counts`: live particles of a device are its first rows; the last device is full. `edge_mask`: slot k of a particle is live when k is below its degree; each live particle has 1 to 60 live slots, dead particles none; some particle has 60. `neighbours`: a live slot names a live own row (0 to 255) or 256 + s * 64 + j, row j of halo slot s of a device inside the grid, never the centre slot s = 4; dead slots hold 0. `send_table`: distinct live rows of the device.
All inputs are finite; a program needn't handle non-finite values.
Results may differ from the reference program's by a relative error of at most 0.008.
Values may be sent and summed in bfloat16 or wider, within the bound.
No kernel may reach another device: no remote copies, remote signals or barrier semaphores. Data moves between devices by JAX's collectives and lax.ppermute only.
A program may use at most 128 MiB of HBM per device.

```python
import math
from functools import partial
import jax
import jax.numpy as jnp
from jax import lax

TOK_DEV = 256
NBR_SLOTS = 64
MAX_DEGREE = 60
LATENT = 128
STEP = 10
HALO = 64
PARTICLES = 8192
N_GX = 8
N_GY = 4


def count_values(key):
    devices = N_GX * N_GY
    index = jnp.arange(devices, dtype=jnp.int32)
    grid_row = index // N_GY
    grid_col = index % N_GY
    least = TOK_DEV // 3
    base = least + (TOK_DEV - least) * (grid_row * (N_GY - 1) + grid_col * (N_GX - 1)) // (2 * (N_GX - 1) * (N_GY - 1))
    jitter = jax.random.randint(jax.random.fold_in(key, 101), (devices,), 0, TOK_DEV // 8 + 1)
    values = jnp.maximum(base - jitter, least)
    return jnp.where(index == devices - 1, TOK_DEV, values).astype(jnp.int32)


def degree_values(key):
    devices = N_GX * N_GY
    counts = count_values(key)
    density = jax.random.randint(jax.random.fold_in(key, 102), (devices, 1), MAX_DEGREE // 3 + 1, MAX_DEGREE + 1)
    degrees = jax.random.randint(jax.random.fold_in(key, 103), (devices, TOK_DEV), 1, density + 1)
    live = jnp.arange(TOK_DEV, dtype=jnp.int32)[None, :] < counts[:, None]
    degrees = jnp.where(live, degrees, 0)
    degrees = degrees.at[0, 0].set(MAX_DEGREE)
    return degrees.reshape(PARTICLES).astype(jnp.int32)


def draw_counts(key, part):
    return count_values(key)


def draw_edge_mask(key, part):
    degrees = degree_values(key)
    slots = jnp.arange(NBR_SLOTS, dtype=jnp.int32)[None, :]
    return (slots < degrees[:, None]).astype(jnp.int32)


def draw_neighbours(key, part):
    degrees = degree_values(key)
    counts = count_values(key)
    key = jax.random.fold_in(key, 4)
    subkeys = jax.random.split(key, 4)
    shape = (PARTICLES, NBR_SLOTS)
    device = jnp.arange(PARTICLES, dtype=jnp.int32) // TOK_DEV
    grid_row = (device // N_GY)[:, None]
    grid_col = (device % N_GY)[:, None]
    own = jax.random.randint(subkeys[0], shape, 0, counts[device][:, None])
    slot = jax.random.randint(subkeys[1], shape, 0, 9)
    entry = jax.random.randint(subkeys[2], shape, 0, HALO)
    remote = jax.random.randint(subkeys[3], shape, 0, 8) < 3
    slot_row = slot // 3 - 1 + grid_row
    slot_col = slot % 3 - 1 + grid_col
    inside = (slot_row >= 0) & (slot_row < N_GX) & (slot_col >= 0) & (slot_col < N_GY) & (slot != 4)
    index = jnp.where(remote & inside, TOK_DEV + slot * HALO + entry, own)
    used = jnp.arange(NBR_SLOTS, dtype=jnp.int32)[None, :] < degrees[:, None]
    result = jnp.where(used, index, 0)
    result = result.at[0, 1].set(TOK_DEV + 9 * HALO - 1)
    return result.astype(jnp.int32)


def draw_send_table(key, part):
    counts = count_values(key)
    key = jax.random.fold_in(key, 5)
    devices = N_GX * N_GY
    rows = jnp.arange(TOK_DEV, dtype=jnp.int32)[None, :]
    scores = jax.random.randint(key, (devices, TOK_DEV), 0, 4096) * TOK_DEV + rows
    scores = jnp.where(rows < counts[:, None], scores, 2 ** 30)
    scores = scores.at[0, 0].set(-1)
    scores = scores.at[devices - 1, TOK_DEV - 1].set(-1)
    order = jnp.argsort(scores, axis=1)
    return order[:, :HALO].astype(jnp.int32)


def block_scale(rng, extent, shards, low, top_value):
    gain = 1.0
    for dim, shards_of in shards:
        steps = jax.random.uniform(jax.random.fold_in(jax.random.fold_in(rng, 6), dim), (shards_of,), jnp.float32, low / len(shards), top_value / len(shards))
        gain = gain * jnp.repeat(jnp.exp(steps), extent[dim] // shards_of).reshape((-1,) + (1,) * (len(extent) - 1 - dim))
    return gain


def scatter_about(stream_key, shape, scale, bound, cuts=(), kind=jnp.bfloat16):
    values = jax.random.normal(stream_key, shape, jnp.float32) * scale
    if len(cuts) > 0:
        values = block_scale(stream_key, shape, cuts, -0.22, 0.18) * values
    return jnp.clip(values, min=-bound, max=bound).astype(kind)


def setup_inputs(seed: int = 0) -> dict:
    arg_keys = jax.random.split(jax.random.key(seed), 17)
    node_latents = scatter_about(arg_keys[0], (PARTICLES, LATENT), 1.0, 6.0, ((0, 32),))
    edge_latents = scatter_about(arg_keys[1], (PARTICLES, NBR_SLOTS, LATENT), 1.0, 6.0, ((0, 32),))
    node_cotangent = scatter_about(arg_keys[2], (PARTICLES, LATENT), 1.0, 6.0, ((0, 32),))
    edge_cotangent = scatter_about(arg_keys[3], (PARTICLES, NBR_SLOTS, LATENT), 1.0, 6.0, ((0, 32),))
    neighbours = draw_neighbours(jax.random.fold_in(arg_keys[16], 71), 0)
    edge_mask = draw_edge_mask(jax.random.fold_in(arg_keys[16], 71), 0)
    send_table = draw_send_table(jax.random.fold_in(arg_keys[16], 71), 0)
    counts = draw_counts(jax.random.fold_in(arg_keys[16], 71), 0)
    weights = scatter_about(arg_keys[8], (9, LATENT, LATENT), (2 * LATENT) ** -0.5, 0.375, (), jnp.float32)
    vectors = jnp.clip(1.0 + 0.18 * jax.random.normal(arg_keys[9], (10, LATENT), jnp.float32), 0.1, 1.9)
    weights_m = scatter_about(arg_keys[10], (9, LATENT, LATENT), (1.0 / (3 * LATENT)), 0.010416667, (), jnp.float32)
    vectors_m = scatter_about(arg_keys[11], (10, LATENT), (4.0 / (3 * LATENT)), 0.041666668, (), jnp.float32)
    weights_v = jnp.clip(jnp.exp(jax.random.uniform(arg_keys[12], (9, LATENT, LATENT), jnp.float32, math.log(6.781684078305261e-06), math.log(2.7126736313221045e-05))), 6.781684078305261e-06, 2.7126736313221045e-05)
    vectors_v = jnp.clip(jnp.exp(jax.random.uniform(arg_keys[13], (10, LATENT), jnp.float32, math.log(0.000108506945), math.log(0.00043402778))), 0.000108506945, 0.00043402778)
    weights_ema = scatter_about(arg_keys[14], (9, LATENT, LATENT), (2 * LATENT) ** -0.5, 0.375, (), jnp.float32)
    vectors_ema = jnp.clip(1.0 + 0.18 * jax.random.normal(arg_keys[15], (10, LATENT), jnp.float32), 0.1, 1.9)
    return {"node_latents": node_latents, "edge_latents": edge_latents, "node_cotangent": node_cotangent, "edge_cotangent": edge_cotangent, "neighbours": neighbours, "edge_mask": edge_mask, "send_table": send_table, "counts": counts, "weights": weights, "vectors": vectors, "weights_m": weights_m, "vectors_m": vectors_m, "weights_v": weights_v, "vectors_v": vectors_v, "weights_ema": weights_ema, "vectors_ema": vectors_ema}


first_decay = 0.5
second_decay = 0.5
adam_epsilon = 1e-08
weight_decay = 0.01
matrix_rate = 0.05
vector_rate = 0.2
average_decay = 0.9
clip_norm = 1.0
norm_epsilon = 1e-05

@jax.custom_vjp
def low(v):
    return lax.optimization_barrier(v.astype(jnp.bfloat16)).astype(jnp.float32)

@jax.custom_vjp
def low_back(v):
    return v

def low_keep(v):
    return (low(v), None)

def low_pass(kept, grad):
    return (grad,)

def back_keep(v):
    return (v, None)

def back_low(kept, grad):
    return (low(grad),)
low.defvjp(low_keep, low_pass)
low_back.defvjp(back_keep, back_low)

def layer_norm(values, scale_row, shift_row):
    center = values - lax.optimization_barrier(jnp.mean(values, axis=-1, keepdims=True))
    spread = lax.optimization_barrier(jnp.mean(center * center, axis=-1, keepdims=True))
    return center * lax.rsqrt(spread + norm_epsilon) * scale_row + shift_row

def product(left, right):
    return jnp.dot(left, right, precision=lax.Precision.HIGHEST, preferred_element_type=jnp.float32)

def device_layer(weights_low, vectors, inputs):
    latents, edges, halo_rows, neighbours, edge_mask, count = inputs
    edge_weight = edge_mask.astype(jnp.float32)[:, :, None]
    node_table = jnp.concatenate([latents, halo_rows], axis=0)
    recv_proj = low_back(product(latents, weights_low[1]))
    send_proj = low_back(product(node_table, weights_low[2]))
    sender = jnp.take(send_proj, neighbours, axis=0)
    first = low_back(product(edges, weights_low[0]) + recv_proj[:, None, :] + sender + vectors[0])
    second = low_back(product(low(jax.nn.silu(first)), weights_low[3]) + vectors[1])
    third = low_back(product(low(jax.nn.silu(second)), weights_low[4]) + vectors[2])
    edges_new = edges + edge_weight * layer_norm(third, vectors[3], vectors[4])
    aggregate = low(lax.optimization_barrier(jnp.sum(edge_weight * edges_new, axis=1)))
    node_first = low_back(product(latents, weights_low[5]) + product(aggregate, weights_low[6]) + vectors[5])
    node_second = low_back(product(low(jax.nn.silu(node_first)), weights_low[7]) + vectors[6])
    node_third = low_back(product(low(jax.nn.silu(node_second)), weights_low[8]) + vectors[7])
    live = (jnp.arange(TOK_DEV, dtype=jnp.int32) < count).astype(jnp.float32)[:, None]
    latents_new = latents + live * layer_norm(node_third, vectors[8], vectors[9])
    return (latents_new, edges_new)

def adamw(param, grad, moment, second, average, scale, rate):
    clipped = grad * scale
    moment_new = first_decay * moment + (1.0 - first_decay) * clipped
    second_new = second_decay * second + (1.0 - second_decay) * clipped * clipped
    corrected = moment_new / (1.0 - first_decay ** STEP)
    denom = jnp.sqrt(second_new / (1.0 - second_decay ** STEP)) + adam_epsilon
    param_new = param - rate * (corrected / denom + weight_decay * param)
    average_new = average_decay * average + (1.0 - average_decay) * param_new
    return (moment_new, second_new, param_new, average_new)

def reference(node_latents, edge_latents, node_cotangent, edge_cotangent, neighbours, edge_mask, send_table, counts, weights, vectors, weights_m, vectors_m, weights_v, vectors_v, weights_ema, vectors_ema):
    devices = N_GX * N_GY
    node_rows = node_latents.astype(jnp.float32).reshape(devices, TOK_DEV, LATENT)
    edge_rows = edge_latents.astype(jnp.float32).reshape(devices, TOK_DEV, NBR_SLOTS, LATENT)
    neighbour_rows = neighbours.reshape(devices, TOK_DEV, NBR_SLOTS).astype(jnp.int32)
    mask_rows = edge_mask.reshape(devices, TOK_DEV, NBR_SLOTS)

    def forward(latents_all, edges_all, weight_blocks, vector_rows):
        weights_low = low(weight_blocks)
        boundary = jax.vmap(lambda rows, picks: jnp.take(rows, picks, axis=0))(latents_all, send_table)
        grid = boundary.reshape(N_GX, N_GY, HALO, LATENT)
        padded = jnp.pad(grid, ((1, 1), (1, 1), (0, 0), (0, 0)))
        slots = [padded[offset_x:offset_x + N_GX, offset_y:offset_y + N_GY] for offset_x in range(3) for offset_y in range(3)]
        halos = low_back(jnp.stack(slots, axis=2).reshape(devices, 9 * HALO, LATENT))
        layer = jax.checkpoint(partial(device_layer, weights_low, vector_rows))
        return lax.map(layer, (latents_all, edges_all, halos, neighbour_rows, mask_rows, counts))
    outputs, pullback = jax.vjp(forward, node_rows, edge_rows, weights, vectors)
    upstream = (node_cotangent.astype(jnp.float32).reshape(devices, TOK_DEV, LATENT), edge_cotangent.astype(jnp.float32).reshape(devices, TOK_DEV, NBR_SLOTS, LATENT))
    node_grad, edge_grad, weight_grad, vector_grad = pullback(upstream)
    grad_norm = jnp.sqrt(jnp.sum(weight_grad * weight_grad) + jnp.sum(vector_grad * vector_grad))
    scale = clip_norm / jnp.maximum(grad_norm, clip_norm)
    weights_m_new, weights_v_new, weights_new, weights_ema_new = adamw(weights, weight_grad, weights_m, weights_v, weights_ema, scale, matrix_rate)
    vectors_m_new, vectors_v_new, vectors_new, vectors_ema_new = adamw(vectors, vector_grad, vectors_m, vectors_v, vectors_ema, scale, vector_rate)
    nodes_out = outputs[0].reshape(PARTICLES, LATENT).astype(jnp.bfloat16)
    edges_out = outputs[1].reshape(PARTICLES, NBR_SLOTS, LATENT).astype(jnp.bfloat16)
    nodes_grad = node_grad.reshape(PARTICLES, LATENT).astype(jnp.bfloat16)
    edges_grad = edge_grad.reshape(PARTICLES, NBR_SLOTS, LATENT).astype(jnp.bfloat16)
    return (nodes_out, edges_out, nodes_grad, edges_grad, grad_norm, weights_m_new, vectors_m_new, weights_v_new, vectors_v_new, weights_new, vectors_new, weights_new.astype(jnp.bfloat16), vectors_new.astype(jnp.bfloat16), weights_ema_new, vectors_ema_new)
```

```python
import math

import jax
import jax.numpy as jnp
from jax import lax
from jax.sharding import PartitionSpec as P

STEP = 10


first_decay = 0.5
second_decay = 0.5
adam_epsilon = 1e-08
weight_decay = 0.01
matrix_rate = 0.05
vector_rate = 0.2
average_decay = 0.9
clip_norm = 1.0
norm_epsilon = 1e-05


def neighbour_pairs(count):
    near = [(i, i ^ 1) for i in range(count) if (i ^ 1) < count]
    far = [(i, i + 1) for i in range(1, count - 1, 2)]
    return near, far + [(target, source) for source, target in far]


def extended(block, sides):
    for axis, dim in sides:
        near, far = neighbour_pairs(lax.axis_size(axis))
        from_far = lax.ppermute(block, axis, far)
        from_near = lax.ppermute(block, axis, near)
        even = lax.axis_index(axis) % 2 == 0
        low = jnp.where(even, from_far, from_near)
        high = jnp.where(even, from_near, from_far)
        block = jnp.concatenate([low, block, high], axis=dim)
    return block


def returned_along(parts, axis):
    near, far = neighbour_pairs(lax.axis_size(axis))
    even = lax.axis_index(axis) % 2 == 0
    low, high = parts[0].astype(jnp.bfloat16), parts[2].astype(jnp.bfloat16)
    from_far = lax.ppermute(jnp.where(even, low, high), axis, far)
    from_near = lax.ppermute(jnp.where(even, high, low), axis, near)
    return parts[1] + from_far.astype(jnp.float32) + from_near.astype(jnp.float32)


def stages(count):
    result, stride = [], 1
    while stride < count:
        factor = 2 if stride == 1 else min(4, count // stride)
        result.append((stride, factor))
        stride *= factor
    return result


def sum_everywhere(total):
    rows, width = total.shape
    split = stages(lax.axis_size("gx"))
    whole_rows = -(-rows // (16 * lax.axis_size("gx"))) * 16 * lax.axis_size("gx")
    total = jnp.pad(total, ((0, whole_rows - rows), (0, 0))).astype(jnp.bfloat16)
    index = lax.axis_index("gx")

    def partners(axis, stride, mask):
        return [(i, i ^ (mask * stride)) for i in range(lax.axis_size(axis))]

    for stride, factor in split:
        part = (index // stride) % factor
        height = total.shape[0] // factor
        mine = lax.dynamic_slice_in_dim(total, part * height, height, 0).astype(jnp.float32)
        for mask in range(factor - 1, 0, -1):
            piece = lax.dynamic_slice_in_dim(total, (part ^ mask) * height, height, 0)
            mine = mine + lax.ppermute(piece, "gx", partners("gx", stride, mask)).astype(jnp.float32)
        total = mine.astype(jnp.bfloat16)
    terms = [total.astype(jnp.float32)] + [
        lax.ppermute(total, "gy", partners("gy", 1, mask)).astype(jnp.float32)
        for mask in range(1, lax.axis_size("gy"))
    ]
    while len(terms) > 1:
        terms = [terms[i] + terms[i + 1] for i in range(0, len(terms), 2)]
    total = terms[0].astype(jnp.bfloat16)
    for stride, factor in reversed(split):
        part = (index // stride) % factor
        height = total.shape[0]
        joined = jnp.zeros((factor * height, width), jnp.bfloat16)
        joined = lax.dynamic_update_slice_in_dim(joined, total, part * height, 0)
        for mask in range(factor - 1, 0, -1):
            piece = lax.ppermute(total, "gx", partners("gx", stride, mask))
            joined = lax.dynamic_update_slice_in_dim(joined, piece, (part ^ mask) * height, 0)
        total = joined
    return total[:rows].astype(jnp.float32)


def layer_norm(values, scale_row, shift_row):
    center = values - jnp.mean(values, axis=-1, keepdims=True)
    spread = jnp.mean(center * center, axis=-1, keepdims=True)
    return center * lax.rsqrt(spread + norm_epsilon) * scale_row + shift_row


def matmul(left, right):
    return jnp.dot(left, right, preferred_element_type=jnp.float32)


def matmul_back(left, right):
    return lax.dot_general(
        left, right, (((left.ndim - 1,), (1,)), ((), ())), preferred_element_type=jnp.float32
    )


def weight_grad(left, right):
    flat_left = left.reshape(-1, left.shape[-1])
    flat_right = right.reshape(-1, right.shape[-1])
    return lax.dot_general(
        flat_left, flat_right, (((0,), (0,)), ((), ())), preferred_element_type=jnp.float32
    )


def column_sum(values):
    return jnp.sum(values.astype(jnp.float32).reshape(-1, values.shape[-1]), axis=0)


def silu_grad(values, upstream):
    sigmoid = jax.nn.sigmoid(values)
    return upstream * (sigmoid + values * sigmoid * (1.0 - sigmoid))


def selector(indices, width, dtype):
    columns = lax.broadcasted_iota(jnp.int32, (indices.shape[0], width), 1)
    return (indices[:, None] == columns).astype(dtype)


def adamw(param, grad, moment, second, average, scale, rate):
    clipped = grad * scale
    moment_new = first_decay * moment + (1.0 - first_decay) * clipped
    second_new = second_decay * second + (1.0 - second_decay) * clipped * clipped
    corrected = moment_new / (1.0 - first_decay**STEP)
    denom = jnp.sqrt(second_new / (1.0 - second_decay**STEP)) + adam_epsilon
    param_new = param - rate * (corrected / denom + weight_decay * param)
    average_new = average_decay * average + (1.0 - average_decay) * param_new
    return (moment_new, second_new, param_new, average_new)


def per_device(
    node_latents,
    edge_latents,
    node_cotangent,
    edge_cotangent,
    neighbours,
    edge_mask,
    send_table,
    counts,
    weights,
    vectors,
    weights_m,
    vectors_m,
    weights_v,
    vectors_v,
    weights_ema,
    vectors_ema,
):
    tok_rows = node_latents.shape[0]
    slots_each = neighbours.shape[1]
    width = node_latents.shape[1]
    weights_low = weights.astype(jnp.bfloat16)
    send_rows = send_table[0]
    boundary_pick = selector(send_rows, tok_rows, jnp.bfloat16)
    boundary = matmul(boundary_pick, node_latents).astype(jnp.bfloat16)
    halo_grid = extended(boundary[None, None], (("gx", 0), ("gy", 1)))
    node_table = jnp.concatenate([node_latents, halo_grid.reshape(-1, width)], axis=0)
    table_rows = node_table.shape[0]
    group_size = math.gcd(tok_rows, max(1, 2048 // slots_each))
    block_edges = group_size * slots_each
    index_blocks = neighbours.reshape(-1, block_edges)

    def pick_rows(indices):
        return matmul(selector(indices, table_rows, jnp.bfloat16), node_table).astype(jnp.bfloat16)

    gathered = lax.map(pick_rows, index_blocks).reshape(tok_rows, slots_each, width)
    recv_proj = matmul(node_latents, weights_low[1])
    sender = matmul(gathered, weights_low[2])
    first = matmul(edge_latents, weights_low[0]) + recv_proj[:, None, :] + sender + vectors[0]
    first_act = jax.nn.silu(first).astype(jnp.bfloat16)
    second = matmul(first_act, weights_low[3]) + vectors[1]
    second_act = jax.nn.silu(second).astype(jnp.bfloat16)
    third = matmul(second_act, weights_low[4]) + vectors[2]
    edge_norm, edge_norm_back = jax.vjp(layer_norm, third, vectors[3], vectors[4])
    edge_weight = edge_mask.astype(jnp.float32)[:, :, None]
    edges_new = edge_latents.astype(jnp.float32) + edge_weight * edge_norm
    aggregate = jnp.sum(edge_weight * edges_new, axis=1).astype(jnp.bfloat16)
    node_first = (
        matmul(node_latents, weights_low[5]) + matmul(aggregate, weights_low[6]) + vectors[5]
    )
    node_first_act = jax.nn.silu(node_first).astype(jnp.bfloat16)
    node_second = matmul(node_first_act, weights_low[7]) + vectors[6]
    node_second_act = jax.nn.silu(node_second).astype(jnp.bfloat16)
    node_third = matmul(node_second_act, weights_low[8]) + vectors[7]
    live = (jnp.arange(tok_rows, dtype=jnp.int32) < counts[0]).astype(jnp.float32)[:, None]
    node_norm, node_norm_back = jax.vjp(layer_norm, node_third, vectors[8], vectors[9])
    latents_new = node_latents.astype(jnp.float32) + live * node_norm
    node_upstream = node_cotangent.astype(jnp.float32)
    third_node_grad, node_scale_grad, node_shift_grad = node_norm_back(live * node_upstream)
    third_node_grad = third_node_grad.astype(jnp.bfloat16)
    second_node_grad = silu_grad(node_second, matmul_back(third_node_grad, weights_low[8])).astype(
        jnp.bfloat16
    )
    first_node_grad = silu_grad(node_first, matmul_back(second_node_grad, weights_low[7])).astype(
        jnp.bfloat16
    )
    aggregate_grad = matmul_back(first_node_grad, weights_low[6])
    node_path_grad = matmul_back(first_node_grad, weights_low[5])
    node_mats = jnp.stack(
        [
            weight_grad(node_latents, first_node_grad),
            weight_grad(aggregate, first_node_grad),
            weight_grad(node_first_act, second_node_grad),
            weight_grad(node_second_act, third_node_grad),
        ]
    )
    node_vecs = jnp.stack(
        [
            column_sum(first_node_grad),
            column_sum(second_node_grad),
            column_sum(third_node_grad),
            node_scale_grad,
            node_shift_grad,
        ]
    )
    edge_upstream = edge_cotangent.astype(jnp.float32) + edge_weight * aggregate_grad[:, None, :]
    third_grad, edge_scale_grad, edge_shift_grad = edge_norm_back(edge_weight * edge_upstream)
    third_grad = third_grad.astype(jnp.bfloat16)
    second_grad = silu_grad(second, matmul_back(third_grad, weights_low[4])).astype(jnp.bfloat16)
    first_grad = silu_grad(first, matmul_back(second_grad, weights_low[3])).astype(jnp.bfloat16)
    edges_in_grad = edge_upstream + matmul_back(first_grad, weights_low[0])
    recv_grad = jnp.sum(first_grad.astype(jnp.float32), axis=1).astype(jnp.bfloat16)

    def add_block(total, pieces):
        indices, grads = pieces
        onehot = selector(indices, table_rows, jnp.bfloat16)
        return (
            total
            + lax.dot_general(
                onehot, grads, (((0,), (0,)), ((), ())), preferred_element_type=jnp.float32
            ),
            None,
        )

    send_total, _ = lax.scan(
        add_block,
        jnp.zeros((table_rows, width), jnp.float32),
        (index_blocks, first_grad.reshape(-1, block_edges, width)),
    )
    send_grad = send_total.astype(jnp.bfloat16)
    table_grad = matmul_back(send_grad, weights_low[2])
    halo_grad = lax.optimization_barrier(table_grad[tok_rows:].astype(jnp.bfloat16))
    halo_grad = halo_grad.astype(jnp.float32).reshape(3, 3, -1, width)
    boundary_grad = returned_along(returned_along(halo_grad, "gx"), "gy")
    returned = lax.dot_general(
        boundary_pick.astype(jnp.float32),
        boundary_grad,
        (((0,), (0,)), ((), ())),
        precision=lax.Precision.HIGHEST,
        preferred_element_type=jnp.float32,
    )
    nodes_in_grad = (
        node_upstream
        + node_path_grad
        + matmul_back(recv_grad, weights_low[1])
        + table_grad[:tok_rows]
        + returned
    )
    edge_mats = jnp.stack(
        [
            weight_grad(edge_latents, first_grad),
            weight_grad(node_latents, recv_grad),
            weight_grad(node_table, send_grad),
            weight_grad(first_act, second_grad),
            weight_grad(second_act, third_grad),
        ]
    )
    edge_vecs = jnp.stack(
        [
            column_sum(first_grad),
            column_sum(second_grad),
            column_sum(third_grad),
            edge_scale_grad,
            edge_shift_grad,
        ]
    )
    partial = jnp.concatenate(
        [
            edge_mats.reshape(-1, width),
            node_mats.reshape(-1, width),
            edge_vecs,
            node_vecs,
        ],
        axis=0,
    )
    summed = sum_everywhere(partial)
    mat_rows = weights.shape[0] * weights.shape[1]
    grad_mats, grad_vecs = summed[:mat_rows].reshape(weights.shape), summed[mat_rows:]
    grad_norm = jnp.sqrt(jnp.sum(grad_mats * grad_mats) + jnp.sum(grad_vecs * grad_vecs))
    scale = clip_norm / jnp.maximum(grad_norm, clip_norm)
    weights_m_new, weights_v_new, weights_new, weights_ema_new = adamw(
        weights, grad_mats, weights_m, weights_v, weights_ema, scale, matrix_rate
    )
    vectors_m_new, vectors_v_new, vectors_new, vectors_ema_new = adamw(
        vectors, grad_vecs, vectors_m, vectors_v, vectors_ema, scale, vector_rate
    )
    return (
        latents_new.astype(jnp.bfloat16),
        edges_new.astype(jnp.bfloat16),
        nodes_in_grad.astype(jnp.bfloat16),
        edges_in_grad.astype(jnp.bfloat16),
        grad_norm,
        weights_m_new,
        vectors_m_new,
        weights_v_new,
        vectors_v_new,
        weights_new,
        vectors_new,
        weights_new.astype(jnp.bfloat16),
        vectors_new.astype(jnp.bfloat16),
        weights_ema_new,
        vectors_ema_new,
    )


def solution(mesh):
    in_specs = (
        P(("gx", "gy"), None),
        P(("gx", "gy"), None, None),
        P(("gx", "gy"), None),
        P(("gx", "gy"), None, None),
        P(("gx", "gy"), None),
        P(("gx", "gy"), None),
        P(("gx", "gy"), None),
        P(("gx", "gy")),
        P(),
        P(),
        P(),
        P(),
        P(),
        P(),
        P(),
        P(),
    )
    out_specs = (
        P(("gx", "gy"), None),
        P(("gx", "gy"), None, None),
        P(("gx", "gy"), None),
        P(("gx", "gy"), None, None),
        P(),
        P(),
        P(),
        P(),
        P(),
        P(),
        P(),
        P(),
        P(),
        P(),
        P(),
    )
    return jax.shard_map(
        per_device, mesh=mesh, in_specs=in_specs, out_specs=out_specs, check_vma=False
    )
```

```python
import functools

import jax
import jax.numpy as jnp
from jax import lax
from jax.experimental import pallas as pl
from jax.experimental.pallas import tpu as pltpu
from jax.sharding import PartitionSpec as P

STEP = 10


first_decay = 0.5
second_decay = 0.5
adam_epsilon = 1e-08
weight_decay = 0.01
matrix_rate = 0.05
vector_rate = 0.2
average_decay = 0.9
clip_norm = 1.0
norm_epsilon = 1e-05


def neighbour_pairs(count):
    near = [(i, i ^ 1) for i in range(count) if (i ^ 1) < count]
    far = [(i, i + 1) for i in range(1, count - 1, 2)]
    return near, far + [(target, source) for source, target in far]


def extended(block, sides):
    for axis, dim in sides:
        near, far = neighbour_pairs(lax.axis_size(axis))
        from_far = lax.ppermute(block, axis, far)
        from_near = lax.ppermute(block, axis, near)
        even = lax.axis_index(axis) % 2 == 0
        low = jnp.where(even, from_far, from_near)
        high = jnp.where(even, from_near, from_far)
        block = jnp.concatenate([low, block, high], axis=dim)
    return block


def returned_along(parts, axis):
    near, far = neighbour_pairs(lax.axis_size(axis))
    even = lax.axis_index(axis) % 2 == 0
    low, high = parts[0].astype(jnp.bfloat16), parts[2].astype(jnp.bfloat16)
    from_far = lax.ppermute(jnp.where(even, low, high), axis, far)
    from_near = lax.ppermute(jnp.where(even, high, low), axis, near)
    return parts[1] + from_far.astype(jnp.float32) + from_near.astype(jnp.float32)


def stages(count):
    result, stride = [], 1
    while stride < count:
        factor = 2 if stride == 1 else min(4, count // stride)
        result.append((stride, factor))
        stride *= factor
    return result


def sum_everywhere(total):
    rows, width = total.shape
    split = stages(lax.axis_size("gx"))
    whole_rows = -(-rows // (16 * lax.axis_size("gx"))) * 16 * lax.axis_size("gx")
    total = jnp.pad(total, ((0, whole_rows - rows), (0, 0))).astype(jnp.bfloat16)
    index = lax.axis_index("gx")

    def partners(axis, stride, mask):
        return [(i, i ^ (mask * stride)) for i in range(lax.axis_size(axis))]

    for stride, factor in split:
        part = (index // stride) % factor
        height = total.shape[0] // factor
        mine = lax.dynamic_slice_in_dim(total, part * height, height, 0).astype(jnp.float32)
        for mask in range(factor - 1, 0, -1):
            piece = lax.dynamic_slice_in_dim(total, (part ^ mask) * height, height, 0)
            mine = mine + lax.ppermute(piece, "gx", partners("gx", stride, mask)).astype(jnp.float32)
        total = mine.astype(jnp.bfloat16)
    terms = [total.astype(jnp.float32)] + [
        lax.ppermute(total, "gy", partners("gy", 1, mask)).astype(jnp.float32)
        for mask in range(1, lax.axis_size("gy"))
    ]
    while len(terms) > 1:
        terms = [terms[i] + terms[i + 1] for i in range(0, len(terms), 2)]
    total = terms[0].astype(jnp.bfloat16)
    for stride, factor in reversed(split):
        part = (index // stride) % factor
        height = total.shape[0]
        joined = jnp.zeros((factor * height, width), jnp.bfloat16)
        joined = lax.dynamic_update_slice_in_dim(joined, total, part * height, 0)
        for mask in range(factor - 1, 0, -1):
            piece = lax.ppermute(total, "gx", partners("gx", stride, mask))
            joined = lax.dynamic_update_slice_in_dim(joined, piece, (part ^ mask) * height, 0)
        total = joined
    return total[:rows].astype(jnp.float32)


def selector(indices, width, dtype):
    columns = lax.broadcasted_iota(jnp.int32, (indices.shape[0], width), 1)
    return (indices[:, None] == columns).astype(dtype)


def adamw(param, grad, moment, second, average, scale, rate):
    clipped = grad * scale
    moment_new = first_decay * moment + (1.0 - first_decay) * clipped
    second_new = second_decay * second + (1.0 - second_decay) * clipped * clipped
    corrected = moment_new / (1.0 - first_decay**STEP)
    denom = jnp.sqrt(second_new / (1.0 - second_decay**STEP)) + adam_epsilon
    param_new = param - rate * (corrected / denom + weight_decay * param)
    average_new = average_decay * average + (1.0 - average_decay) * param_new
    return (moment_new, second_new, param_new, average_new)


CHUNK = 16
GROUP = 32
TILE = CHUNK * GROUP
LANES = 128
LOW_SCALE = 256.0


def dot(left, right):
    return jnp.dot(left, right, preferred_element_type=jnp.float32)


def dot_nt(left, right):
    return lax.dot_general(
        left, right, (((1,), (1,)), ((), ())), preferred_element_type=jnp.float32
    )


def dot_tn(left, right):
    return lax.dot_general(
        left, right, (((0,), (0,)), ((), ())), preferred_element_type=jnp.float32
    )


def split_pair(values):
    high = values.astype(jnp.bfloat16)
    low = ((values - high.astype(jnp.float32)) * LOW_SCALE).astype(jnp.bfloat16)
    return jnp.concatenate([high, low], axis=1)


def halves(pair):
    width = pair.shape[1] // 2
    return pair[:, :width] + pair[:, width:] * (1.0 / LOW_SCALE)


def silu_and_slope(values):
    gate = 0.5 * jnp.tanh(0.5 * values) + 0.5
    act = values * gate
    return act, gate + act * (1.0 - gate)


def row_mean(values):
    return jnp.mean(values, axis=-1, keepdims=True)


def normalized(values):
    center = values - row_mean(values)
    inverse = lax.rsqrt(row_mean(center * center) + norm_epsilon)
    return center * inverse, inverse


def normalized_back(upstream, unit, inverse):
    return inverse * (upstream - row_mean(upstream) - unit * row_mean(upstream * unit))


def column_total(values):
    return jnp.sum(values, axis=0, keepdims=True)


def layer_kernel(
    halo,
    count_ref,
    neighbour_ref,
    mask_ref,
    table_ref,
    upstream_ref,
    weights_ref,
    vectors_ref,
    edges_hbm,
    cotangent_hbm,
    nodes_out_ref,
    edges_out_hbm,
    edges_grad_hbm,
    node_part_ref,
    halo_grad_ref,
    grads_ref,
    edges_buf,
    cotangent_buf,
    kept_edges,
    kept_index,
    kept_act1,
    kept_act2,
    kept_slope1,
    kept_slope2,
    kept_unit,
    kept_inverse,
    low_ref,
    sender_ref,
    receiver_ref,
    neighbour_rows,
    segment_ref,
    chunk_sums,
    index_acc,
    mat_acc,
    vec_acc,
    work,
    upstream_tile,
    degree_rows,
    degree_smem,
    list_smem,
    in_sems,
    out_sems,
    degree_sem,
):
    f32, bf16 = jnp.float32, jnp.bfloat16
    particles, slots = neighbour_ref.shape
    per_particle = slots // CHUNK
    chunks = particles * per_particle
    rows, width = table_ref.shape
    index_width = index_acc.shape[1] - width
    pieces = in_sems.shape[0] // 2
    piece = chunks // pieces

    loads = []
    for order, (source, target) in enumerate(
        ((edges_hbm, edges_buf), (cotangent_hbm, cotangent_buf))
    ):
        loads.append(
            [
                pltpu.make_async_copy(
                    source.at[pl.ds(p * piece, piece)],
                    target.at[pl.ds(p * piece, piece)],
                    in_sems.at[order * pieces + p],
                )
                for p in range(pieces)
            ]
        )
    for copy in loads[0] + loads[1]:
        copy.start()
    edges_buf[chunks] = jnp.zeros((CHUNK, width), bf16)
    cotangent_buf[chunks] = jnp.zeros((CHUNK, width), bf16)

    mask = mask_ref[...].astype(f32)
    degree_rows[...] = jnp.zeros(degree_rows.shape, jnp.int32)
    degree_rows[:, 0:particles] = dot_nt(jnp.ones((8, slots), bf16), mask.astype(bf16)).astype(
        jnp.int32
    )
    fetch = pltpu.make_async_copy(degree_rows, degree_smem, degree_sem)
    fetch.start()

    neighbour = neighbour_ref[...]
    after_centre = particles + 5 * halo
    neighbour = jnp.where(neighbour >= after_centre, neighbour - halo, neighbour)
    neighbour_rows[...] = jnp.zeros(neighbour_rows.shape, f32)
    neighbour_rows[0:particles, 0:slots] = neighbour.astype(f32)

    for block in range(weights_ref.shape[0]):
        low_ref[block] = weights_ref[block].astype(bf16)
    vectors = vectors_ref[...]

    def vector(row):
        return vectors[row : row + 1, :]

    latents = table_ref[0:particles, :]
    sender_ref[...] = split_pair(dot(table_ref[...], low_ref[2]))
    receiver_ref[0:particles, :] = dot(latents, low_ref[1]) + vector(0)
    receiver_ref[particles:, :] = jnp.zeros((receiver_ref.shape[0] - particles, width), f32)

    degree = jnp.sum(mask, axis=1, keepdims=True).astype(jnp.int32)
    taken = jnp.broadcast_to(((degree + (CHUNK - 1)) >> 4).astype(f32), (particles, width))
    before = lax.broadcasted_iota(jnp.int32, (particles, particles), 1) < lax.broadcasted_iota(
        jnp.int32, (particles, particles), 0
    )
    begin = dot(before.astype(bf16), taken.astype(bf16))
    end = begin + taken
    for block in range(chunks // width):
        lane = lax.broadcasted_iota(jnp.int32, (particles, width), 1).astype(f32) + block * width
        segment_ref[:, block * width : (block + 1) * width] = (
            (lane >= begin) & (lane < end)
        ).astype(bf16)
    chunk_sums[...] = jnp.zeros(chunk_sums.shape, f32)
    index_acc[...] = jnp.zeros(index_acc.shape, f32)
    mat_acc[...] = jnp.zeros(mat_acc.shape, f32)
    vec_acc[...] = jnp.zeros(vec_acc.shape, f32)

    fetch.wait()

    def list_particle(i, position):
        used = (degree_smem[0, i] + (CHUNK - 1)) >> 4
        for c in range(per_particle):
            list_smem[position + c] = i * per_particle + c
        return position + used

    total = lax.fori_loop(0, particles, list_particle, jnp.int32(0), unroll=8)
    for j in range(GROUP):
        list_smem[total + j] = chunks
    tiles = (total + (GROUP - 1)) // GROUP

    for copy in loads[0]:
        copy.wait()

    sublane = lax.broadcasted_iota(jnp.int32, (CHUNK, width), 0)
    diagonal = lax.broadcasted_iota(jnp.int32, (CHUNK, width), 1) - sublane

    def entry(t, j):
        chunk = list_smem[t * GROUP + j]
        particle = chunk // per_particle
        first = (chunk % per_particle) * CHUNK
        live = (sublane < degree_smem[0, particle] - first).astype(f32)
        return chunk, particle, first, live

    def flat(ref, t):
        return ref[pl.ds(t * GROUP, GROUP)].reshape(TILE, width)

    def one_hot(t):
        index = flat(kept_index, t)
        lane = lax.broadcasted_iota(jnp.int32, (TILE, width), 1)
        return [(index == lane + b * width).astype(bf16) for b in range(index_width // width)]

    def forward(t, carry):
        base = t * GROUP
        entries = [entry(t, j) for j in range(GROUP)]
        for j, (chunk, particle, first, live) in enumerate(entries):
            kept_edges[base + j] = edges_buf[chunk]
            row = jnp.broadcast_to(neighbour_rows[pl.ds(particle, 1), :], (CHUNK, width))
            index = jnp.sum(jnp.where(diagonal == first, row, 0.0), axis=1, keepdims=True)
            kept_index[base + j] = jnp.broadcast_to(index, (CHUNK, width)).astype(jnp.int32)
        edge_tile = flat(kept_edges, t)
        receiver = jnp.concatenate(
            [
                jnp.broadcast_to(receiver_ref[pl.ds(particle, 1), :], (CHUNK, width))
                for _, particle, _, _ in entries
            ],
            axis=0,
        )
        first_in = halves(dot(jnp.concatenate(one_hot(t), axis=1), sender_ref[...]))
        first_in = first_in + (dot(edge_tile, low_ref[0]) + receiver)
        act, slope = silu_and_slope(first_in)
        act = act.astype(bf16)
        kept_act1[pl.ds(base, GROUP)] = act.reshape(GROUP, CHUNK, width)
        kept_slope1[pl.ds(base, GROUP)] = slope.astype(bf16).reshape(GROUP, CHUNK, width)
        act, slope = silu_and_slope(dot(act, low_ref[3]) + vector(1))
        act = act.astype(bf16)
        kept_act2[pl.ds(base, GROUP)] = act.reshape(GROUP, CHUNK, width)
        kept_slope2[pl.ds(base, GROUP)] = slope.astype(bf16).reshape(GROUP, CHUNK, width)
        unit, inverse = normalized(dot(act, low_ref[4]) + vector(2))
        kept_unit[pl.ds(base, GROUP)] = unit.astype(bf16).reshape(GROUP, CHUNK, width)
        kept_inverse[pl.ds(base, GROUP)] = jnp.broadcast_to(inverse, (TILE, width)).reshape(
            GROUP, CHUNK, width
        )
        live = jnp.concatenate([item[3] for item in entries], axis=0)
        edges_new = edge_tile.astype(f32) + live * (unit * vector(3) + vector(4))
        chunk_sums[pl.ds(base, GROUP), :] = jnp.sum(
            (live * edges_new).reshape(GROUP, CHUNK, width), axis=1
        )
        edges_new = edges_new.astype(bf16).reshape(GROUP, CHUNK, width)
        for j, (chunk, _, _, _) in enumerate(entries):
            edges_buf[chunk] = edges_new[j]
        return carry

    lax.fori_loop(0, tiles, forward, 0)

    stores = [
        pltpu.make_async_copy(
            edges_buf.at[pl.ds(p * piece, piece)],
            edges_out_hbm.at[pl.ds(p * piece, piece)],
            out_sems.at[p],
        )
        for p in range(pieces)
    ]
    for copy in stores:
        copy.start()

    def segment_sum():
        return halves(dot(segment_ref[...], split_pair(chunk_sums[...])))

    aggregate = segment_sum().astype(bf16)
    act1, slope1 = silu_and_slope(
        dot(latents, low_ref[5]) + dot(aggregate, low_ref[6]) + vector(5)
    )
    act1 = act1.astype(bf16)
    act2, slope2 = silu_and_slope(dot(act1, low_ref[7]) + vector(6))
    act2 = act2.astype(bf16)
    unit, inverse = normalized(dot(act2, low_ref[8]) + vector(7))
    alive = (
        lax.broadcasted_iota(jnp.int32, (particles, width), 0) < count_ref[0]
    ).astype(f32)
    upstream = upstream_ref[...].astype(f32)
    nodes_out_ref[...] = (
        latents.astype(f32) + alive * (unit * vector(8) + vector(9))
    ).astype(bf16)
    held = alive * upstream
    third = normalized_back(held * vector(8), unit, inverse).astype(bf16)
    second = (slope2 * dot_nt(third, low_ref[8])).astype(bf16)
    first = (slope1 * dot_nt(second, low_ref[7])).astype(bf16)
    receiver_ref[0:particles, :] = dot_nt(first, low_ref[6])
    node_part_ref[...] = upstream + dot_nt(first, low_ref[5])

    def put_block(block, values):
        grads_ref[block * width : (block + 1) * width, :] = values

    put_block(5, dot_tn(latents, first))
    put_block(6, dot_tn(aggregate, first))
    put_block(7, dot_tn(act1, second))
    put_block(8, dot_tn(act2, third))
    tail = weights_ref.shape[0] * width
    grads_ref[tail:, :] = jnp.zeros((grads_ref.shape[0] - tail, width), f32)
    for row, values in enumerate(
        (first.astype(f32), second.astype(f32), third.astype(f32), held * unit, held)
    ):
        grads_ref[tail + 5 + row : tail + 6 + row, :] = column_total(values)

    for copy in loads[1]:
        copy.wait()

    def backward(t, carry):
        base = t * GROUP
        entries = [entry(t, j) for j in range(GROUP)]
        live = jnp.concatenate([item[3] for item in entries], axis=0)
        passed = jnp.concatenate(
            [
                cotangent_buf[chunk].astype(f32) + alive_rows * receiver_ref[pl.ds(particle, 1), :]
                for chunk, particle, _, alive_rows in entries
            ],
            axis=0,
        )
        upstream_tile[...] = passed
        held = live * passed
        unit = flat(kept_unit, t).astype(f32)
        third = normalized_back(held * vector(3), unit, flat(kept_inverse, t)).astype(bf16)
        second = (flat(kept_slope2, t).astype(f32) * dot_nt(third, low_ref[4])).astype(bf16)
        first = (flat(kept_slope1, t).astype(f32) * dot_nt(second, low_ref[3])).astype(bf16)
        result = (upstream_tile[...] + dot_nt(first, low_ref[0])).astype(bf16)
        result = result.reshape(GROUP, CHUNK, width)
        for j, (chunk, _, _, _) in enumerate(entries):
            cotangent_buf[chunk] = result[j]
        index_acc[...] += dot_tn(first, jnp.concatenate(one_hot(t) + [flat(kept_edges, t)], axis=1))
        mat_acc[0] += dot_tn(flat(kept_act1, t), second)
        mat_acc[1] += dot_tn(flat(kept_act2, t), third)
        first = first.astype(f32)
        chunk_sums[pl.ds(base, GROUP), :] = jnp.sum(first.reshape(GROUP, CHUNK, width), axis=1)
        for row, values in enumerate(
            (first, second.astype(f32), third.astype(f32), held * unit, held)
        ):
            vec_acc[8 * row : 8 * row + 8, :] += jnp.sum(
                values.reshape(TILE // 8, 8, width), axis=0
            )
        return carry

    lax.fori_loop(0, tiles, backward, 0)

    results = [
        pltpu.make_async_copy(
            cotangent_buf.at[pl.ds(p * piece, piece)],
            edges_grad_hbm.at[pl.ds(p * piece, piece)],
            out_sems.at[pieces + p],
        )
        for p in range(pieces)
    ]
    for copy in results:
        copy.start()

    receiver_grad = segment_sum().astype(bf16)
    sent = index_acc[:, 0:index_width].astype(bf16)
    put_block(0, index_acc[:, index_width:].T)
    put_block(1, dot_tn(latents, receiver_grad))
    put_block(2, dot(sent, table_ref[...]).T)
    put_block(3, mat_acc[0])
    put_block(4, mat_acc[1])
    table_grad = lax.dot_general(
        sent, low_ref[2], (((0,), (1,)), ((), ())), preferred_element_type=f32
    )
    node_part_ref[...] += dot_nt(receiver_grad, low_ref[1]) + table_grad[0:particles, :]
    halo_grad_ref[...] = table_grad[particles:, :].astype(bf16)
    for row in range(5):
        grads_ref[tail + row : tail + row + 1, :] = column_total(vec_acc[8 * row : 8 * row + 8, :])

    for copy in stores + results:
        copy.wait()


def layer_call(
    table, halo, counts, neighbours, edge_mask, upstream, weights, vectors, edges, cotangents
):
    f32, bf16, i32 = jnp.float32, jnp.bfloat16, jnp.int32
    particles, slots = neighbours.shape
    width = table.shape[1]
    table_rows = table.shape[0]
    chunks = particles * slots // CHUNK
    pieces = 4
    grad_rows = weights.shape[0] * width + 16
    whole = pl.BlockSpec(memory_space=pltpu.VMEM)
    outside = pl.BlockSpec(memory_space=pl.ANY)
    edge_shape = (chunks, CHUNK, width)
    kept = pltpu.VMEM(edge_shape, bf16)
    buffer = pltpu.VMEM((chunks + 1, CHUNK, width), bf16)
    return pl.pallas_call(
        functools.partial(layer_kernel, halo),
        out_shape=(
            jax.ShapeDtypeStruct((particles, width), bf16),
            jax.ShapeDtypeStruct(edge_shape, bf16),
            jax.ShapeDtypeStruct(edge_shape, bf16),
            jax.ShapeDtypeStruct((particles, width), f32),
            jax.ShapeDtypeStruct((table_rows - particles, width), bf16),
            jax.ShapeDtypeStruct((grad_rows, width), f32),
        ),
        in_specs=[
            pl.BlockSpec(memory_space=pltpu.SMEM),
            whole,
            whole,
            whole,
            whole,
            whole,
            whole,
            outside,
            outside,
        ],
        out_specs=(whole, outside, outside, whole, whole, whole),
        scratch_shapes=[
            buffer,
            buffer,
            kept,
            pltpu.VMEM(edge_shape, i32),
            kept,
            kept,
            kept,
            kept,
            kept,
            pltpu.VMEM(edge_shape, f32),
            pltpu.VMEM(weights.shape, bf16),
            pltpu.VMEM((table_rows, 2 * width), bf16),
            pltpu.VMEM((particles + 8, width), f32),
            pltpu.VMEM((particles + 8, width), f32),
            pltpu.VMEM((particles, chunks), bf16),
            pltpu.VMEM((chunks, width), f32),
            pltpu.VMEM((width, table_rows + width), f32),
            pltpu.VMEM((2, width, width), f32),
            pltpu.VMEM((40, width), f32),
            pltpu.VMEM((TILE, width), f32),
            pltpu.VMEM((TILE, width), f32),
            pltpu.VMEM((8, particles + LANES), i32),
            pltpu.SMEM((8, particles + LANES), i32),
            pltpu.SMEM((chunks + GROUP + 16,), i32),
            pltpu.SemaphoreType.DMA((2 * pieces,)),
            pltpu.SemaphoreType.DMA((2 * pieces,)),
            pltpu.SemaphoreType.DMA,
        ],
        compiler_params=pltpu.CompilerParams(vmem_limit_bytes=60 * 1024 * 1024),
        name="edge_layer",
    )(
        counts,
        neighbours,
        edge_mask,
        table,
        upstream,
        weights,
        vectors,
        edges.reshape(edge_shape),
        cotangents.reshape(edge_shape),
    )


def per_device(
    node_latents,
    edge_latents,
    node_cotangent,
    edge_cotangent,
    neighbours,
    edge_mask,
    send_table,
    counts,
    weights,
    vectors,
    weights_m,
    vectors_m,
    weights_v,
    vectors_v,
    weights_ema,
    vectors_ema,
):
    tok_rows, width = node_latents.shape
    halo = send_table.shape[1]
    boundary_pick = selector(send_table[0], tok_rows, jnp.bfloat16)
    boundary = jnp.dot(boundary_pick, node_latents, preferred_element_type=jnp.float32)
    halo_grid = extended(boundary.astype(jnp.bfloat16)[None, None], (("gx", 0), ("gy", 1)))
    halo_rows = halo_grid.reshape(9, halo, width)
    node_table = jnp.concatenate(
        [
            node_latents,
            halo_rows[:4].reshape(-1, width),
            halo_rows[5:].reshape(-1, width),
        ],
        axis=0,
    )
    nodes_out, edges_out, edges_in_grad, node_part, halo_grad, partial = layer_call(
        node_table,
        halo,
        counts,
        neighbours,
        edge_mask,
        node_cotangent,
        weights,
        vectors,
        edge_latents,
        edge_cotangent,
    )
    halo_grad = halo_grad.astype(jnp.float32)
    halo_grad = jnp.concatenate(
        [halo_grad[: 4 * halo], jnp.zeros((halo, width), jnp.float32), halo_grad[4 * halo :]]
    ).reshape(3, 3, halo, width)
    boundary_grad = returned_along(returned_along(halo_grad, "gx"), "gy")
    returned = lax.dot_general(
        boundary_pick.astype(jnp.float32),
        boundary_grad,
        (((0,), (0,)), ((), ())),
        precision=lax.Precision.HIGHEST,
        preferred_element_type=jnp.float32,
    )
    nodes_in_grad = node_part + returned
    summed = sum_everywhere(partial)
    mat_rows = weights.shape[0] * weights.shape[1]
    vec_rows = vectors.shape[0]
    grad_mats = summed[:mat_rows].reshape(weights.shape)
    grad_vecs = summed[mat_rows : mat_rows + vec_rows]
    grad_norm = jnp.sqrt(jnp.sum(grad_mats * grad_mats) + jnp.sum(grad_vecs * grad_vecs))
    scale = clip_norm / jnp.maximum(grad_norm, clip_norm)
    weights_m_new, weights_v_new, weights_new, weights_ema_new = adamw(
        weights, grad_mats, weights_m, weights_v, weights_ema, scale, matrix_rate
    )
    vectors_m_new, vectors_v_new, vectors_new, vectors_ema_new = adamw(
        vectors, grad_vecs, vectors_m, vectors_v, vectors_ema, scale, vector_rate
    )
    return (
        nodes_out,
        edges_out.reshape(edge_latents.shape),
        nodes_in_grad.astype(jnp.bfloat16),
        edges_in_grad.reshape(edge_latents.shape),
        grad_norm,
        weights_m_new,
        vectors_m_new,
        weights_v_new,
        vectors_v_new,
        weights_new,
        vectors_new,
        weights_new.astype(jnp.bfloat16),
        vectors_new.astype(jnp.bfloat16),
        weights_ema_new,
        vectors_ema_new,
    )


def solution(mesh):
    in_specs = (
        P(("gx", "gy"), None),
        P(("gx", "gy"), None, None),
        P(("gx", "gy"), None),
        P(("gx", "gy"), None, None),
        P(("gx", "gy"), None),
        P(("gx", "gy"), None),
        P(("gx", "gy"), None),
        P(("gx", "gy")),
        P(),
        P(),
        P(),
        P(),
        P(),
        P(),
        P(),
        P(),
    )
    out_specs = (
        P(("gx", "gy"), None),
        P(("gx", "gy"), None, None),
        P(("gx", "gy"), None),
        P(("gx", "gy"), None, None),
        P(),
        P(),
        P(),
        P(),
        P(),
        P(),
        P(),
        P(),
        P(),
        P(),
        P(),
    )
    return jax.shard_map(
        per_device, mesh=mesh, in_specs=in_specs, out_specs=out_specs, check_vma=False
    )
```

```python
import functools

import jax
import jax.numpy as jnp
from jax import lax
from jax.experimental import pallas as pl
from jax.experimental.pallas import tpu as pltpu
from jax.sharding import PartitionSpec as P

STEP = 10


first_decay = 0.5
second_decay = 0.5
adam_epsilon = 1e-08
weight_decay = 0.01
matrix_rate = 0.05
vector_rate = 0.2
average_decay = 0.9
clip_norm = 1.0
norm_epsilon = 1e-05


def neighbour_pairs(count):
    near = [(i, i ^ 1) for i in range(count) if (i ^ 1) < count]
    far = [(i, i + 1) for i in range(1, count - 1, 2)]
    return near, far + [(target, source) for source, target in far]


def stages(count):
    result, stride = [], 1
    while stride < count:
        factor = 2 if stride == 1 else min(4, count // stride)
        result.append((stride, factor))
        stride *= factor
    return result


def selector(indices, width, dtype):
    columns = lax.broadcasted_iota(jnp.int32, (indices.shape[0], width), 1)
    return (indices[:, None] == columns).astype(dtype)


def adamw(param, grad, moment, second, average, scale, rate):
    clipped = grad * scale
    moment_new = first_decay * moment + (1.0 - first_decay) * clipped
    second_new = second_decay * second + (1.0 - second_decay) * clipped * clipped
    corrected = moment_new / (1.0 - first_decay**STEP)
    denom = jnp.sqrt(second_new / (1.0 - second_decay**STEP)) + adam_epsilon
    param_new = param - rate * (corrected / denom + weight_decay * param)
    average_new = average_decay * average + (1.0 - average_decay) * param_new
    return (moment_new, second_new, param_new, average_new)


CHUNK = 16
GROUP = 32
TILE = CHUNK * GROUP
LANES = 128
PIECES = 8


def dot(left, right):
    return jnp.dot(left, right, preferred_element_type=jnp.float32)


def dot_nt(left, right):
    return lax.dot_general(
        left, right, (((1,), (1,)), ((), ())), preferred_element_type=jnp.float32
    )


def dot_tn(left, right):
    return lax.dot_general(
        left, right, (((0,), (0,)), ((), ())), preferred_element_type=jnp.float32
    )


def split_pair(values, axis=1):
    high = values.astype(jnp.bfloat16)
    low = (values - high.astype(jnp.float32)).astype(jnp.bfloat16)
    return jnp.concatenate([high, low], axis=axis)


def halves(pair):
    width = pair.shape[1] // 2
    return pair[:, :width] + pair[:, width:]


def silu_of_half(half):
    turn = jnp.tanh(half)
    lift = 1.0 + turn
    act = half * lift
    return act, lift + act * (1.0 - turn)


def row_sum(values):
    return jnp.sum(values, axis=-1, keepdims=True)


def scaled_unit(values, width):
    center = values - row_sum(values) * (1.0 / width)
    inverse = lax.rsqrt(row_sum(center * center) + width * norm_epsilon)
    return center * inverse, inverse


def scaled_unit_back(scaled, unit, inverse, width):
    shift = row_sum(scaled) * (1.0 / width)
    return inverse * (scaled - shift - unit * row_sum(scaled * unit))


def column_total(values):
    return jnp.sum(values, axis=0, keepdims=True)


def iota(shape, dim):
    return lax.broadcasted_iota(jnp.int32, shape, dim)


def layer_kernel(
    halo,
    count_ref,
    neighbour_ref,
    mask_ref,
    latents_ref,
    ring_ref,
    ring_far_ref,
    ring_near_ref,
    upstream_ref,
    vectors_ref,
    weights_hbm,
    edges_hbm,
    cotangent_hbm,
    nodes_out_ref,
    edges_out_hbm,
    edges_grad_hbm,
    node_part_ref,
    halo_far_ref,
    halo_near_ref,
    halo_own_ref,
    grads_send_ref,
    grads_keep_ref,
    edges_buf,
    cotangent_buf,
    kept_edges,
    kept_index,
    kept_act1,
    kept_act2,
    kept_slope1,
    kept_slope2,
    kept_unit,
    kept_inverse,
    weights_buf,
    low_ref,
    table_ref,
    gather_ref,
    receiver_ref,
    receiver_tile,
    neighbour_rows,
    segment_ref,
    blocks_ref,
    chunk_sums,
    chunk_grads,
    index_acc,
    mat_acc,
    vec_acc,
    first_tile,
    third_tile,
    passed_tile,
    halo_grad,
    grads,
    list_rows,
    listed,
    in_sems,
    out_sems,
    list_sem,
    weights_sem,
):
    f32, bf16, i32 = jnp.float32, jnp.bfloat16, jnp.int32
    slots, particles = neighbour_ref.shape
    per = slots // CHUNK
    chunks = particles * per
    width = latents_ref.shape[1]
    rows = table_ref.shape[0]
    piece = chunks // PIECES
    root = float(width) ** 0.5
    odd_x = lax.axis_index("gx") & 1
    odd_y = lax.axis_index("gy") & 1

    fetch_weights = pltpu.make_async_copy(weights_hbm, weights_buf, weights_sem)
    fetch_weights.start()
    loads = [
        [
            pltpu.make_async_copy(
                source.at[pl.ds(p * piece, piece)],
                target.at[pl.ds(p * piece, piece)],
                in_sems.at[order * PIECES + p],
            )
            for p in range(PIECES)
        ]
        for order, (source, target) in enumerate(
            ((edges_hbm, edges_buf), (cotangent_hbm, cotangent_buf))
        )
    ]
    for copy in loads[0] + loads[1]:
        copy.start()
    edges_buf[chunks] = jnp.zeros((CHUNK, width), bf16)
    cotangent_buf[chunks] = jnp.zeros((CHUNK, width), bf16)

    mask = mask_ref[...].astype(f32)
    degree = jnp.sum(mask, axis=0, keepdims=True)
    taken = ((degree.astype(i32) + (CHUNK - 1)) >> 4).astype(f32)
    earlier = iota((particles, particles), 0) < iota((particles, particles), 1)
    begin = dot(jnp.broadcast_to(taken, (16, particles)).astype(bf16), earlier.astype(bf16))
    degree_col = dot_tn(mask.astype(bf16), jnp.ones((slots, width), bf16))
    taken_col = ((degree_col.astype(i32) + (CHUNK - 1)) >> 4).astype(f32)
    later = iota((particles, particles), 1) < iota((particles, particles), 0)
    begin_col = dot(later.astype(bf16), taken_col.astype(bf16))
    end_col = begin_col + taken_col
    for block in range(chunks // width):
        lane = iota((particles, width), 1).astype(f32) + block * width
        segment_ref[:, block * width : (block + 1) * width] = (
            (lane >= begin_col) & (lane < end_col)
        ).astype(bf16)
    total = row_sum(taken)
    who = iota((16, particles), 1).astype(f32)
    offset = per * who - begin
    coarse = jnp.floor(offset * 0.125) * 8.0
    line = iota((16, particles), 0)
    facts = jnp.where(
        line == 0,
        who,
        jnp.where(line == 1, coarse, jnp.where(line == 2, offset - coarse, degree)),
    )
    listing = dot(facts.astype(bf16), segment_ref[...])
    place = iota((1, chunks), 1).astype(f32)
    particle = listing[0:1, :]
    chunk = listing[1:2, :] + listing[2:3, :] + place
    rest = listing[3:4, :] - CHUNK * (chunk - per * particle)
    used = place < total
    list_rows[...] = jnp.zeros(list_rows.shape, i32)
    list_rows[0:1, 0:chunks] = jnp.where(used, chunk, float(chunks)).astype(i32)
    list_rows[0:1, chunks:] = jnp.full((1, list_rows.shape[1] - chunks), chunks, i32)
    list_rows[1:2, 0:chunks] = jnp.where(used, particle, float(particles)).astype(i32)
    list_rows[1:2, chunks:] = jnp.full((1, list_rows.shape[1] - chunks), particles, i32)
    list_rows[2:3, 0:chunks] = jnp.where(used, rest, 0.0).astype(i32)
    list_rows[3:4, 0:particles] = jnp.broadcast_to(total, (1, particles)).astype(i32)
    list_rows[4:5, 0:particles] = (begin[0:1, :] + taken).astype(i32)
    fetch_list = pltpu.make_async_copy(list_rows, listed, list_sem)
    fetch_list.start()

    neighbour = neighbour_ref[...]
    neighbour = jnp.where(neighbour >= particles + 5 * halo, neighbour - halo, neighbour)
    neighbour_rows[...] = jnp.zeros(neighbour_rows.shape, f32)
    neighbour_rows[0:particles, 0:slots] = neighbour.astype(f32).T

    block_of = iota((TILE, LANES), 0) >> 4
    for quarter in range(LANES // GROUP):
        blocks_ref[quarter] = (iota((TILE, LANES), 1) == block_of + quarter * GROUP).astype(bf16)
    chunk_sums[...] = jnp.zeros(chunk_sums.shape, f32)
    chunk_grads[...] = jnp.zeros(chunk_grads.shape, f32)
    index_acc[...] = jnp.zeros(index_acc.shape, f32)
    mat_acc[...] = jnp.zeros(mat_acc.shape, f32)
    vec_acc[...] = jnp.zeros(vec_acc.shape, f32)
    gather_ref[rows + width :, :] = jnp.zeros((LANES, 2 * width), bf16)
    tail = low_ref.shape[0] * width
    grads[tail:, :] = jnp.zeros((grads.shape[0] - tail, width), f32)

    table_ref[0:particles, :] = latents_ref[...]
    far, near, own = ring_far_ref[...], ring_near_ref[...], ring_ref[...]
    low_y = jnp.where(odd_y == 0, far, near)
    high_y = jnp.where(odd_y == 0, near, far)
    spot = particles
    for a in range(3):
        for b, strip in enumerate((low_y, own, high_y)):
            if a == 1 and b == 1:
                continue
            if a == 1:
                part = strip[2 * halo :]
            elif a == 0:
                part = jnp.where(odd_x == 0, strip[0:halo], strip[halo : 2 * halo])
            else:
                part = jnp.where(odd_x == 0, strip[halo : 2 * halo], strip[0:halo])
            table_ref[spot : spot + halo, :] = part
            spot += halo

    vectors = vectors_ref[...]

    def vector(row):
        return vectors[row : row + 1, :]

    fetch_weights.wait()
    for block in range(low_ref.shape[0]):
        low_ref[block] = weights_buf[block].astype(bf16)
    half3 = (0.5 * low_ref[3].astype(f32)).astype(bf16)
    half4 = (0.5 * low_ref[4].astype(f32)).astype(bf16)
    latents = latents_ref[...]
    gather_ref[0:rows, :] = split_pair(0.5 * dot(table_ref[...], low_ref[2]))
    gather_ref[rows : rows + width, :] = jnp.concatenate(
        [(0.5 * low_ref[0].astype(f32)).astype(bf16), jnp.zeros((width, width), bf16)], axis=1
    )
    receiver_ref[0:particles, :] = 0.5 * (dot(latents, low_ref[1]) + vector(0))
    receiver_ref[particles:, :] = jnp.zeros((receiver_ref.shape[0] - particles, width), f32)

    fetch_list.wait()
    tiles = (listed[3, 0] + (GROUP - 1)) >> 5
    for copy in loads[0]:
        copy.wait()

    sublane = iota((CHUNK, width), 0)
    diagonal = iota((CHUNK, width), 1) - sublane
    lane16 = iota((TILE, width), 1).astype(jnp.int16)

    def flat(ref, t):
        return ref[pl.ds(t * GROUP, GROUP)].reshape(TILE, width)

    def keep(ref, t, values):
        ref[pl.ds(t * GROUP, GROUP)] = values.astype(ref.dtype).reshape(GROUP, CHUNK, width)

    def span(j):
        return slice(j * CHUNK, (j + 1) * CHUNK)

    def one_hot(t):
        index = flat(kept_index, t)
        return [
            jnp.where(index == lane16 + jnp.int16(b * width), bf16(1), bf16(0))
            for b in range(rows // width)
        ]

    def gather(t):
        base = t * GROUP
        for j in range(GROUP):
            chunk, particle = listed[0, base + j], listed[1, base + j]
            kept_edges[base + j] = edges_buf[chunk]
            row = jnp.broadcast_to(neighbour_rows[pl.ds(particle, 1), :], (CHUNK, width))
            start = (chunk & (per - 1)) * CHUNK
            index = row_sum(jnp.where(diagonal == start, row, 0.0))
            kept_index[base + j] = (
                jnp.broadcast_to(index, (CHUNK, width)).astype(i32).astype(jnp.int16)
            )
            receiver_tile[j : j + 1, :] = receiver_ref[pl.ds(particle, 1), :]
        gather_ref[rows + width : rows + width + GROUP, :] = split_pair(receiver_tile[...])
        picks = jnp.concatenate(one_hot(t) + [flat(kept_edges, t), blocks_ref[0]], axis=1)
        first_tile[...] = halves(dot(picks, gather_ref[...]))

    gain_root = vector(3) * root

    def forward(t, carry):
        base = t * GROUP
        act, slope = silu_of_half(first_tile[...])
        act = act.astype(bf16)
        keep(kept_act1, t, act)
        keep(kept_slope1, t, slope)
        gather(t + 1)
        act, slope = silu_of_half(dot(act, half3) + 0.5 * vector(1))
        act = act.astype(bf16)
        keep(kept_act2, t, act)
        keep(kept_slope2, t, slope)
        unit, inverse = scaled_unit(dot(act, low_ref[4]) + vector(2), width)
        keep(kept_unit, t, unit)
        keep(kept_inverse, t, jnp.broadcast_to(inverse, (TILE, width)))
        change = unit * gain_root + vector(4)
        for j in range(GROUP):
            chunk = listed[0, base + j]
            alive = sublane < listed[2, base + j]
            fresh = kept_edges[base + j].astype(f32) + jnp.where(alive, change[span(j)], 0.0)
            edges_buf[chunk] = fresh.astype(bf16)
            chunk_sums[pl.ds(base + j, 1), :] = column_total(jnp.where(alive, fresh, 0.0))
        return carry

    gather(0)
    lax.fori_loop(0, tiles, forward, 0)
    keep(kept_unit, tiles, jnp.zeros((TILE, width), f32))

    stores = [
        pltpu.make_async_copy(
            edges_buf.at[pl.ds(p * piece, piece)],
            edges_out_hbm.at[pl.ds(p * piece, piece)],
            out_sems.at[p],
        )
        for p in range(PIECES)
    ]
    for copy in stores:
        copy.start()

    aggregate = halves(dot(segment_ref[...], split_pair(chunk_sums[...]))).astype(bf16)
    half1 = 0.5 * (dot(latents, low_ref[5]) + dot(aggregate, low_ref[6]) + vector(5))
    act1, slope1 = silu_of_half(half1)
    act1 = act1.astype(bf16)
    act2, slope2 = silu_of_half(0.5 * (dot(act1, low_ref[7]) + vector(6)))
    act2 = act2.astype(bf16)
    unit, inverse = scaled_unit(dot(act2, low_ref[8]) + vector(7), width)
    alive = (iota((particles, width), 0) < count_ref[0]).astype(f32)
    upstream = upstream_ref[...].astype(f32)
    nodes_out_ref[...] = (
        latents.astype(f32) + alive * (unit * (vector(8) * root) + vector(9))
    ).astype(bf16)
    held = alive * upstream
    third = scaled_unit_back(held * (vector(8) * root), unit, inverse, width).astype(bf16)
    second = (0.5 * slope2 * dot_nt(third, low_ref[8])).astype(bf16)
    first = (0.5 * slope1 * dot_nt(second, low_ref[7])).astype(bf16)
    receiver_ref[0:particles, :] = dot_nt(first, low_ref[6])
    node_part_ref[...] = upstream + dot_nt(first, low_ref[5])

    def put_block(block, values):
        grads[block * width : (block + 1) * width, :] = values

    put_block(5, dot_tn(latents, first))
    put_block(6, dot_tn(aggregate, first))
    put_block(7, dot_tn(act1, second))
    put_block(8, dot_tn(act2, third))
    for row, values in enumerate(
        (first.astype(f32), second.astype(f32), third.astype(f32), held * unit * root, held)
    ):
        grads[tail + 5 + row : tail + 6 + row, :] = column_total(values)

    for copy in loads[1]:
        copy.wait()

    def add_columns(row, values):
        vec_acc[8 * row : 8 * row + 8, :] += jnp.sum(values.reshape(TILE // 8, 8, width), axis=0)

    def descend(t):
        base = t * GROUP
        parts = []
        for j in range(GROUP):
            chunk, particle = listed[0, base + j], listed[1, base + j]
            alive = sublane < listed[2, base + j]
            passed = cotangent_buf[chunk].astype(f32) + jnp.where(
                alive, receiver_ref[pl.ds(particle, 1), :], 0.0
            )
            passed_tile[t & 1, span(j), :] = passed
            parts.append(jnp.where(alive, passed, 0.0))
        held = jnp.concatenate(parts, axis=0)
        unit = flat(kept_unit, t).astype(f32)
        third = scaled_unit_back(held * gain_root, unit, flat(kept_inverse, t), width)
        third_tile[...] = third.astype(bf16)
        return held, unit, third

    def backward(t, carry):
        base = t * GROUP
        third = third_tile[...]
        third_f32 = third.astype(f32)
        second = 1.0 * flat(kept_slope2, t).astype(f32) * dot_nt(third, half4)
        add_columns(1, second)
        add_columns(2, third_f32)
        second = second.astype(bf16)
        mat_acc[1] += dot_tn(flat(kept_act2, t), third)
        held, unit, _ = descend(t + 1)
        add_columns(3, held * unit)
        add_columns(4, held)
        first = (flat(kept_slope1, t).astype(f32) * dot_nt(second, half3)).astype(bf16)
        result = passed_tile[t & 1] + dot_nt(first, low_ref[0])
        for j in range(GROUP):
            cotangent_buf[listed[0, base + j]] = result[span(j)].astype(bf16)
        mat_acc[0] += dot_tn(flat(kept_act1, t), second)
        picks = jnp.concatenate(one_hot(t) + [flat(kept_edges, t), blocks_ref[t & 3]], axis=1)
        index_acc[...] += dot_tn(first, picks[:, 0 : rows + width])
        chunk_grads[t >> 2] += dot_tn(first, picks[:, rows + width :])
        return carry

    held, unit, _ = descend(0)
    add_columns(3, held * unit)
    add_columns(4, held)
    results = [
        pltpu.make_async_copy(
            cotangent_buf.at[pl.ds(p * piece, piece)],
            edges_grad_hbm.at[pl.ds(p * piece, piece)],
            out_sems.at[PIECES + p],
        )
        for p in range(PIECES)
    ]
    lax.fori_loop(0, tiles, backward, 0)
    for copy in results:
        copy.start()

    stacked = split_pair(
        jnp.concatenate([chunk_grads[g] for g in range(chunk_grads.shape[0])], axis=1), axis=0
    )
    receiver_grad = halves(dot_nt(segment_ref[...], stacked)).astype(bf16)
    grads[tail : tail + 1, :] = halves(dot_nt(jnp.ones((8, chunks), bf16), stacked))[0:1, :]
    for row in range(1, 5):
        values = column_total(vec_acc[8 * row : 8 * row + 8, :])
        grads[tail + row : tail + row + 1, :] = values * root if row == 3 else values
    sent = index_acc[:, 0:rows].astype(bf16)
    put_block(0, index_acc[:, rows:].T)
    put_block(1, dot_tn(latents, receiver_grad))
    put_block(2, dot(sent, table_ref[...]).T)
    put_block(3, mat_acc[0])
    put_block(4, mat_acc[1])
    table_grad = lax.dot_general(
        sent, low_ref[2], (((0,), (1,)), ((), ())), preferred_element_type=f32
    )
    node_part_ref[...] += dot_nt(receiver_grad, low_ref[1]) + table_grad[0:particles, :]
    halo_grad[...] = table_grad[particles:, :].astype(bf16)
    low_x = halo_grad[0 : 3 * halo, :]
    high_x = halo_grad[5 * halo : 8 * halo, :]
    halo_far_ref[...] = jnp.where(odd_x == 0, low_x, high_x)
    halo_near_ref[...] = jnp.where(odd_x == 0, high_x, low_x)
    halo_own_ref[...] = halo_grad[3 * halo : 5 * halo, :]
    part_rows = grads_keep_ref.shape[0]
    lower, upper = grads[0:part_rows, :], grads[part_rows:, :]
    grads_keep_ref[...] = jnp.where(odd_x == 0, lower, upper)
    grads_send_ref[...] = jnp.where(odd_x == 0, upper, lower).astype(bf16)

    for copy in stores + results:
        copy.wait()


def layer_call(
    halo, grad_rows, counts, neighbours, edge_mask, latents, ring, ring_far, ring_near, upstream,
    vectors, weights, edges, cotangents,
):
    f32, bf16, i32 = jnp.float32, jnp.bfloat16, jnp.int32
    particles, slots = neighbours.shape
    width = latents.shape[1]
    rows = particles + 8 * halo
    chunks = particles * slots // CHUNK
    whole = pl.BlockSpec(memory_space=pltpu.VMEM)
    outside = pl.BlockSpec(memory_space=pl.ANY)
    edge_shape = (chunks, CHUNK, width)
    kept_shape = (chunks + GROUP, CHUNK, width)
    kept = pltpu.VMEM(kept_shape, bf16)
    buffer = pltpu.VMEM((chunks + 1, CHUNK, width), bf16)
    strip = jax.ShapeDtypeStruct((3 * halo, width), bf16)
    return pl.pallas_call(
        functools.partial(layer_kernel, halo),
        out_shape=(
            jax.ShapeDtypeStruct((particles, width), bf16),
            jax.ShapeDtypeStruct(edge_shape, bf16),
            jax.ShapeDtypeStruct(edge_shape, bf16),
            jax.ShapeDtypeStruct((particles, width), f32),
            strip,
            strip,
            jax.ShapeDtypeStruct((2 * halo, width), bf16),
            jax.ShapeDtypeStruct((grad_rows // 2, width), bf16),
            jax.ShapeDtypeStruct((grad_rows // 2, width), f32),
        ),
        in_specs=[pl.BlockSpec(memory_space=pltpu.SMEM)] + [whole] * 8 + [outside] * 3,
        out_specs=(whole, outside, outside, whole, whole, whole, whole, whole, whole),
        scratch_shapes=[
            buffer,
            buffer,
            kept,
            pltpu.VMEM(kept_shape, jnp.int16),
            kept,
            kept,
            kept,
            kept,
            kept,
            pltpu.VMEM(kept_shape, f32),
            pltpu.VMEM(weights.shape, f32),
            pltpu.VMEM(weights.shape, bf16),
            pltpu.VMEM((rows, width), bf16),
            pltpu.VMEM((rows + width + LANES, 2 * width), bf16),
            pltpu.VMEM((particles + 8, width), f32),
            pltpu.VMEM((GROUP, width), f32),
            pltpu.VMEM((particles + 8, width), f32),
            pltpu.VMEM((particles, chunks), bf16),
            pltpu.VMEM((LANES // GROUP, TILE, LANES), bf16),
            pltpu.VMEM((chunks, width), f32),
            pltpu.VMEM((chunks // LANES, width, LANES), f32),
            pltpu.VMEM((width, rows + width), f32),
            pltpu.VMEM((2, width, width), f32),
            pltpu.VMEM((40, width), f32),
            pltpu.VMEM((TILE, width), f32),
            pltpu.VMEM((TILE, width), bf16),
            pltpu.VMEM((2, TILE, width), f32),
            pltpu.VMEM((8 * halo, width), bf16),
            pltpu.VMEM((grad_rows, width), f32),
            pltpu.VMEM((8, chunks + LANES), i32),
            pltpu.SMEM((8, chunks + LANES), i32),
            pltpu.SemaphoreType.DMA((2 * PIECES,)),
            pltpu.SemaphoreType.DMA((2 * PIECES,)),
            pltpu.SemaphoreType.DMA,
            pltpu.SemaphoreType.DMA,
        ],
        compiler_params=pltpu.CompilerParams(vmem_limit_bytes=60 * 1024 * 1024),
        name="edge_layer",
    )(
        counts,
        neighbours.T,
        edge_mask.T,
        latents,
        ring,
        ring_far,
        ring_near,
        upstream,
        vectors,
        weights,
        edges.reshape(edge_shape),
        cotangents.reshape(edge_shape),
    )


def update_kernel(
    mine_ref,
    other_ref,
    weights_ref,
    vectors_ref,
    weights_m_ref,
    vectors_m_ref,
    weights_v_ref,
    vectors_v_ref,
    weights_ema_ref,
    vectors_ema_ref,
    norm_ref,
    weights_m_out,
    vectors_m_out,
    weights_v_out,
    vectors_v_out,
    weights_out,
    vectors_out,
    weights_copy_out,
    vectors_copy_out,
    weights_ema_out,
    vectors_ema_out,
    grads,
):
    f32 = jnp.float32
    odd = lax.axis_index("gx") & 1
    part_rows, width = mine_ref.shape
    mine, other = mine_ref[...].astype(f32), other_ref[...].astype(f32)
    grads[0:part_rows, :] = jnp.where(odd == 0, mine, other)
    grads[part_rows:, :] = jnp.where(odd == 0, other, mine)
    squares = jnp.sum((mine * mine + other * other).reshape(part_rows // 8, 8, width), axis=0)
    norm = jnp.sqrt(jnp.sum(jnp.sum(squares, axis=1, keepdims=True), axis=0, keepdims=True))
    norm_ref[...] = norm
    scale = clip_norm / jnp.maximum(norm, clip_norm)
    for block in range(weights_ref.shape[0]):
        moment, second, param, average = adamw(
            weights_ref[block],
            grads[block * width : (block + 1) * width, :],
            weights_m_ref[block],
            weights_v_ref[block],
            weights_ema_ref[block],
            scale,
            matrix_rate,
        )
        weights_m_out[block] = moment
        weights_v_out[block] = second
        weights_out[block] = param
        weights_copy_out[block] = param.astype(jnp.bfloat16)
        weights_ema_out[block] = average
    tail = weights_ref.shape[0] * width
    moment, second, param, average = adamw(
        vectors_ref[...],
        grads[tail : tail + vectors_ref.shape[0], :],
        vectors_m_ref[...],
        vectors_v_ref[...],
        vectors_ema_ref[...],
        scale,
        vector_rate,
    )
    vectors_m_out[...] = moment
    vectors_v_out[...] = second
    vectors_out[...] = param
    vectors_copy_out[...] = param.astype(jnp.bfloat16)
    vectors_ema_out[...] = average


def update_call(mine, other, weights, vectors, weights_m, vectors_m, weights_v, vectors_v,
                weights_ema, vectors_ema):
    f32, bf16 = jnp.float32, jnp.bfloat16
    mat, vec = weights.shape, vectors.shape
    kinds = (
        ((1, 1), f32), (mat, f32), (vec, f32), (mat, f32), (vec, f32), (mat, f32), (vec, f32),
        (mat, bf16), (vec, bf16), (mat, f32), (vec, f32),
    )
    whole = pl.BlockSpec(memory_space=pltpu.VMEM)
    return pl.pallas_call(
        update_kernel,
        out_shape=tuple(jax.ShapeDtypeStruct(*kind) for kind in kinds),
        in_specs=[whole] * 10,
        out_specs=(whole,) * 11,
        scratch_shapes=[pltpu.VMEM((2 * mine.shape[0], mine.shape[1]), f32)],
        compiler_params=pltpu.CompilerParams(vmem_limit_bytes=24 * 1024 * 1024),
        name="update",
    )(mine, other, weights, vectors, weights_m, vectors_m, weights_v, vectors_v, weights_ema,
      vectors_ema)


def pair_exchange(to_far, to_near, axis):
    near, far = neighbour_pairs(lax.axis_size(axis))
    return lax.ppermute(to_far, axis, far), lax.ppermute(to_near, axis, near)


def partners(axis, stride, mask):
    return [(i, i ^ (mask * stride)) for i in range(lax.axis_size(axis))]


def per_device(
    node_latents,
    edge_latents,
    node_cotangent,
    edge_cotangent,
    neighbours,
    edge_mask,
    send_table,
    counts,
    weights,
    vectors,
    weights_m,
    vectors_m,
    weights_v,
    vectors_v,
    weights_ema,
    vectors_ema,
):
    f32, bf16 = jnp.float32, jnp.bfloat16
    tok_rows, width = node_latents.shape
    halo = send_table.shape[1]
    boundary_pick = selector(send_table[0], tok_rows, bf16)
    boundary = jnp.dot(boundary_pick, node_latents, preferred_element_type=f32).astype(bf16)
    from_far, from_near = pair_exchange(boundary, boundary, "gx")
    ring = jnp.concatenate([from_far, from_near, boundary], axis=0)
    ring_far, ring_near = pair_exchange(ring, ring, "gy")
    unit = 16 * lax.axis_size("gx")
    grad_rows = -(-(weights.shape[0] * width + vectors.shape[0]) // unit) * unit
    (
        nodes_out,
        edges_out,
        edges_in_grad,
        node_part,
        halo_far,
        halo_near,
        halo_own,
        grads_send,
        grads_keep,
    ) = layer_call(
        halo, grad_rows, counts, neighbours, edge_mask, node_latents, ring, ring_far, ring_near,
        node_cotangent, vectors, weights, edge_latents, edge_cotangent,
    )
    index = lax.axis_index("gx")
    got = lax.ppermute(grads_send, "gx", partners("gx", 1, 1))
    total = (grads_keep + got.astype(f32)).astype(bf16)
    split = stages(lax.axis_size("gx"))[1:]
    for stride, factor in split:
        part = (index // stride) % factor
        height = total.shape[0] // factor
        mine = lax.dynamic_slice_in_dim(total, part * height, height, 0).astype(f32)
        for mask in range(factor - 1, 0, -1):
            piece = lax.dynamic_slice_in_dim(total, (part ^ mask) * height, height, 0)
            mine = mine + lax.ppermute(piece, "gx", partners("gx", stride, mask)).astype(f32)
        total = mine.astype(bf16)
    total, halo_far, halo_near = lax.optimization_barrier((total, halo_far, halo_near))
    back_far, back_near = pair_exchange(halo_far, halo_near, "gx")
    terms = [total.astype(f32)] + [
        lax.ppermute(total, "gy", partners("gy", 1, mask)).astype(f32)
        for mask in range(1, lax.axis_size("gy"))
    ]
    while len(terms) > 1:
        terms = [terms[i] + terms[i + 1] for i in range(0, len(terms), 2)]
    total = terms[0].astype(bf16)
    strips = back_far.astype(f32) + back_near.astype(f32)
    strips = strips + jnp.concatenate(
        [halo_own[:halo], jnp.zeros((halo, width), bf16), halo_own[halo:]], axis=0
    ).astype(f32)
    even_y = lax.axis_index("gy") % 2 == 0
    low_y, high_y = strips[:halo].astype(bf16), strips[2 * halo :].astype(bf16)
    total, low_y, high_y = lax.optimization_barrier((total, low_y, high_y))
    last_far, last_near = pair_exchange(
        jnp.where(even_y, low_y, high_y), jnp.where(even_y, high_y, low_y), "gy"
    )
    for stride, factor in reversed(split):
        part = (index // stride) % factor
        height = total.shape[0]
        joined = jnp.zeros((factor * height, width), bf16)
        joined = lax.dynamic_update_slice_in_dim(joined, total, part * height, 0)
        for mask in range(factor - 1, 0, -1):
            piece = lax.ppermute(total, "gx", partners("gx", stride, mask))
            joined = lax.dynamic_update_slice_in_dim(joined, piece, (part ^ mask) * height, 0)
        total = joined
    other = lax.ppermute(total, "gx", partners("gx", 1, 1))
    boundary_grad = strips[halo : 2 * halo] + last_far.astype(f32) + last_near.astype(f32)
    returned = lax.dot_general(
        boundary_pick.astype(f32),
        boundary_grad,
        (((0,), (0,)), ((), ())),
        precision=lax.Precision.HIGHEST,
        preferred_element_type=f32,
    )
    nodes_in_grad = (node_part + returned).astype(bf16)
    updated = update_call(
        total, other, weights, vectors, weights_m, vectors_m, weights_v, vectors_v, weights_ema,
        vectors_ema,
    )
    return (
        nodes_out,
        edges_out.reshape(edge_latents.shape),
        nodes_in_grad,
        edges_in_grad.reshape(edge_latents.shape),
        updated[0].reshape(()),
    ) + tuple(updated[1:])


def solution(mesh):
    in_specs = (
        P(("gx", "gy"), None),
        P(("gx", "gy"), None, None),
        P(("gx", "gy"), None),
        P(("gx", "gy"), None, None),
        P(("gx", "gy"), None),
        P(("gx", "gy"), None),
        P(("gx", "gy"), None),
        P(("gx", "gy")),
        P(),
        P(),
        P(),
        P(),
        P(),
        P(),
        P(),
        P(),
    )
    out_specs = (
        P(("gx", "gy"), None),
        P(("gx", "gy"), None, None),
        P(("gx", "gy"), None),
        P(("gx", "gy"), None, None),
        P(),
        P(),
        P(),
        P(),
        P(),
        P(),
        P(),
        P(),
        P(),
        P(),
        P(),
    )
    return jax.shard_map(
        per_device, mesh=mesh, in_specs=in_specs, out_specs=out_specs, check_vma=False
    )
```

```python
import functools

import jax
import jax.numpy as jnp
from jax import lax
from jax.experimental import pallas as pl
from jax.experimental.pallas import tpu as pltpu
from jax.sharding import PartitionSpec as P

STEP = 10


first_decay = 0.5
second_decay = 0.5
adam_epsilon = 1e-08
weight_decay = 0.01
matrix_rate = 0.05
vector_rate = 0.2
average_decay = 0.9
clip_norm = 1.0
norm_epsilon = 1e-05


def neighbour_pairs(count):
    near = [(i, i ^ 1) for i in range(count) if (i ^ 1) < count]
    far = [(i, i + 1) for i in range(1, count - 1, 2)]
    return near, far + [(target, source) for source, target in far]


def stages(count):
    result, stride = [], 1
    while stride < count:
        factor = 2 if stride == 1 else min(4, count // stride)
        result.append((stride, factor))
        stride *= factor
    return result


def selector(indices, width, dtype):
    columns = lax.broadcasted_iota(jnp.int32, (indices.shape[0], width), 1)
    return (indices[:, None] == columns).astype(dtype)


def adamw(param, grad, moment, second, average, scale, rate):
    clipped = grad * scale
    moment_new = first_decay * moment + (1.0 - first_decay) * clipped
    second_new = second_decay * second + (1.0 - second_decay) * clipped * clipped
    corrected = moment_new / (1.0 - first_decay**STEP)
    denom = jnp.sqrt(second_new / (1.0 - second_decay**STEP)) + adam_epsilon
    param_new = param - rate * (corrected / denom + weight_decay * param)
    average_new = average_decay * average + (1.0 - average_decay) * param_new
    return (moment_new, second_new, param_new, average_new)


CHUNK = 16
GROUP = 32
TILE = CHUNK * GROUP
LANES = 128
PIECES = 8


def dot(left, right):
    return jnp.dot(left, right, preferred_element_type=jnp.float32)


def dot_nt(left, right):
    return lax.dot_general(
        left, right, (((1,), (1,)), ((), ())), preferred_element_type=jnp.float32
    )


def dot_tn(left, right):
    return lax.dot_general(
        left, right, (((0,), (0,)), ((), ())), preferred_element_type=jnp.float32
    )


def split_pair(values, axis=1):
    high = values.astype(jnp.bfloat16)
    low = (values - high.astype(jnp.float32)).astype(jnp.bfloat16)
    return jnp.concatenate([high, low], axis=axis)


def halves(pair):
    width = pair.shape[1] // 2
    return pair[:, :width] + pair[:, width:]


def silu_of_half(half):
    turn = jnp.tanh(half)
    lift = 1.0 + turn
    act = half * lift
    return act, lift + act * (1.0 - turn)


def row_sum(values):
    return jnp.sum(values, axis=-1, keepdims=True)


def scaled_unit(values, width):
    center = values - row_sum(values) * (1.0 / width)
    inverse = lax.rsqrt(row_sum(center * center) + width * norm_epsilon)
    return center * inverse, inverse


def scaled_unit_back(scaled, unit, inverse, width):
    shift = row_sum(scaled) * (1.0 / width)
    return inverse * (scaled - shift - unit * row_sum(scaled * unit))


def column_total(values):
    return jnp.sum(values, axis=0, keepdims=True)


def iota(shape, dim):
    return lax.broadcasted_iota(jnp.int32, shape, dim)


def slot_rows(quarter, halo):
    return (0, quarter, 3 * quarter + 3 * halo, 2 * quarter + 3 * halo)


def layer_kernel(
    halo,
    relayed,
    count_ref,
    neighbour_ref,
    mask_ref,
    latents_ref,
    ring_ref,
    ring_far_ref,
    ring_near_ref,
    upstream_ref,
    vectors_ref,
    weights_hbm,
    edges_hbm,
    cotangent_hbm,
    nodes_out_ref,
    edges_out_hbm,
    edges_grad_hbm,
    node_part_ref,
    halo_own_ref,
    send_ref,
    keep_ref,
    edges_buf,
    cotangent_buf,
    kept_edges,
    kept_index,
    kept_act1,
    kept_act2,
    kept_slope1,
    kept_slope2,
    kept_unit,
    kept_inverse,
    weights_buf,
    low_ref,
    table_ref,
    gather_ref,
    receiver_ref,
    receiver_tile,
    neighbour_rows,
    segment_ref,
    blocks_ref,
    chunk_sums,
    chunk_grads,
    index_acc,
    mat_acc,
    vec_acc,
    first_tile,
    third_tile,
    first_back,
    second_back,
    passed_tile,
    halo_grad,
    grads,
    list_rows,
    listed,
    in_sems,
    out_sems,
    list_sem,
    weights_sem,
):
    f32, bf16, i32 = jnp.float32, jnp.bfloat16, jnp.int32
    slots, particles = neighbour_ref.shape
    per = slots // CHUNK
    chunks = particles * per
    width = latents_ref.shape[1]
    rows = table_ref.shape[0]
    piece = chunks // PIECES
    root = float(width) ** 0.5
    odd_x = lax.axis_index("gx") & 1
    odd_y = lax.axis_index("gy") & 1

    fetch_weights = pltpu.make_async_copy(weights_hbm, weights_buf, weights_sem)
    fetch_weights.start()
    loads = [
        [
            pltpu.make_async_copy(
                source.at[pl.ds(p * piece, piece)],
                target.at[pl.ds(p * piece, piece)],
                in_sems.at[order * PIECES + p],
            )
            for p in range(PIECES)
        ]
        for order, (source, target) in enumerate(
            ((edges_hbm, edges_buf), (cotangent_hbm, cotangent_buf))
        )
    ]
    for copy in loads[0] + loads[1]:
        copy.start()
    edges_buf[chunks] = jnp.zeros((CHUNK, width), bf16)
    cotangent_buf[chunks] = jnp.zeros((CHUNK, width), bf16)

    mask = mask_ref[...].astype(f32)
    degree = jnp.sum(mask, axis=0, keepdims=True)
    taken = ((degree.astype(i32) + (CHUNK - 1)) >> 4).astype(f32)
    earlier = iota((particles, particles), 0) < iota((particles, particles), 1)
    begin = dot(jnp.broadcast_to(taken, (16, particles)).astype(bf16), earlier.astype(bf16))
    degree_col = dot_tn(mask.astype(bf16), jnp.ones((slots, width), bf16))
    taken_col = ((degree_col.astype(i32) + (CHUNK - 1)) >> 4).astype(f32)
    later = iota((particles, particles), 1) < iota((particles, particles), 0)
    begin_col = dot(later.astype(bf16), taken_col.astype(bf16))
    end_col = begin_col + taken_col
    for block in range(chunks // width):
        lane = iota((particles, width), 1).astype(f32) + block * width
        segment_ref[:, block * width : (block + 1) * width] = (
            (lane >= begin_col) & (lane < end_col)
        ).astype(bf16)
    total = row_sum(taken)
    who = iota((16, particles), 1).astype(f32)
    offset = per * who - begin
    coarse = jnp.floor(offset * 0.125) * 8.0
    line = iota((16, particles), 0)
    facts = jnp.where(
        line == 0,
        who,
        jnp.where(line == 1, coarse, jnp.where(line == 2, offset - coarse, degree)),
    )
    listing = dot(facts.astype(bf16), segment_ref[...])
    place = iota((1, chunks), 1).astype(f32)
    particle = listing[0:1, :]
    chunk = listing[1:2, :] + listing[2:3, :] + place
    rest = listing[3:4, :] - CHUNK * (chunk - per * particle)
    used = place < total
    list_rows[...] = jnp.zeros(list_rows.shape, i32)
    list_rows[0:1, 0:chunks] = jnp.where(used, chunk, float(chunks)).astype(i32)
    list_rows[0:1, chunks:] = jnp.full((1, list_rows.shape[1] - chunks), chunks, i32)
    list_rows[1:2, 0:chunks] = jnp.where(used, particle, float(particles)).astype(i32)
    list_rows[1:2, chunks:] = jnp.full((1, list_rows.shape[1] - chunks), particles, i32)
    list_rows[2:3, 0:chunks] = jnp.where(used, rest, 0.0).astype(i32)
    list_rows[3:4, 0:particles] = jnp.broadcast_to(total, (1, particles)).astype(i32)
    list_rows[4:5, 0:particles] = (begin[0:1, :] + taken).astype(i32)
    fetch_list = pltpu.make_async_copy(list_rows, listed, list_sem)
    fetch_list.start()

    neighbour = neighbour_ref[...]
    neighbour = jnp.where(neighbour >= particles + 5 * halo, neighbour - halo, neighbour)
    neighbour_rows[...] = jnp.zeros(neighbour_rows.shape, f32)
    neighbour_rows[0:particles, 0:slots] = neighbour.astype(f32).T

    block_of = iota((TILE, LANES), 0) >> 4
    for quarter in range(LANES // GROUP):
        blocks_ref[quarter] = (iota((TILE, LANES), 1) == block_of + quarter * GROUP).astype(bf16)
    chunk_sums[...] = jnp.zeros(chunk_sums.shape, f32)
    chunk_grads[...] = jnp.zeros(chunk_grads.shape, f32)
    index_acc[...] = jnp.zeros(index_acc.shape, f32)
    mat_acc[...] = jnp.zeros(mat_acc.shape, f32)
    vec_acc[...] = jnp.zeros(vec_acc.shape, f32)
    gather_ref[rows + width :, :] = jnp.zeros((LANES, 2 * width), bf16)
    tail = low_ref.shape[0] * width
    grads[tail:, :] = jnp.zeros((grads.shape[0] - tail, width), f32)

    table_ref[0:particles, :] = latents_ref[...]
    far, near, own = ring_far_ref[...], ring_near_ref[...], ring_ref[...]
    low_y = jnp.where(odd_y == 0, far, near)
    high_y = jnp.where(odd_y == 0, near, far)
    spot = particles
    for a in range(3):
        for b, strip in enumerate((low_y, own, high_y)):
            if a == 1 and b == 1:
                continue
            if a == 1:
                part = strip[2 * halo :]
            elif a == 0:
                part = jnp.where(odd_x == 0, strip[0:halo], strip[halo : 2 * halo])
            else:
                part = jnp.where(odd_x == 0, strip[halo : 2 * halo], strip[0:halo])
            table_ref[spot : spot + halo, :] = part
            spot += halo

    vectors = vectors_ref[...]

    def vector(row):
        return vectors[row : row + 1, :]

    fetch_weights.wait()
    for block in range(low_ref.shape[0]):
        low_ref[block] = weights_buf[block].astype(bf16)
    half3 = (0.5 * low_ref[3].astype(f32)).astype(bf16)
    half4 = (0.5 * low_ref[4].astype(f32)).astype(bf16)
    latents = latents_ref[...]
    gather_ref[0:rows, :] = split_pair(0.5 * dot(table_ref[...], low_ref[2]))
    gather_ref[rows : rows + width, :] = jnp.concatenate(
        [(0.5 * low_ref[0].astype(f32)).astype(bf16), jnp.zeros((width, width), bf16)], axis=1
    )
    receiver_ref[0:particles, :] = 0.5 * (dot(latents, low_ref[1]) + vector(0))
    receiver_ref[particles:, :] = jnp.zeros((receiver_ref.shape[0] - particles, width), f32)

    fetch_list.wait()
    tiles = (listed[3, 0] + (GROUP - 1)) >> 5
    for copy in loads[0]:
        copy.wait()

    sublane = iota((CHUNK, width), 0)
    diagonal = iota((CHUNK, width), 1) - sublane
    lane16 = iota((TILE, width), 1).astype(jnp.int16)

    def flat(ref, t):
        return ref[pl.ds(t * GROUP, GROUP)].reshape(TILE, width)

    def keep(ref, t, values):
        ref[pl.ds(t * GROUP, GROUP)] = values.astype(ref.dtype).reshape(GROUP, CHUNK, width)

    def span(j):
        return slice(j * CHUNK, (j + 1) * CHUNK)

    def one_hot(t):
        index = flat(kept_index, t)
        return [
            jnp.where(index == lane16 + jnp.int16(b * width), bf16(1), bf16(0))
            for b in range(rows // width)
        ]

    def gather(t):
        base = t * GROUP
        for j in range(GROUP):
            chunk, particle = listed[0, base + j], listed[1, base + j]
            kept_edges[base + j] = edges_buf[chunk]
            row = jnp.broadcast_to(neighbour_rows[pl.ds(particle, 1), :], (CHUNK, width))
            start = (chunk & (per - 1)) * CHUNK
            index = row_sum(jnp.where(diagonal == start, row, 0.0))
            kept_index[base + j] = (
                jnp.broadcast_to(index, (CHUNK, width)).astype(i32).astype(jnp.int16)
            )
            receiver_tile[j : j + 1, :] = receiver_ref[pl.ds(particle, 1), :]
        gather_ref[rows + width : rows + width + GROUP, :] = split_pair(receiver_tile[...])

    def project(t):
        picks = jnp.concatenate(one_hot(t) + [flat(kept_edges, t), blocks_ref[0]], axis=1)
        first_tile[...] = halves(dot(picks, gather_ref[...]))

    gain_root = vector(3) * root

    def forward(t, carry):
        base = t * GROUP
        gather(t + 1)
        act, slope = silu_of_half(first_tile[...])
        act = act.astype(bf16)
        keep(kept_act1, t, act)
        keep(kept_slope1, t, slope)
        act, slope = silu_of_half(dot(act, half3) + 0.5 * vector(1))
        act = act.astype(bf16)
        keep(kept_act2, t, act)
        keep(kept_slope2, t, slope)
        last = dot(act, low_ref[4]) + vector(2)
        project(t + 1)
        unit, inverse = scaled_unit(last, width)
        keep(kept_unit, t, unit)
        keep(kept_inverse, t, jnp.broadcast_to(inverse, (TILE, width)))
        change = unit * gain_root + vector(4)
        for j in range(GROUP):
            chunk = listed[0, base + j]
            alive = sublane < listed[2, base + j]
            fresh = kept_edges[base + j].astype(f32) + jnp.where(alive, change[span(j)], 0.0)
            edges_buf[chunk] = fresh.astype(bf16)
            chunk_sums[pl.ds(base + j, 1), :] = column_total(jnp.where(alive, fresh, 0.0))
        return carry

    gather(0)
    project(0)
    lax.fori_loop(0, tiles, forward, 0)
    for ref in (kept_act1, kept_unit, kept_inverse):
        keep(ref, tiles, jnp.zeros((TILE, width), f32))

    stores = [
        pltpu.make_async_copy(
            edges_buf.at[pl.ds(p * piece, piece)],
            edges_out_hbm.at[pl.ds(p * piece, piece)],
            out_sems.at[p],
        )
        for p in range(PIECES)
    ]
    for copy in stores:
        copy.start()

    aggregate = halves(dot(segment_ref[...], split_pair(chunk_sums[...]))).astype(bf16)
    half1 = 0.5 * (dot(latents, low_ref[5]) + dot(aggregate, low_ref[6]) + vector(5))
    act1, slope1 = silu_of_half(half1)
    act1 = act1.astype(bf16)
    act2, slope2 = silu_of_half(0.5 * (dot(act1, low_ref[7]) + vector(6)))
    act2 = act2.astype(bf16)
    unit, inverse = scaled_unit(dot(act2, low_ref[8]) + vector(7), width)
    alive = (iota((particles, width), 0) < count_ref[0]).astype(f32)
    upstream = upstream_ref[...].astype(f32)
    nodes_out_ref[...] = (
        latents.astype(f32) + alive * (unit * (vector(8) * root) + vector(9))
    ).astype(bf16)
    held = alive * upstream
    third = scaled_unit_back(held * (vector(8) * root), unit, inverse, width).astype(bf16)
    second = (0.5 * slope2 * dot_nt(third, low_ref[8])).astype(bf16)
    first = (0.5 * slope1 * dot_nt(second, low_ref[7])).astype(bf16)
    receiver_ref[0:particles, :] = dot_nt(first, low_ref[6])
    node_part_ref[...] = upstream + dot_nt(first, low_ref[5])

    def put_block(block, values):
        grads[block * width : (block + 1) * width, :] = values

    put_block(5, dot_tn(latents, first))
    put_block(6, dot_tn(aggregate, first))
    put_block(7, dot_tn(act1, second))
    put_block(8, dot_tn(act2, third))
    for row, values in enumerate(
        (first.astype(f32), second.astype(f32), third.astype(f32), held * unit * root, held)
    ):
        grads[tail + 5 + row : tail + 6 + row, :] = column_total(values)

    for copy in loads[1]:
        copy.wait()

    def add_columns(row, values):
        vec_acc[8 * row : 8 * row + 8, :] += jnp.sum(values.reshape(TILE // 8, 8, width), axis=0)

    def accept(t):
        base = t * GROUP
        parts = []
        for j in range(GROUP):
            chunk, particle = listed[0, base + j], listed[1, base + j]
            alive = sublane < listed[2, base + j]
            passed = cotangent_buf[chunk].astype(f32) + jnp.where(
                alive, receiver_ref[pl.ds(particle, 1), :], 0.0
            )
            passed_tile[t & 3, span(j), :] = passed
            parts.append(jnp.where(alive, passed, 0.0))
        return jnp.concatenate(parts, axis=0)

    def descend(t, held):
        unit = flat(kept_unit, t).astype(f32)
        third = scaled_unit_back(held * gain_root, unit, flat(kept_inverse, t), width)
        third_tile[...] = third.astype(bf16)
        add_columns(2, third)
        add_columns(3, held * unit)
        add_columns(4, held)

    def settle(t, slot):
        base = t * GROUP
        first = first_back[...]
        result = passed_tile[slot] + dot_nt(first, low_ref[0])
        for j in range(GROUP):
            cotangent_buf[listed[0, base + j]] = result[span(j)].astype(bf16)
        picks = jnp.concatenate(one_hot(t) + [flat(kept_edges, t), blocks_ref[t & 3]], axis=1)
        index_acc[...] += dot_tn(first, picks[:, 0 : rows + width])
        chunk_grads[t >> 2] += dot_tn(first, picks[:, rows + width :])
        mat_acc[0] += dot_tn(flat(kept_act1, t), second_back[...])

    def backward(t, carry):
        third = third_tile[...]
        second = dot_nt(third, half4)
        held = accept(t + 1)
        settle(jnp.where(t == 0, tiles, t - 1), (t + 3) & 3)
        second = flat(kept_slope2, t).astype(f32) * second
        add_columns(1, second)
        second = second.astype(bf16)
        descend(t + 1, held)
        first = flat(kept_slope1, t).astype(f32) * dot_nt(second, half3)
        mat_acc[1] += dot_tn(flat(kept_act2, t), third)
        first_back[...] = first.astype(bf16)
        second_back[...] = second
        return carry

    first_back[...] = jnp.zeros(first_back.shape, bf16)
    second_back[...] = jnp.zeros(second_back.shape, bf16)
    passed_tile[3] = jnp.zeros((TILE, width), f32)
    descend(0, accept(0))
    results = [
        pltpu.make_async_copy(
            cotangent_buf.at[pl.ds(p * piece, piece)],
            edges_grad_hbm.at[pl.ds(p * piece, piece)],
            out_sems.at[PIECES + p],
        )
        for p in range(PIECES)
    ]
    lax.fori_loop(0, tiles, backward, 0)
    settle(jnp.where(tiles == 0, tiles, tiles - 1), (tiles + 3) & 3)
    for copy in results:
        copy.start()

    stacked = split_pair(
        jnp.concatenate([chunk_grads[g] for g in range(chunks // LANES)], axis=1), axis=0
    )
    receiver_grad = halves(dot_nt(segment_ref[...], stacked)).astype(bf16)
    grads[tail : tail + 1, :] = halves(dot_nt(jnp.ones((8, chunks), bf16), stacked))[0:1, :]
    for row in range(1, 5):
        values = column_total(vec_acc[8 * row : 8 * row + 8, :])
        grads[tail + row : tail + row + 1, :] = values * root if row == 3 else values
    sent = index_acc[:, 0:rows].astype(bf16)
    put_block(0, index_acc[:, rows:].T)
    put_block(1, dot_tn(latents, receiver_grad))
    put_block(2, dot(sent, table_ref[...]).T)
    put_block(3, mat_acc[0])
    put_block(4, mat_acc[1])
    table_grad = lax.dot_general(
        sent, low_ref[2], (((0,), (1,)), ((), ())), preferred_element_type=f32
    )
    node_part_ref[...] += dot_nt(receiver_grad, low_ref[1]) + table_grad[0:particles, :]
    halo_grad[...] = table_grad[particles:, :].astype(bf16)
    low_x = halo_grad[0 : 3 * halo, :]
    high_x = halo_grad[5 * halo : 8 * halo, :]
    halo_own_ref[0:halo, :] = halo_grad[3 * halo : 4 * halo, :]
    halo_own_ref[halo : 2 * halo, :] = jnp.zeros((halo, width), bf16)
    halo_own_ref[2 * halo :, :] = halo_grad[4 * halo : 5 * halo, :]
    quarter = grads.shape[0] // 8
    order = (lax.axis_index("gx") >> 1) & 3 if relayed else 0
    relay = 2 * quarter
    send_ref[relay : relay + 3 * halo, :] = jnp.where(odd_x == 0, low_x, high_x)
    send_ref[relay + 2 * quarter + 3 * halo :, :] = jnp.where(odd_x == 0, high_x, low_x)
    keep_ref[relay : relay + 3 * halo, :] = jnp.zeros((3 * halo, width), f32)
    for slot, spot in enumerate(slot_rows(quarter, halo)):
        inner = (slot ^ order) * quarter
        kept_rows = pl.ds(pl.multiple_of(odd_x * 4 * quarter + inner, 16), quarter)
        sent_rows = pl.ds(pl.multiple_of((1 - odd_x) * 4 * quarter + inner, 16), quarter)
        keep_ref[spot : spot + quarter, :] = grads[kept_rows, :]
        send_ref[spot : spot + quarter, :] = grads[sent_rows, :].astype(bf16)

    for copy in stores + results:
        copy.wait()


def layer_call(
    halo, relayed, grad_rows, counts, neighbours, edge_mask, latents, ring, ring_far, ring_near, upstream,
    vectors, weights, edges, cotangents,
):
    f32, bf16, i32 = jnp.float32, jnp.bfloat16, jnp.int32
    particles, slots = neighbours.shape
    width = latents.shape[1]
    rows = particles + 8 * halo
    chunks = particles * slots // CHUNK
    whole = pl.BlockSpec(memory_space=pltpu.VMEM)
    outside = pl.BlockSpec(memory_space=pl.ANY)
    edge_shape = (chunks, CHUNK, width)
    kept_shape = (chunks + GROUP, CHUNK, width)
    kept = pltpu.VMEM(kept_shape, bf16)
    buffer = pltpu.VMEM((chunks + 1, CHUNK, width), bf16)
    half = grad_rows // 2
    return pl.pallas_call(
        functools.partial(layer_kernel, halo, relayed),
        out_shape=(
            jax.ShapeDtypeStruct((particles, width), bf16),
            jax.ShapeDtypeStruct(edge_shape, bf16),
            jax.ShapeDtypeStruct(edge_shape, bf16),
            jax.ShapeDtypeStruct((particles, width), f32),
            jax.ShapeDtypeStruct((3 * halo, width), bf16),
            jax.ShapeDtypeStruct((half + 6 * halo, width), bf16),
            jax.ShapeDtypeStruct((half + 3 * halo, width), f32),
        ),
        in_specs=[pl.BlockSpec(memory_space=pltpu.SMEM)] + [whole] * 8 + [outside] * 3,
        out_specs=(whole, outside, outside, whole, whole, whole, whole),
        scratch_shapes=[
            buffer,
            buffer,
            kept,
            pltpu.VMEM(kept_shape, jnp.int16),
            kept,
            kept,
            kept,
            kept,
            kept,
            pltpu.VMEM(kept_shape, f32),
            pltpu.VMEM(weights.shape, f32),
            pltpu.VMEM(weights.shape, bf16),
            pltpu.VMEM((rows, width), bf16),
            pltpu.VMEM((rows + width + LANES, 2 * width), bf16),
            pltpu.VMEM((particles + 8, width), f32),
            pltpu.VMEM((GROUP, width), f32),
            pltpu.VMEM((particles + 8, width), f32),
            pltpu.VMEM((particles, chunks), bf16),
            pltpu.VMEM((LANES // GROUP, TILE, LANES), bf16),
            pltpu.VMEM((chunks, width), f32),
            pltpu.VMEM((chunks // LANES + 1, width, LANES), f32),
            pltpu.VMEM((width, rows + width), f32),
            pltpu.VMEM((2, width, width), f32),
            pltpu.VMEM((40, width), f32),
            pltpu.VMEM((TILE, width), f32),
            pltpu.VMEM((TILE, width), bf16),
            pltpu.VMEM((TILE, width), bf16),
            pltpu.VMEM((TILE, width), bf16),
            pltpu.VMEM((4, TILE, width), f32),
            pltpu.VMEM((8 * halo, width), bf16),
            pltpu.VMEM((grad_rows, width), f32),
            pltpu.VMEM((8, chunks + LANES), i32),
            pltpu.SMEM((8, chunks + LANES), i32),
            pltpu.SemaphoreType.DMA((2 * PIECES,)),
            pltpu.SemaphoreType.DMA((2 * PIECES,)),
            pltpu.SemaphoreType.DMA,
            pltpu.SemaphoreType.DMA,
        ],
        compiler_params=pltpu.CompilerParams(vmem_limit_bytes=60 * 1024 * 1024),
        name="edge_layer",
    )(
        counts,
        neighbours.T,
        edge_mask.T,
        latents,
        ring,
        ring_far,
        ring_near,
        upstream,
        vectors,
        weights,
        edges.reshape(edge_shape),
        cotangents.reshape(edge_shape),
    )


def update_kernel(
    relayed,
    part0_ref,
    part1_ref,
    part2_ref,
    part3_ref,
    weights_ref,
    vectors_ref,
    weights_m_ref,
    vectors_m_ref,
    weights_v_ref,
    vectors_v_ref,
    weights_ema_ref,
    vectors_ema_ref,
    norm_ref,
    weights_m_out,
    vectors_m_out,
    weights_v_out,
    vectors_v_out,
    weights_out,
    vectors_out,
    weights_copy_out,
    vectors_copy_out,
    weights_ema_out,
    vectors_ema_out,
    grads,
):
    f32 = jnp.float32
    odd = lax.axis_index("gx") & 1
    pair_rows, width = part0_ref.shape
    quarter = pair_rows // 2
    order = (lax.axis_index("gx") >> 1) & 3 if relayed else 0
    squares = jnp.zeros((8, width), f32)
    for slot, part_ref in enumerate((part0_ref, part1_ref, part2_ref, part3_ref)):
        part = part_ref[...].astype(f32)
        for side in range(2):
            values = part[side * quarter : (side + 1) * quarter, :]
            spot = ((odd ^ side) * 4 + (slot ^ order)) * quarter
            grads[pl.ds(pl.multiple_of(spot, 16), quarter), :] = values
            squares = squares + jnp.sum((values * values).reshape(quarter // 8, 8, width), axis=0)
    norm = jnp.sqrt(jnp.sum(jnp.sum(squares, axis=1, keepdims=True), axis=0, keepdims=True))
    norm_ref[...] = norm
    scale = clip_norm / jnp.maximum(norm, clip_norm)
    for block in range(weights_ref.shape[0]):
        moment, second, param, average = adamw(
            weights_ref[block],
            grads[block * width : (block + 1) * width, :],
            weights_m_ref[block],
            weights_v_ref[block],
            weights_ema_ref[block],
            scale,
            matrix_rate,
        )
        weights_m_out[block] = moment
        weights_v_out[block] = second
        weights_out[block] = param
        weights_copy_out[block] = param.astype(jnp.bfloat16)
        weights_ema_out[block] = average
    tail = weights_ref.shape[0] * width
    moment, second, param, average = adamw(
        vectors_ref[...],
        grads[tail : tail + vectors_ref.shape[0], :],
        vectors_m_ref[...],
        vectors_v_ref[...],
        vectors_ema_ref[...],
        scale,
        vector_rate,
    )
    vectors_m_out[...] = moment
    vectors_v_out[...] = second
    vectors_out[...] = param
    vectors_copy_out[...] = param.astype(jnp.bfloat16)
    vectors_ema_out[...] = average


def update_call(relayed, parts, weights, vectors, weights_m, vectors_m, weights_v, vectors_v,
                weights_ema, vectors_ema):
    f32, bf16 = jnp.float32, jnp.bfloat16
    mat, vec = weights.shape, vectors.shape
    kinds = (
        ((1, 1), f32), (mat, f32), (vec, f32), (mat, f32), (vec, f32), (mat, f32), (vec, f32),
        (mat, bf16), (vec, bf16), (mat, f32), (vec, f32),
    )
    whole = pl.BlockSpec(memory_space=pltpu.VMEM)
    return pl.pallas_call(
        functools.partial(update_kernel, relayed),
        out_shape=tuple(jax.ShapeDtypeStruct(*kind) for kind in kinds),
        in_specs=[whole] * 12,
        out_specs=(whole,) * 11,
        scratch_shapes=[pltpu.VMEM((4 * parts[0].shape[0], parts[0].shape[1]), f32)],
        compiler_params=pltpu.CompilerParams(vmem_limit_bytes=24 * 1024 * 1024),
        name="update",
    )(*parts, weights, vectors, weights_m, vectors_m, weights_v, vectors_v, weights_ema,
      vectors_ema)


def pair_exchange(to_far, to_near, axis):
    near, far = neighbour_pairs(lax.axis_size(axis))
    return lax.ppermute(to_far, axis, far), lax.ppermute(to_near, axis, near)


def partners(axis, stride, mask):
    return [(i, i ^ (mask * stride)) for i in range(lax.axis_size(axis))]


def even_pick(axis, even, odd):
    return jnp.where(lax.axis_index(axis) % 2 == 0, even, odd)


def swap(values, axis, stride, mask):
    return lax.ppermute(values, axis, partners(axis, stride, mask))


def tree_sum(terms):
    while len(terms) > 1:
        terms = [terms[i] + terms[i + 1] for i in range(0, len(terms), 2)]
    return terms[0]


def sum_relayed(send, keep, halo_own, halo):
    f32, bf16 = jnp.float32, jnp.bfloat16
    quarter = (send.shape[0] - 6 * halo) // 4
    slots = slot_rows(quarter, halo)
    index, row = lax.axis_index("gx"), lax.axis_index("gy")
    got = swap(send, "gx", 1, 1)
    near = got[4 * quarter + 3 * halo :].astype(f32)
    total = (keep + got[: 4 * quarter + 3 * halo].astype(f32)).astype(bf16)
    from3 = swap(total[2 * quarter : 3 * quarter + 3 * halo], "gx", 2, 3)
    from2 = swap(total[slots[2] : slots[2] + quarter], "gx", 2, 2)
    from1 = swap(total[quarter : 2 * quarter + 3 * halo], "gx", 2, 1)
    mine = tree_sum(
        [
            total[:quarter].astype(f32),
            from1[:quarter].astype(f32),
            from2.astype(f32),
            from3[3 * halo :].astype(f32),
        ]
    ).astype(bf16)
    far = jnp.where((index == 3) | (index == 4), from3[: 3 * halo], from1[quarter:])
    far = jnp.where((index == 0) | (index == 7), 0.0, far.astype(f32))
    strips = halo_own + near + far
    low, high = strips[:halo].astype(bf16), strips[2 * halo :].astype(bf16)
    along3 = swap(jnp.concatenate([even_pick("gy", low, high), mine]), "gy", 1, 3)
    along2 = swap(mine, "gy", 1, 2)
    along1 = swap(jnp.concatenate([even_pick("gy", high, low), mine]), "gy", 1, 1)
    mine = tree_sum(
        [
            mine.astype(f32),
            along1[halo:].astype(f32),
            along2.astype(f32),
            along3[halo:].astype(f32),
        ]
    ).astype(bf16)
    last_far = jnp.where((row == 0) | (row == 3), bf16(0), along3[:halo])
    pair = jnp.concatenate([mine, swap(mine, "gx", 1, 1)])
    parts = [pair] + [None] * 3
    for mask in (3, 2, 1):
        parts[mask] = swap(pair, "gx", 2, mask)
    return parts, strips, last_far, along1[:halo]


def sum_staged(send, keep, halo_own, halo):
    f32, bf16 = jnp.float32, jnp.bfloat16
    width = send.shape[1]
    quarter = (send.shape[0] - 6 * halo) // 4
    slots = slot_rows(quarter, halo)

    def joined_slots(values):
        return jnp.concatenate([values[spot : spot + quarter] for spot in slots])

    far = send[2 * quarter : 2 * quarter + 3 * halo]
    near = send[4 * quarter + 3 * halo :]
    back_far, back_near = pair_exchange(far, near, "gx")
    strips = halo_own + back_far.astype(f32) + back_near.astype(f32)
    low, high = strips[:halo].astype(bf16), strips[2 * halo :].astype(bf16)
    last_far, last_near = pair_exchange(
        even_pick("gy", low, high), even_pick("gy", high, low), "gy"
    )
    index = lax.axis_index("gx")
    got = swap(joined_slots(send), "gx", 1, 1)
    total = (joined_slots(keep) + got.astype(f32)).astype(bf16)
    split = stages(lax.axis_size("gx"))[1:]
    for stride, factor in split:
        part = (index // stride) % factor
        height = total.shape[0] // factor
        mine = lax.dynamic_slice_in_dim(total, part * height, height, 0).astype(f32)
        for mask in range(factor - 1, 0, -1):
            piece = lax.dynamic_slice_in_dim(total, (part ^ mask) * height, height, 0)
            mine = mine + swap(piece, "gx", stride, mask).astype(f32)
        total = mine.astype(bf16)
    total = tree_sum(
        [total.astype(f32)]
        + [swap(total, "gy", 1, mask).astype(f32) for mask in range(1, lax.axis_size("gy"))]
    ).astype(bf16)
    for stride, factor in reversed(split):
        part = (index // stride) % factor
        height = total.shape[0]
        joined = jnp.zeros((factor * height, width), bf16)
        joined = lax.dynamic_update_slice_in_dim(joined, total, part * height, 0)
        for mask in range(factor - 1, 0, -1):
            piece = swap(total, "gx", stride, mask)
            joined = lax.dynamic_update_slice_in_dim(joined, piece, (part ^ mask) * height, 0)
        total = joined
    other = swap(total, "gx", 1, 1)
    parts = [
        jnp.concatenate([half[m * quarter : (m + 1) * quarter] for half in (total, other)])
        for m in range(4)
    ]
    return parts, strips, last_far, last_near


def per_device(
    node_latents,
    edge_latents,
    node_cotangent,
    edge_cotangent,
    neighbours,
    edge_mask,
    send_table,
    counts,
    weights,
    vectors,
    weights_m,
    vectors_m,
    weights_v,
    vectors_v,
    weights_ema,
    vectors_ema,
):
    f32, bf16 = jnp.float32, jnp.bfloat16
    tok_rows, width = node_latents.shape
    halo = send_table.shape[1]
    boundary_pick = selector(send_table[0], tok_rows, bf16)
    boundary = jnp.dot(boundary_pick, node_latents, preferred_element_type=f32).astype(bf16)
    from_far, from_near = pair_exchange(boundary, boundary, "gx")
    ring = jnp.concatenate([from_far, from_near, boundary], axis=0)
    ring_far, ring_near = pair_exchange(ring, ring, "gy")
    unit = 16 * lax.axis_size("gx")
    grad_rows = -(-(weights.shape[0] * width + vectors.shape[0]) // unit) * unit
    relayed = lax.axis_size("gx") == 8 and lax.axis_size("gy") == 4
    nodes_out, edges_out, edges_in_grad, node_part, halo_own, send, keep = layer_call(
        halo, relayed, grad_rows, counts, neighbours, edge_mask, node_latents, ring, ring_far,
        ring_near, node_cotangent, vectors, weights, edge_latents, edge_cotangent,
    )
    sums = sum_relayed if relayed else sum_staged
    parts, strips, last_far, last_near = sums(send, keep, halo_own.astype(f32), halo)
    boundary_grad = strips[halo : 2 * halo] + last_far.astype(f32) + last_near.astype(f32)
    returned = lax.dot_general(
        boundary_pick.astype(f32),
        boundary_grad,
        (((0,), (0,)), ((), ())),
        precision=lax.Precision.HIGHEST,
        preferred_element_type=f32,
    )
    nodes_in_grad = (node_part + returned).astype(bf16)
    updated = update_call(
        relayed, parts, weights, vectors, weights_m, vectors_m, weights_v, vectors_v, weights_ema,
        vectors_ema,
    )
    return (
        nodes_out,
        edges_out.reshape(edge_latents.shape),
        nodes_in_grad,
        edges_in_grad.reshape(edge_latents.shape),
        updated[0].reshape(()),
    ) + tuple(updated[1:])


def solution(mesh):
    in_specs = (
        P(("gx", "gy"), None),
        P(("gx", "gy"), None, None),
        P(("gx", "gy"), None),
        P(("gx", "gy"), None, None),
        P(("gx", "gy"), None),
        P(("gx", "gy"), None),
        P(("gx", "gy"), None),
        P(("gx", "gy")),
        P(),
        P(),
        P(),
        P(),
        P(),
        P(),
        P(),
        P(),
    )
    out_specs = (
        P(("gx", "gy"), None),
        P(("gx", "gy"), None, None),
        P(("gx", "gy"), None),
        P(("gx", "gy"), None, None),
        P(),
        P(),
        P(),
        P(),
        P(),
        P(),
        P(),
        P(),
        P(),
        P(),
        P(),
    )
    return jax.shard_map(
        per_device, mesh=mesh, in_specs=in_specs, out_specs=out_specs, check_vma=False
    )
```

```python
import functools

import jax
import jax.numpy as jnp
from jax import lax
from jax.experimental import pallas as pl
from jax.experimental.pallas import tpu as pltpu
from jax.sharding import PartitionSpec as P

STEP = 10


first_decay = 0.5
second_decay = 0.5
adam_epsilon = 1e-08
weight_decay = 0.01
matrix_rate = 0.05
vector_rate = 0.2
average_decay = 0.9
clip_norm = 1.0
norm_epsilon = 1e-05


def neighbour_pairs(count):
    near = [(i, i ^ 1) for i in range(count) if (i ^ 1) < count]
    far = [(i, i + 1) for i in range(1, count - 1, 2)]
    return near, far + [(target, source) for source, target in far]


def stages(count):
    result, stride = [], 1
    while stride < count:
        factor = 2 if stride == 1 else min(4, count // stride)
        result.append((stride, factor))
        stride *= factor
    return result


def selector(indices, width, dtype):
    columns = lax.broadcasted_iota(jnp.int32, (indices.shape[0], width), 1)
    return (indices[:, None] == columns).astype(dtype)


def adamw(param, grad, moment, second, average, scale, rate):
    clipped = grad * scale
    moment_new = first_decay * moment + (1.0 - first_decay) * clipped
    second_new = second_decay * second + (1.0 - second_decay) * clipped * clipped
    corrected = moment_new / (1.0 - first_decay**STEP)
    denom = jnp.sqrt(second_new / (1.0 - second_decay**STEP)) + adam_epsilon
    param_new = param - rate * (corrected / denom + weight_decay * param)
    average_new = average_decay * average + (1.0 - average_decay) * param_new
    return (moment_new, second_new, param_new, average_new)


CHUNK = 16
GROUP = 32
TILE = CHUNK * GROUP
LANES = 128
PIECES = 8


def dot(left, right):
    return jnp.dot(left, right, preferred_element_type=jnp.float32)


def dot_nt(left, right):
    return lax.dot_general(
        left, right, (((1,), (1,)), ((), ())), preferred_element_type=jnp.float32
    )


def dot_tn(left, right):
    return lax.dot_general(
        left, right, (((0,), (0,)), ((), ())), preferred_element_type=jnp.float32
    )


def split_pair(values, axis=1):
    high = values.astype(jnp.bfloat16)
    low = (values - high.astype(jnp.float32)).astype(jnp.bfloat16)
    return jnp.concatenate([high, low], axis=axis)


def halves(pair):
    width = pair.shape[1] // 2
    return pair[:, :width] + pair[:, width:]


def silu_of_half(half):
    turn = jnp.tanh(half)
    lift = 1.0 + turn
    act = half * lift
    return act, lift + act * (1.0 - turn)


def row_sum(values):
    return jnp.sum(values, axis=-1, keepdims=True)


def scaled_unit(values, width):
    center = values - row_sum(values) * (1.0 / width)
    inverse = lax.rsqrt(row_sum(center * center) + width * norm_epsilon)
    return center * inverse, inverse


def scaled_unit_back(scaled, unit, inverse, width):
    shift = row_sum(scaled) * (1.0 / width)
    return inverse * (scaled - shift - unit * row_sum(scaled * unit))


def column_total(values):
    return jnp.sum(values, axis=0, keepdims=True)


def iota(shape, dim):
    return lax.broadcasted_iota(jnp.int32, shape, dim)


def slot_rows(quarter, halo):
    return (0, quarter, 2 * quarter + 3 * halo, 3 * quarter + 3 * halo)


def part_rows(relayed, side, slot, quarter):
    chip = lax.axis_index("gx") >> 1
    part = (chip + slot * (1 - 2 * side)) & 3 if relayed else slot
    return pl.ds(pl.multiple_of((side * 4 + part) * quarter, 16), quarter)


def plan_kernel(
    halo,
    neighbour_ref,
    mask_ref,
    latents_ref,
    vectors_ref,
    weights_hbm,
    edges_hbm,
    edges_buf,
    list_rows,
    segment_ref,
    neighbour_rows,
    receiver_ref,
    low_ref,
    gather_ref,
    blocks_ref,
    weights_ref,
    sems,
):
    f32, bf16, i32 = jnp.float32, jnp.bfloat16, jnp.int32
    slots, particles = neighbour_ref.shape
    per = slots // CHUNK
    chunks = particles * per
    width = latents_ref.shape[1]
    rows = particles + 8 * halo
    fetch_weights = pltpu.make_async_copy(weights_hbm, weights_ref, sems.at[0])
    fetch_weights.start()
    piece = chunks // PIECES
    loads = [
        pltpu.make_async_copy(
            edges_hbm.at[pl.ds(p * piece, piece)],
            edges_buf.at[pl.ds(p * piece, piece)],
            sems.at[1 + p],
        )
        for p in range(PIECES)
    ]
    for copy in loads:
        copy.start()
    edges_buf[chunks] = jnp.zeros((CHUNK, width), bf16)

    mask = mask_ref[...].astype(f32)
    degree = jnp.sum(mask, axis=0, keepdims=True)
    taken = ((degree.astype(i32) + (CHUNK - 1)) >> 4).astype(f32)
    earlier = iota((particles, particles), 0) < iota((particles, particles), 1)
    begin = dot(jnp.broadcast_to(taken, (16, particles)).astype(bf16), earlier.astype(bf16))
    degree_col = dot_tn(mask.astype(bf16), jnp.ones((slots, width), bf16))
    taken_col = ((degree_col.astype(i32) + (CHUNK - 1)) >> 4).astype(f32)
    later = iota((particles, particles), 1) < iota((particles, particles), 0)
    begin_col = dot(later.astype(bf16), taken_col.astype(bf16))
    end_col = begin_col + taken_col
    for block in range(chunks // width):
        lane = iota((particles, width), 1).astype(f32) + block * width
        segment_ref[:, block * width : (block + 1) * width] = (
            (lane >= begin_col) & (lane < end_col)
        ).astype(bf16)
    total = row_sum(taken)
    who = iota((16, particles), 1).astype(f32)
    offset = per * who - begin
    coarse = jnp.floor(offset * 0.125) * 8.0
    line = iota((16, particles), 0)
    facts = jnp.where(
        line == 0,
        who,
        jnp.where(line == 1, coarse, jnp.where(line == 2, offset - coarse, degree)),
    )
    listing = dot(facts.astype(bf16), segment_ref[...])
    place = iota((1, chunks), 1).astype(f32)
    particle = listing[0:1, :]
    chunk = listing[1:2, :] + listing[2:3, :] + place
    rest = listing[3:4, :] - CHUNK * (chunk - per * particle)
    used = place < total
    list_rows[...] = jnp.zeros(list_rows.shape, i32)
    list_rows[0:1, 0:chunks] = jnp.where(used, chunk, float(chunks)).astype(i32)
    list_rows[0:1, chunks:] = jnp.full((1, list_rows.shape[1] - chunks), chunks, i32)
    list_rows[1:2, 0:chunks] = jnp.where(used, particle, float(particles)).astype(i32)
    list_rows[1:2, chunks:] = jnp.full((1, list_rows.shape[1] - chunks), particles, i32)
    list_rows[2:3, 0:chunks] = jnp.where(used, rest, 0.0).astype(i32)
    list_rows[3:4, 0:particles] = jnp.broadcast_to(total, (1, particles)).astype(i32)
    list_rows[4:5, 0:particles] = (begin[0:1, :] + taken).astype(i32)

    neighbour = neighbour_ref[...]
    neighbour = jnp.where(neighbour >= particles + 5 * halo, neighbour - halo, neighbour)
    neighbour_rows[...] = jnp.zeros(neighbour_rows.shape, f32)
    neighbour_rows[0:particles, 0:slots] = neighbour.astype(f32).T

    block_of = iota((TILE, LANES), 0) >> 4
    for quarter in range(LANES // GROUP):
        blocks_ref[quarter] = (iota((TILE, LANES), 1) == block_of + quarter * GROUP).astype(bf16)

    fetch_weights.wait()
    for block in range(weights_ref.shape[0]):
        low_ref[block] = weights_ref[block].astype(bf16)
    for extra, block in ((9, 3), (10, 4)):
        low_ref[extra] = (0.5 * low_ref[block].astype(f32)).astype(bf16)
    latents = latents_ref[...]
    gather_ref[0:particles, :] = split_pair(0.5 * dot(latents, low_ref[2]))
    gather_ref[particles:rows, :] = jnp.zeros((rows - particles, 2 * width), bf16)
    gather_ref[rows : rows + width, :] = jnp.concatenate(
        [(0.5 * low_ref[0].astype(f32)).astype(bf16), jnp.zeros((width, width), bf16)], axis=1
    )
    gather_ref[rows + width :, :] = jnp.zeros((LANES, 2 * width), bf16)
    receiver_ref[0:particles, :] = 0.5 * (dot(latents, low_ref[1]) + vectors_ref[0:1, :])
    receiver_ref[particles:, :] = jnp.zeros((receiver_ref.shape[0] - particles, width), f32)
    for copy in loads:
        copy.wait()


def layer_kernel(
    halo,
    relayed,
    count_ref,
    latents_ref,
    ring_ref,
    ring_far_ref,
    ring_near_ref,
    upstream_ref,
    vectors_ref,
    list_rows,
    segment_ref,
    neighbour_rows,
    receiver_ref,
    low_ref,
    blocks_ref,
    edges_in,
    gather_in,
    cotangent_hbm,
    nodes_out_ref,
    edges_out_hbm,
    edges_grad_hbm,
    node_part_ref,
    halo_own_ref,
    send_ref,
    keep_ref,
    edges_buf,
    gather_ref,
    cotangent_buf,
    kept_edges,
    kept_index,
    kept_act1,
    kept_act2,
    kept_slope1,
    kept_slope2,
    kept_unit,
    kept_inverse,
    table_ref,
    descent_ref,
    receiver_tile,
    chunk_sums,
    chunk_grads,
    index_acc,
    mat_acc,
    vec_acc,
    first_tile,
    last_tile,
    third_tile,
    first_back,
    second_back,
    passed_tile,
    halo_grad,
    grads,
    listed,
    in_sems,
    out_sems,
    list_sem,
):
    f32, bf16, i32 = jnp.float32, jnp.bfloat16, jnp.int32
    fetch_list = pltpu.make_async_copy(list_rows, listed, list_sem)
    fetch_list.start()
    particles, chunks = segment_ref.shape
    per = chunks // particles
    width = latents_ref.shape[1]
    rows = table_ref.shape[0]
    piece = chunks // PIECES
    root = float(width) ** 0.5
    odd_x = lax.axis_index("gx") & 1
    odd_y = lax.axis_index("gy") & 1
    loads = [
        pltpu.make_async_copy(
            cotangent_hbm.at[pl.ds(p * piece, piece)],
            cotangent_buf.at[pl.ds(p * piece, piece)],
            in_sems.at[p],
        )
        for p in range(PIECES)
    ]
    for copy in loads:
        copy.start()
    cotangent_buf[chunks] = jnp.zeros((CHUNK, width), bf16)

    table_ref[0:particles, :] = latents_ref[...]
    far, near, own = ring_far_ref[...], ring_near_ref[...], ring_ref[...]
    low_y = jnp.where(odd_y == 0, far, near)
    high_y = jnp.where(odd_y == 0, near, far)
    spot = particles
    for a in range(3):
        for b, strip in enumerate((low_y, own, high_y)):
            if a == 1 and b == 1:
                continue
            if a == 1:
                part = strip[2 * halo :]
            elif a == 0:
                part = jnp.where(odd_x == 0, strip[0:halo], strip[halo : 2 * halo])
            else:
                part = jnp.where(odd_x == 0, strip[halo : 2 * halo], strip[0:halo])
            table_ref[spot : spot + halo, :] = part
            spot += halo

    vectors = vectors_ref[...]

    def vector(row):
        return vectors[row : row + 1, :]

    latents = latents_ref[...]
    half3, half4 = low_ref[9], low_ref[10]
    gather_ref[particles:rows, :] = split_pair(0.5 * dot(table_ref[particles:, :], low_ref[2]))
    chunk_sums[...] = jnp.zeros(chunk_sums.shape, f32)
    chunk_grads[...] = jnp.zeros(chunk_grads.shape, f32)
    index_acc[...] = jnp.zeros(index_acc.shape, f32)
    mat_acc[...] = jnp.zeros(mat_acc.shape, f32)
    vec_acc[...] = jnp.zeros(vec_acc.shape, f32)
    tail = 9 * width
    grads[tail:, :] = jnp.zeros((grads.shape[0] - tail, width), f32)
    descent_ref[particles:, :] = jnp.zeros((descent_ref.shape[0] - particles, width), f32)

    fetch_list.wait()
    tiles = (listed[3, 0] + (GROUP - 1)) >> 5

    sublane = iota((CHUNK, width), 0)
    diagonal = iota((CHUNK, width), 1) - sublane
    lane16 = iota((TILE, width), 1).astype(jnp.int16)

    def flat(ref, t):
        return ref[pl.ds(t * GROUP, GROUP)].reshape(TILE, width)

    def keep(ref, t, values):
        ref[pl.ds(t * GROUP, GROUP)] = values.astype(ref.dtype).reshape(GROUP, CHUNK, width)

    def span(j):
        return slice(j * CHUNK, (j + 1) * CHUNK)

    def one_hot(t):
        index = flat(kept_index, t)
        return [
            jnp.where(index == lane16 + jnp.int16(b * width), bf16(1), bf16(0))
            for b in range(rows // width)
        ]

    def gather(t):
        base = t * GROUP
        for j in range(GROUP):
            chunk, particle = listed[0, base + j], listed[1, base + j]
            kept_edges[base + j] = edges_buf[chunk]
            row = jnp.broadcast_to(neighbour_rows[pl.ds(particle, 1), :], (CHUNK, width))
            start = (chunk & (per - 1)) * CHUNK
            index = row_sum(jnp.where(diagonal == start, row, 0.0))
            kept_index[base + j] = (
                jnp.broadcast_to(index, (CHUNK, width)).astype(i32).astype(jnp.int16)
            )
            receiver_tile[j : j + 1, :] = receiver_ref[pl.ds(particle, 1), :]
        gather_ref[rows + width : rows + width + GROUP, :] = split_pair(receiver_tile[...])

    def project(t):
        picks = jnp.concatenate(one_hot(t) + [flat(kept_edges, t), blocks_ref[0]], axis=1)
        first_tile[...] = halves(dot(picks, gather_ref[...]))

    gain_root = vector(3) * root

    def finish(t):
        base = t * GROUP
        unit, inverse = scaled_unit(last_tile[...], width)
        keep(kept_unit, t, unit)
        keep(kept_inverse, t, jnp.broadcast_to(inverse, (TILE, width)))
        change = unit * gain_root + vector(4)
        for j in range(GROUP):
            chunk = listed[0, base + j]
            alive = sublane < listed[2, base + j]
            fresh = kept_edges[base + j].astype(f32) + jnp.where(alive, change[span(j)], 0.0)
            edges_buf[chunk] = fresh.astype(bf16)
            chunk_sums[pl.ds(base + j, 1), :] = column_total(jnp.where(alive, fresh, 0.0))

    def forward(t, carry):
        gather(t + 1)
        act, slope = silu_of_half(first_tile[...])
        act = act.astype(bf16)
        keep(kept_act1, t, act)
        keep(kept_slope1, t, slope)
        finish(jnp.where(t == 0, tiles, t - 1))
        act, slope = silu_of_half(dot(act, half3) + 0.5 * vector(1))
        act = act.astype(bf16)
        keep(kept_act2, t, act)
        keep(kept_slope2, t, slope)
        project(t + 1)
        last_tile[...] = dot(act, low_ref[4]) + vector(2)
        return carry

    for ref in (kept_act1, kept_edges):
        keep(ref, tiles, jnp.zeros((TILE, width), f32))
    last_tile[...] = jnp.zeros(last_tile.shape, f32)
    gather(0)
    project(0)
    lax.fori_loop(0, tiles, forward, 0)
    finish(jnp.where(tiles == 0, tiles, tiles - 1))

    stores = [
        pltpu.make_async_copy(
            edges_buf.at[pl.ds(p * piece, piece)],
            edges_out_hbm.at[pl.ds(p * piece, piece)],
            out_sems.at[p],
        )
        for p in range(PIECES)
    ]
    for copy in stores:
        copy.start()

    aggregate = halves(dot(segment_ref[...], split_pair(chunk_sums[0:chunks, :]))).astype(bf16)
    half1 = 0.5 * (dot(latents, low_ref[5]) + dot(aggregate, low_ref[6]) + vector(5))
    act1, slope1 = silu_of_half(half1)
    act1 = act1.astype(bf16)
    act2, slope2 = silu_of_half(0.5 * (dot(act1, low_ref[7]) + vector(6)))
    act2 = act2.astype(bf16)
    unit, inverse = scaled_unit(dot(act2, low_ref[8]) + vector(7), width)
    alive = (iota((particles, width), 0) < count_ref[0]).astype(f32)
    upstream = upstream_ref[...].astype(f32)
    nodes_out_ref[...] = (
        latents.astype(f32) + alive * (unit * (vector(8) * root) + vector(9))
    ).astype(bf16)
    held = alive * upstream
    third = scaled_unit_back(held * (vector(8) * root), unit, inverse, width).astype(bf16)
    second = (0.5 * slope2 * dot_nt(third, low_ref[8])).astype(bf16)
    first = (0.5 * slope1 * dot_nt(second, low_ref[7])).astype(bf16)
    descent_ref[0:particles, :] = dot_nt(first, low_ref[6])
    node_part_ref[...] = upstream + dot_nt(first, low_ref[5])

    def put_block(block, values):
        grads[block * width : (block + 1) * width, :] = values

    put_block(5, dot_tn(latents, first))
    put_block(6, dot_tn(aggregate, first))
    put_block(7, dot_tn(act1, second))
    put_block(8, dot_tn(act2, third))
    for row, values in enumerate(
        (first.astype(f32), second.astype(f32), third.astype(f32), held * unit * root, held)
    ):
        grads[tail + 5 + row : tail + 6 + row, :] = column_total(values)

    for copy in loads:
        copy.wait()

    def add_columns(row, values):
        vec_acc[8 * row : 8 * row + 8, :] += jnp.sum(values.reshape(TILE // 8, 8, width), axis=0)

    def accept(t):
        base = t * GROUP
        parts = []
        for j in range(GROUP):
            chunk, particle = listed[0, base + j], listed[1, base + j]
            alive = sublane < listed[2, base + j]
            passed = cotangent_buf[chunk].astype(f32) + jnp.where(
                alive, descent_ref[pl.ds(particle, 1), :], 0.0
            )
            passed_tile[t & 3, span(j), :] = passed
            parts.append(jnp.where(alive, passed, 0.0))
        return jnp.concatenate(parts, axis=0)

    def descend(t, held):
        unit = flat(kept_unit, t).astype(f32)
        third = scaled_unit_back(held * gain_root, unit, flat(kept_inverse, t), width)
        third_tile[...] = third.astype(bf16)
        add_columns(2, third)
        add_columns(3, held * unit)
        add_columns(4, held)

    def settle(t, slot):
        base = t * GROUP
        first = first_back[...]
        result = passed_tile[slot] + dot_nt(first, low_ref[0])
        for j in range(GROUP):
            cotangent_buf[listed[0, base + j]] = result[span(j)].astype(bf16)
        picks = jnp.concatenate(one_hot(t) + [flat(kept_edges, t), blocks_ref[t & 3]], axis=1)
        index_acc[...] += dot_tn(first, picks[:, 0 : rows + width])
        chunk_grads[t >> 2] += dot_tn(first, picks[:, rows + width :])
        mat_acc[0] += dot_tn(flat(kept_act1, t), second_back[...])

    def backward(t, carry):
        third = third_tile[...]
        second = dot_nt(third, half4)
        held = accept(t + 1)
        settle(jnp.where(t == 0, tiles, t - 1), (t + 3) & 3)
        second = flat(kept_slope2, t).astype(f32) * second
        add_columns(1, second)
        second = second.astype(bf16)
        descend(t + 1, held)
        first = flat(kept_slope1, t).astype(f32) * dot_nt(second, half3)
        mat_acc[1] += dot_tn(flat(kept_act2, t), third)
        first_back[...] = first.astype(bf16)
        second_back[...] = second
        return carry

    first_back[...] = jnp.zeros(first_back.shape, bf16)
    second_back[...] = jnp.zeros(second_back.shape, bf16)
    passed_tile[3] = jnp.zeros((TILE, width), f32)
    descend(0, accept(0))
    def send_piece(p):
        pltpu.make_async_copy(
            cotangent_buf.at[pl.ds(p * piece, piece)],
            edges_grad_hbm.at[pl.ds(p * piece, piece)],
            out_sems.at[PIECES + p],
        ).start()

    def last_tile(p):
        return (listed[4, (p + 1) * (piece // per) - 1] + (GROUP - 1)) >> 5

    def backward_piece(p, t):
        upto = last_tile(p) + 1
        stop = jnp.minimum(upto, tiles)
        lax.fori_loop(t, stop, backward, 0)

        @pl.when(upto <= tiles)
        def _():
            send_piece(p)

        return jnp.maximum(t, stop)

    lax.fori_loop(0, PIECES, backward_piece, jnp.int32(0))
    settle(jnp.where(tiles == 0, tiles, tiles - 1), (tiles + 3) & 3)

    @pl.loop(0, PIECES)
    def _(p):
        @pl.when(last_tile(p) + 1 > tiles)
        def _():
            send_piece(p)

    stacked = split_pair(
        jnp.concatenate([chunk_grads[g] for g in range(chunks // LANES)], axis=1), axis=0
    )
    receiver_grad = halves(dot_nt(segment_ref[...], stacked)).astype(bf16)
    grads[tail : tail + 1, :] = halves(dot_nt(jnp.ones((8, chunks), bf16), stacked))[0:1, :]
    for row in range(1, 5):
        values = column_total(vec_acc[8 * row : 8 * row + 8, :])
        grads[tail + row : tail + row + 1, :] = values * root if row == 3 else values
    sent = index_acc[:, 0:rows].astype(bf16)
    put_block(0, index_acc[:, rows:].T)
    put_block(1, dot_tn(latents, receiver_grad))
    put_block(2, dot(sent, table_ref[...]).T)
    put_block(3, mat_acc[0])
    put_block(4, mat_acc[1])
    table_grad = lax.dot_general(
        sent, low_ref[2], (((0,), (1,)), ((), ())), preferred_element_type=f32
    )
    node_part_ref[...] += dot_nt(receiver_grad, low_ref[1]) + table_grad[0:particles, :]
    halo_grad[...] = table_grad[particles:, :].astype(bf16)
    low_x = halo_grad[0 : 3 * halo, :]
    high_x = halo_grad[5 * halo : 8 * halo, :]
    halo_own_ref[0:halo, :] = halo_grad[3 * halo : 4 * halo, :]
    halo_own_ref[halo : 2 * halo, :] = jnp.zeros((halo, width), bf16)
    halo_own_ref[2 * halo :, :] = halo_grad[4 * halo : 5 * halo, :]
    quarter = grads.shape[0] // 8
    relay = 2 * quarter
    send_ref[relay : relay + 3 * halo, :] = jnp.where(odd_x == 0, low_x, high_x)
    send_ref[4 * quarter + 3 * halo :, :] = jnp.where(odd_x == 0, high_x, low_x)
    keep_ref[relay : relay + 3 * halo, :] = jnp.zeros((3 * halo, width), f32)
    for slot, spot in enumerate(slot_rows(quarter, halo)):
        kept_rows = part_rows(relayed, odd_x, slot, quarter)
        sent_rows = part_rows(relayed, 1 - odd_x, slot, quarter)
        keep_ref[spot : spot + quarter, :] = grads[kept_rows, :]
        send_ref[spot : spot + quarter, :] = grads[sent_rows, :].astype(bf16)

    for copy in stores:
        copy.wait()
    for p in range(PIECES):
        pltpu.make_async_copy(
            cotangent_buf.at[pl.ds(p * piece, piece)],
            edges_grad_hbm.at[pl.ds(p * piece, piece)],
            out_sems.at[PIECES + p],
        ).wait()


def pinned(values):
    return pltpu.with_memory_space_constraint(values, pltpu.VMEM)


def outer(values):
    return pltpu.with_memory_space_constraint(values, pltpu.HBM)


def plan_call(halo, neighbours, edge_mask, latents, vectors, weights, edges):
    f32, bf16, i32 = jnp.float32, jnp.bfloat16, jnp.int32
    particles, slots = neighbours.shape
    width = latents.shape[1]
    chunks = particles * slots // CHUNK
    whole = pl.BlockSpec(memory_space=pltpu.VMEM)
    outside = pl.BlockSpec(memory_space=pl.ANY)
    buffer = pltpu.VMEM((chunks + 1, CHUNK, width), bf16)
    return pl.pallas_call(
        functools.partial(plan_kernel, halo),
        out_shape=(
            buffer,
            pltpu.VMEM((8, chunks + LANES), i32),
            pltpu.VMEM((particles, chunks), bf16),
            pltpu.VMEM((particles + 8, width), f32),
            pltpu.VMEM((particles + 8, width), f32),
            pltpu.VMEM((weights.shape[0] + 2, width, width), bf16),
            pltpu.VMEM((particles + 8 * halo + width + LANES, 2 * width), bf16),
            pltpu.VMEM((LANES // GROUP, TILE, LANES), bf16),
        ),
        in_specs=[whole] * 4 + [outside] * 2,
        out_specs=(whole,) * 8,
        scratch_shapes=[
            pltpu.VMEM(weights.shape, f32),
            pltpu.SemaphoreType.DMA((1 + PIECES,)),
        ],
        compiler_params=pltpu.CompilerParams(vmem_limit_bytes=16 * 1024 * 1024),
        cost_estimate=pl.CostEstimate(
            flops=10**9, bytes_accessed=12 * 10**6, transcendentals=0
        ),
        name="plan",
    )(
        outer(neighbours.T),
        outer(edge_mask.T),
        outer(latents),
        outer(vectors),
        outer(weights),
        outer(edges),
    )


def layer_call(halo, relayed, grad_rows, counts, latents, ring, ring_far, ring_near, upstream,
               vectors, cotangents, plan):
    f32, bf16, i32 = jnp.float32, jnp.bfloat16, jnp.int32
    edges, listing, segment, neighbour_rows, receiver, low, gather, blocks = plan
    particles, chunks = segment.shape
    width = latents.shape[1]
    rows = particles + 8 * halo
    whole = pl.BlockSpec(memory_space=pltpu.VMEM)
    outside = pl.BlockSpec(memory_space=pl.ANY)
    edge_shape = (chunks, CHUNK, width)
    kept_shape = (chunks + GROUP, CHUNK, width)
    kept = pltpu.VMEM(kept_shape, bf16)
    half = grad_rows // 2
    return pl.pallas_call(
        functools.partial(layer_kernel, halo, relayed),
        out_shape=(
            jax.ShapeDtypeStruct((particles, width), bf16),
            jax.ShapeDtypeStruct(edge_shape, bf16),
            jax.ShapeDtypeStruct(edge_shape, bf16),
            jax.ShapeDtypeStruct((particles, width), f32),
            jax.ShapeDtypeStruct((3 * halo, width), bf16),
            jax.ShapeDtypeStruct((half + 6 * halo, width), bf16),
            jax.ShapeDtypeStruct((half + 3 * halo, width), f32),
            pltpu.VMEM(edges.shape, bf16),
            pltpu.VMEM(gather.shape, bf16),
        ),
        in_specs=[pl.BlockSpec(memory_space=pltpu.SMEM)] + [whole] * 14 + [outside],
        out_specs=(whole, outside, outside) + (whole,) * 6,
        input_output_aliases={13: 7, 14: 8},
        scratch_shapes=[
            pltpu.VMEM(edges.shape, bf16),
            kept,
            pltpu.VMEM(kept_shape, jnp.int16),
            kept,
            kept,
            kept,
            kept,
            kept,
            pltpu.VMEM(kept_shape, f32),
            pltpu.VMEM((rows, width), bf16),
            pltpu.VMEM((particles + 8, width), f32),
            pltpu.VMEM((GROUP, width), f32),
            pltpu.VMEM((chunks + GROUP, width), f32),
            pltpu.VMEM((chunks // LANES + 1, width, LANES), f32),
            pltpu.VMEM((width, rows + width), f32),
            pltpu.VMEM((2, width, width), f32),
            pltpu.VMEM((40, width), f32),
            pltpu.VMEM((TILE, width), f32),
            pltpu.VMEM((TILE, width), f32),
            pltpu.VMEM((TILE, width), bf16),
            pltpu.VMEM((TILE, width), bf16),
            pltpu.VMEM((TILE, width), bf16),
            pltpu.VMEM((4, TILE, width), f32),
            pltpu.VMEM((8 * halo, width), bf16),
            pltpu.VMEM((grad_rows, width), f32),
            pltpu.SMEM((8, chunks + LANES), i32),
            pltpu.SemaphoreType.DMA((PIECES,)),
            pltpu.SemaphoreType.DMA((2 * PIECES,)),
            pltpu.SemaphoreType.DMA,
        ],
        compiler_params=pltpu.CompilerParams(vmem_limit_bytes=52 * 1024 * 1024),
        name="edge_layer",
    )(
        counts,
        outer(latents),
        pinned(ring),
        pinned(ring_far),
        pinned(ring_near),
        outer(upstream),
        outer(vectors),
        pinned(listing),
        pinned(segment),
        pinned(neighbour_rows),
        pinned(receiver),
        pinned(low),
        pinned(blocks),
        pinned(edges),
        pinned(gather),
        outer(cotangents),
    )[:7]


def update_kernel(
    relayed,
    mine_ref,
    other_ref,
    weights_ref,
    vectors_ref,
    weights_m_ref,
    vectors_m_ref,
    weights_v_ref,
    vectors_v_ref,
    weights_ema_ref,
    vectors_ema_ref,
    norm_ref,
    weights_m_out,
    vectors_m_out,
    weights_v_out,
    vectors_v_out,
    weights_out,
    vectors_out,
    weights_copy_out,
    vectors_copy_out,
    weights_ema_out,
    vectors_ema_out,
    grads,
):
    f32 = jnp.float32
    odd = lax.axis_index("gx") & 1
    half_rows, width = mine_ref.shape
    quarter = half_rows // 4
    squares = jnp.zeros((8, width), f32)
    for side, part_ref in ((odd, mine_ref), (1 - odd, other_ref)):
        for slot in range(4):
            values = part_ref[slot * quarter : (slot + 1) * quarter, :].astype(f32)
            grads[part_rows(relayed, side, slot, quarter), :] = values
            squares = squares + jnp.sum((values * values).reshape(quarter // 8, 8, width), axis=0)
    norm = jnp.sqrt(jnp.sum(jnp.sum(squares, axis=1, keepdims=True), axis=0, keepdims=True))
    norm_ref[...] = norm
    scale = clip_norm / jnp.maximum(norm, clip_norm)
    for block in range(weights_ref.shape[0]):
        moment, second, param, average = adamw(
            weights_ref[block],
            grads[block * width : (block + 1) * width, :],
            weights_m_ref[block],
            weights_v_ref[block],
            weights_ema_ref[block],
            scale,
            matrix_rate,
        )
        weights_m_out[block] = moment
        weights_v_out[block] = second
        weights_out[block] = param
        weights_copy_out[block] = param.astype(jnp.bfloat16)
        weights_ema_out[block] = average
    tail = weights_ref.shape[0] * width
    moment, second, param, average = adamw(
        vectors_ref[...],
        grads[tail : tail + vectors_ref.shape[0], :],
        vectors_m_ref[...],
        vectors_v_ref[...],
        vectors_ema_ref[...],
        scale,
        vector_rate,
    )
    vectors_m_out[...] = moment
    vectors_v_out[...] = second
    vectors_out[...] = param
    vectors_copy_out[...] = param.astype(jnp.bfloat16)
    vectors_ema_out[...] = average


def update_call(relayed, mine, other, weights, vectors, weights_m, vectors_m, weights_v, vectors_v,
                weights_ema, vectors_ema):
    f32, bf16 = jnp.float32, jnp.bfloat16
    mat, vec = weights.shape, vectors.shape
    kinds = (
        ((1, 1), f32), (mat, f32), (vec, f32), (mat, f32), (vec, f32), (mat, f32), (vec, f32),
        (mat, bf16), (vec, bf16), (mat, f32), (vec, f32),
    )
    whole = pl.BlockSpec(memory_space=pltpu.VMEM)
    return pl.pallas_call(
        functools.partial(update_kernel, relayed),
        out_shape=tuple(jax.ShapeDtypeStruct(*kind) for kind in kinds),
        in_specs=[whole] * 10,
        out_specs=(whole,) * 11,
        scratch_shapes=[pltpu.VMEM((2 * mine.shape[0], mine.shape[1]), f32)],
        compiler_params=pltpu.CompilerParams(vmem_limit_bytes=24 * 1024 * 1024),
        name="update",
    )(mine, other, weights, vectors, weights_m, vectors_m, weights_v, vectors_v, weights_ema,
      vectors_ema)


def pair_exchange(to_far, to_near, axis):
    near, far = neighbour_pairs(lax.axis_size(axis))
    return lax.ppermute(to_far, axis, far), lax.ppermute(to_near, axis, near)


def partners(axis, stride, mask):
    return [(i, i ^ (mask * stride)) for i in range(lax.axis_size(axis))]


def even_pick(axis, even, odd):
    return jnp.where(lax.axis_index(axis) % 2 == 0, even, odd)


def swap(values, axis, stride, mask):
    return lax.ppermute(values, axis, partners(axis, stride, mask))


def tree_sum(terms):
    while len(terms) > 1:
        terms = [terms[i] + terms[i + 1] for i in range(0, len(terms), 2)]
    return terms[0]


def sum_relayed(send, keep, halo_own, halo):
    f32, bf16 = jnp.float32, jnp.bfloat16
    quarter = (send.shape[0] - 6 * halo) // 4
    slots = slot_rows(quarter, halo)
    index, row = lax.axis_index("gx"), lax.axis_index("gy")
    got = swap(send, "gx", 1, 1)
    near = got[4 * quarter + 3 * halo :].astype(f32)
    total = (keep + got[: 4 * quarter + 3 * halo].astype(f32)).astype(bf16)
    def turned(values, step):
        pairs = [(i, ((i >> 1) + step * (1 - 2 * (i & 1))) % 4 * 2 + (i & 1)) for i in range(8)]
        return lax.ppermute(values, "gx", pairs)

    at1 = turned(total[quarter : 2 * quarter + 3 * halo], 1)
    at3 = turned(total[slots[3] : slots[3] + quarter], 3)
    at2 = turned(total[slots[2] : slots[2] + quarter], 2)
    mine = tree_sum(
        [total[:quarter].astype(f32), at1[:quarter].astype(f32), at2.astype(f32), at3.astype(f32)]
    ).astype(bf16)
    far = jnp.where((index == 0) | (index == 7), 0.0, at1[quarter:].astype(f32))
    strips = halo_own + near + far
    low, high = strips[:halo].astype(bf16), strips[2 * halo :].astype(bf16)
    along3 = swap(jnp.concatenate([even_pick("gy", low, high), mine]), "gy", 1, 3)
    along2 = swap(mine, "gy", 1, 2)
    along1 = swap(jnp.concatenate([even_pick("gy", high, low), mine]), "gy", 1, 1)
    mine = tree_sum(
        [
            mine.astype(f32),
            along1[halo:].astype(f32),
            along2.astype(f32),
            along3[halo:].astype(f32),
        ]
    ).astype(bf16)
    last_far = jnp.where((row == 0) | (row == 3), bf16(0), along3[:halo])
    mine = jnp.concatenate([mine, turned(mine, 3), turned(mine, 2), turned(mine, 1)])
    return mine, swap(mine, "gx", 1, 1), strips, last_far, along1[:halo]


def sum_staged(send, keep, halo_own, halo):
    f32, bf16 = jnp.float32, jnp.bfloat16
    width = send.shape[1]
    quarter = (send.shape[0] - 6 * halo) // 4
    slots = slot_rows(quarter, halo)

    def joined_slots(values):
        return jnp.concatenate([values[spot : spot + quarter] for spot in slots])

    far = send[2 * quarter : 2 * quarter + 3 * halo]
    near = send[4 * quarter + 3 * halo :]
    back_far, back_near = pair_exchange(far, near, "gx")
    strips = halo_own + back_far.astype(f32) + back_near.astype(f32)
    low, high = strips[:halo].astype(bf16), strips[2 * halo :].astype(bf16)
    last_far, last_near = pair_exchange(
        even_pick("gy", low, high), even_pick("gy", high, low), "gy"
    )
    index = lax.axis_index("gx")
    got = swap(joined_slots(send), "gx", 1, 1)
    total = (joined_slots(keep) + got.astype(f32)).astype(bf16)
    split = stages(lax.axis_size("gx"))[1:]
    for stride, factor in split:
        part = (index // stride) % factor
        height = total.shape[0] // factor
        mine = lax.dynamic_slice_in_dim(total, part * height, height, 0).astype(f32)
        for mask in range(factor - 1, 0, -1):
            piece = lax.dynamic_slice_in_dim(total, (part ^ mask) * height, height, 0)
            mine = mine + swap(piece, "gx", stride, mask).astype(f32)
        total = mine.astype(bf16)
    total = tree_sum(
        [total.astype(f32)]
        + [swap(total, "gy", 1, mask).astype(f32) for mask in range(1, lax.axis_size("gy"))]
    ).astype(bf16)
    for stride, factor in reversed(split):
        part = (index // stride) % factor
        height = total.shape[0]
        joined = jnp.zeros((factor * height, width), bf16)
        joined = lax.dynamic_update_slice_in_dim(joined, total, part * height, 0)
        for mask in range(factor - 1, 0, -1):
            piece = swap(total, "gx", stride, mask)
            joined = lax.dynamic_update_slice_in_dim(joined, piece, (part ^ mask) * height, 0)
        total = joined
    return total, swap(total, "gx", 1, 1), strips, last_far, last_near


def per_device(
    node_latents,
    edge_latents,
    node_cotangent,
    edge_cotangent,
    neighbours,
    edge_mask,
    send_table,
    counts,
    weights,
    vectors,
    weights_m,
    vectors_m,
    weights_v,
    vectors_v,
    weights_ema,
    vectors_ema,
):
    f32, bf16 = jnp.float32, jnp.bfloat16
    tok_rows, width = node_latents.shape
    halo = send_table.shape[1]
    boundary_pick = selector(send_table[0], tok_rows, bf16)
    boundary = jnp.dot(boundary_pick, node_latents, preferred_element_type=f32).astype(bf16)
    from_far, from_near = pair_exchange(boundary, boundary, "gx")
    ring = jnp.concatenate([from_far, from_near, boundary], axis=0)
    ring_far, ring_near = pair_exchange(ring, ring, "gy")
    unit = 16 * lax.axis_size("gx")
    grad_rows = -(-(weights.shape[0] * width + vectors.shape[0]) // unit) * unit
    relayed = lax.axis_size("gx") == 8 and lax.axis_size("gy") == 4
    edge_shape = (tok_rows * neighbours.shape[1] // CHUNK, CHUNK, width)
    plan = plan_call(
        halo, neighbours, edge_mask, node_latents, vectors, weights,
        edge_latents.reshape(edge_shape),
    )
    nodes_out, edges_out, edges_in_grad, node_part, halo_own, send, keep = layer_call(
        halo, relayed, grad_rows, counts, node_latents, ring, ring_far, ring_near,
        node_cotangent, vectors, edge_cotangent.reshape(edge_shape), plan,
    )
    sums = sum_relayed if relayed else sum_staged
    mine, other, strips, last_far, last_near = sums(send, keep, halo_own.astype(f32), halo)
    boundary_grad = strips[halo : 2 * halo] + last_far.astype(f32) + last_near.astype(f32)
    returned = lax.dot_general(
        boundary_pick.astype(f32),
        boundary_grad,
        (((0,), (0,)), ((), ())),
        precision=lax.Precision.HIGHEST,
        preferred_element_type=f32,
    )
    nodes_in_grad = (node_part + returned).astype(bf16)
    updated = update_call(
        relayed, mine, other, weights, vectors, weights_m, vectors_m, weights_v, vectors_v, weights_ema,
        vectors_ema,
    )
    return (
        nodes_out,
        edges_out.reshape(edge_latents.shape),
        nodes_in_grad,
        edges_in_grad.reshape(edge_latents.shape),
        updated[0].reshape(()),
    ) + tuple(updated[1:])


def solution(mesh):
    in_specs = (
        P(("gx", "gy"), None),
        P(("gx", "gy"), None, None),
        P(("gx", "gy"), None),
        P(("gx", "gy"), None, None),
        P(("gx", "gy"), None),
        P(("gx", "gy"), None),
        P(("gx", "gy"), None),
        P(("gx", "gy")),
        P(),
        P(),
        P(),
        P(),
        P(),
        P(),
        P(),
        P(),
    )
    out_specs = (
        P(("gx", "gy"), None),
        P(("gx", "gy"), None, None),
        P(("gx", "gy"), None),
        P(("gx", "gy"), None, None),
        P(),
        P(),
        P(),
        P(),
        P(),
        P(),
        P(),
        P(),
        P(),
        P(),
        P(),
    )
    return jax.shard_map(
        per_device, mesh=mesh, in_specs=in_specs, out_specs=out_specs, check_vma=False
    )
```

```python
import functools

import jax
import jax.numpy as jnp
from jax import lax
from jax.experimental import pallas as pl
from jax.experimental.pallas import tpu as pltpu
from jax.sharding import PartitionSpec as P

STEP = 10


first_decay = 0.5
second_decay = 0.5
adam_epsilon = 1e-08
weight_decay = 0.01
matrix_rate = 0.05
vector_rate = 0.2
average_decay = 0.9
clip_norm = 1.0
norm_epsilon = 1e-05


def neighbour_pairs(count):
    near = [(i, i ^ 1) for i in range(count) if (i ^ 1) < count]
    far = [(i, i + 1) for i in range(1, count - 1, 2)]
    return near, far + [(target, source) for source, target in far]


def stages(count):
    result, stride = [], 1
    while stride < count:
        factor = 2 if stride == 1 else min(4, count // stride)
        result.append((stride, factor))
        stride *= factor
    return result


def selector(indices, width, dtype):
    columns = lax.broadcasted_iota(jnp.int32, (indices.shape[0], width), 1)
    return (indices[:, None] == columns).astype(dtype)


def adamw(param, grad, moment, second, average, scale, rate):
    clipped = grad * scale
    moment_new = first_decay * moment + (1.0 - first_decay) * clipped
    second_new = second_decay * second + (1.0 - second_decay) * clipped * clipped
    corrected = moment_new / (1.0 - first_decay**STEP)
    denom = jnp.sqrt(second_new / (1.0 - second_decay**STEP)) + adam_epsilon
    param_new = param - rate * (corrected / denom + weight_decay * param)
    average_new = average_decay * average + (1.0 - average_decay) * param_new
    return (moment_new, second_new, param_new, average_new)


CHUNK = 16
GROUP = 32
TILE = CHUNK * GROUP
LANES = 128
PIECES = 8


def dot(left, right):
    return jnp.dot(left, right, preferred_element_type=jnp.float32)


def dot_nt(left, right):
    return lax.dot_general(
        left, right, (((1,), (1,)), ((), ())), preferred_element_type=jnp.float32
    )


def dot_tn(left, right):
    return lax.dot_general(
        left, right, (((0,), (0,)), ((), ())), preferred_element_type=jnp.float32
    )


def split_pair(values, axis=1):
    high = values.astype(jnp.bfloat16)
    low = (values - high.astype(jnp.float32)).astype(jnp.bfloat16)
    return jnp.concatenate([high, low], axis=axis)


def halves(pair):
    width = pair.shape[1] // 2
    return pair[:, :width] + pair[:, width:]


def silu_of_half(half):
    turn = jnp.tanh(half)
    lift = 1.0 + turn
    act = half * lift
    return act, lift + act * (1.0 - turn)


def row_sum(values):
    return jnp.sum(values, axis=-1, keepdims=True)


def scaled_unit(values, width):
    center = values - row_sum(values) * (1.0 / width)
    inverse = lax.rsqrt(row_sum(center * center) + width * norm_epsilon)
    return center * inverse, inverse


def scaled_unit_back(scaled, unit, inverse, width):
    shift = row_sum(scaled) * (1.0 / width)
    return inverse * (scaled - shift - unit * row_sum(scaled * unit))


def column_total(values):
    return jnp.sum(values, axis=0, keepdims=True)


def iota(shape, dim):
    return lax.broadcasted_iota(jnp.int32, shape, dim)


def slot_rows(quarter, halo):
    return (0, quarter, 2 * quarter + 3 * halo, 3 * quarter + 3 * halo)


def part_rows(relayed, side, slot, quarter):
    chip = lax.axis_index("gx") >> 1
    part = (chip + slot * (1 - 2 * side)) & 3 if relayed else slot
    return pl.ds(pl.multiple_of((side * 4 + part) * quarter, 16), quarter)


def plan_kernel(
    halo,
    neighbour_ref,
    mask_ref,
    latents_ref,
    vectors_ref,
    weights_hbm,
    edges_hbm,
    edges_buf,
    list_rows,
    segment_ref,
    neighbour_rows,
    receiver_ref,
    low_ref,
    gather_ref,
    blocks_ref,
    weights_ref,
    sems,
):
    f32, bf16, i32 = jnp.float32, jnp.bfloat16, jnp.int32
    slots, particles = neighbour_ref.shape
    per = slots // CHUNK
    chunks = particles * per
    width = latents_ref.shape[1]
    rows = particles + 8 * halo
    fetch_weights = pltpu.make_async_copy(weights_hbm, weights_ref, sems.at[0])
    fetch_weights.start()
    piece = chunks // PIECES
    loads = [
        pltpu.make_async_copy(
            edges_hbm.at[pl.ds(p * piece, piece)],
            edges_buf.at[pl.ds(p * piece, piece)],
            sems.at[1 + p],
        )
        for p in range(PIECES)
    ]
    for copy in loads:
        copy.start()
    edges_buf[chunks] = jnp.zeros((CHUNK, width), bf16)

    mask = mask_ref[...].astype(f32)
    degree = jnp.sum(mask, axis=0, keepdims=True)
    taken = ((degree.astype(i32) + (CHUNK - 1)) >> 4).astype(f32)
    earlier = iota((particles, particles), 0) < iota((particles, particles), 1)
    begin = dot(jnp.broadcast_to(taken, (16, particles)).astype(bf16), earlier.astype(bf16))
    degree_col = dot_tn(mask.astype(bf16), jnp.ones((slots, width), bf16))
    taken_col = ((degree_col.astype(i32) + (CHUNK - 1)) >> 4).astype(f32)
    later = iota((particles, particles), 1) < iota((particles, particles), 0)
    begin_col = dot(later.astype(bf16), taken_col.astype(bf16))
    end_col = begin_col + taken_col
    for block in range(chunks // width):
        lane = iota((particles, width), 1).astype(f32) + block * width
        segment_ref[:, block * width : (block + 1) * width] = (
            (lane >= begin_col) & (lane < end_col)
        ).astype(bf16)
    total = row_sum(taken)
    who = iota((16, particles), 1).astype(f32)
    offset = per * who - begin
    coarse = jnp.floor(offset * 0.125) * 8.0
    line = iota((16, particles), 0)
    facts = jnp.where(
        line == 0,
        who,
        jnp.where(line == 1, coarse, jnp.where(line == 2, offset - coarse, degree)),
    )
    listing = dot(facts.astype(bf16), segment_ref[...])
    place = iota((1, chunks), 1).astype(f32)
    particle = listing[0:1, :]
    chunk = listing[1:2, :] + listing[2:3, :] + place
    rest = listing[3:4, :] - CHUNK * (chunk - per * particle)
    used = place < total
    list_rows[...] = jnp.zeros(list_rows.shape, i32)
    list_rows[0:1, 0:chunks] = jnp.where(used, chunk, float(chunks)).astype(i32)
    list_rows[0:1, chunks:] = jnp.full((1, list_rows.shape[1] - chunks), chunks, i32)
    list_rows[1:2, 0:chunks] = jnp.where(used, particle, float(particles)).astype(i32)
    list_rows[1:2, chunks:] = jnp.full((1, list_rows.shape[1] - chunks), particles, i32)
    list_rows[2:3, 0:chunks] = jnp.where(used, rest, 0.0).astype(i32)
    list_rows[3:4, 0:particles] = jnp.broadcast_to(total, (1, particles)).astype(i32)
    list_rows[4:5, 0:particles] = (begin[0:1, :] + taken).astype(i32)

    neighbour = neighbour_ref[...]
    neighbour = jnp.where(neighbour >= particles + 5 * halo, neighbour - halo, neighbour)
    neighbour_rows[...] = jnp.zeros(neighbour_rows.shape, f32)
    neighbour_rows[0:particles, 0:slots] = neighbour.astype(f32).T

    block_of = iota((TILE, LANES), 0) >> 4
    for quarter in range(LANES // GROUP):
        blocks_ref[quarter] = (iota((TILE, LANES), 1) == block_of + quarter * GROUP).astype(bf16)

    fetch_weights.wait()
    for block in range(weights_ref.shape[0]):
        low_ref[block] = weights_ref[block].astype(bf16)
    for extra, block in ((9, 3), (10, 4)):
        low_ref[extra] = (0.5 * low_ref[block].astype(f32)).astype(bf16)
    latents = latents_ref[...]
    gather_ref[0:particles, :] = split_pair(0.5 * dot(latents, low_ref[2]))
    gather_ref[particles:rows, :] = jnp.zeros((rows - particles, 2 * width), bf16)
    gather_ref[rows : rows + width, :] = jnp.concatenate(
        [(0.5 * low_ref[0].astype(f32)).astype(bf16), jnp.zeros((width, width), bf16)], axis=1
    )
    gather_ref[rows + width :, :] = jnp.zeros((LANES, 2 * width), bf16)
    receiver_ref[0:particles, :] = 0.5 * (dot(latents, low_ref[1]) + vectors_ref[0:1, :])
    receiver_ref[particles:, :] = jnp.zeros((receiver_ref.shape[0] - particles, width), f32)
    for copy in loads:
        copy.wait()


def layer_kernel(
    halo,
    relayed,
    count_ref,
    latents_ref,
    ring_ref,
    ring_far_ref,
    ring_near_ref,
    upstream_ref,
    vectors_ref,
    list_rows,
    segment_ref,
    neighbour_rows,
    receiver_ref,
    low_ref,
    blocks_ref,
    edges_in,
    gather_in,
    cotangent_hbm,
    nodes_out_ref,
    edges_out_hbm,
    edges_grad_hbm,
    node_part_ref,
    halo_own_ref,
    send_ref,
    keep_ref,
    edges_buf,
    gather_ref,
    cotangent_buf,
    kept_edges,
    kept_index,
    kept_act1,
    kept_act2,
    kept_slope1,
    kept_slope2,
    kept_unit,
    kept_inverse,
    table_ref,
    descent_ref,
    receiver_tile,
    chunk_sums,
    chunk_grads,
    index_acc,
    mat_acc,
    vec_acc,
    first_tile,
    last_tile,
    third_tile,
    first_back,
    second_back,
    passed_tile,
    halo_grad,
    grads,
    listed,
    in_sems,
    out_sems,
    list_sem,
):
    f32, bf16, i32 = jnp.float32, jnp.bfloat16, jnp.int32
    fetch_list = pltpu.make_async_copy(list_rows, listed, list_sem)
    fetch_list.start()
    particles, chunks = segment_ref.shape
    per = chunks // particles
    width = latents_ref.shape[1]
    rows = table_ref.shape[0]
    piece = chunks // PIECES
    root = float(width) ** 0.5
    odd_x = lax.axis_index("gx") & 1
    odd_y = lax.axis_index("gy") & 1
    loads = [
        pltpu.make_async_copy(
            cotangent_hbm.at[pl.ds(p * piece, piece)],
            cotangent_buf.at[pl.ds(p * piece, piece)],
            in_sems.at[p],
        )
        for p in range(PIECES)
    ]
    for copy in loads:
        copy.start()
    cotangent_buf[chunks] = jnp.zeros((CHUNK, width), bf16)

    table_ref[0:particles, :] = latents_ref[...]
    far, near, own = ring_far_ref[...], ring_near_ref[...], ring_ref[...]
    low_y = jnp.where(odd_y == 0, far, near)
    high_y = jnp.where(odd_y == 0, near, far)
    spot = particles
    for a in range(3):
        for b, strip in enumerate((low_y, own, high_y)):
            if a == 1 and b == 1:
                continue
            if a == 1:
                part = strip[2 * halo :]
            elif a == 0:
                part = jnp.where(odd_x == 0, strip[0:halo], strip[halo : 2 * halo])
            else:
                part = jnp.where(odd_x == 0, strip[halo : 2 * halo], strip[0:halo])
            table_ref[spot : spot + halo, :] = part
            spot += halo

    vectors = vectors_ref[...]

    def vector(row):
        return vectors[row : row + 1, :]

    latents = latents_ref[...]
    half3, half4 = low_ref[9], low_ref[10]
    gather_ref[particles:rows, :] = split_pair(0.5 * dot(table_ref[particles:, :], low_ref[2]))
    chunk_sums[...] = jnp.zeros(chunk_sums.shape, f32)
    chunk_grads[...] = jnp.zeros(chunk_grads.shape, f32)
    index_acc[...] = jnp.zeros(index_acc.shape, f32)
    mat_acc[...] = jnp.zeros(mat_acc.shape, f32)
    vec_acc[...] = jnp.zeros(vec_acc.shape, f32)
    tail = 9 * width
    grads[tail:, :] = jnp.zeros((grads.shape[0] - tail, width), f32)
    descent_ref[particles:, :] = jnp.zeros((descent_ref.shape[0] - particles, width), f32)

    fetch_list.wait()
    tiles = (listed[3, 0] + (GROUP - 1)) >> 5

    sublane = iota((CHUNK, width), 0)
    diagonal = iota((CHUNK, width), 1) - sublane
    lane16 = iota((TILE, width), 1).astype(jnp.int16)

    def flat(ref, t):
        return ref[pl.ds(t * GROUP, GROUP)].reshape(TILE, width)

    def keep(ref, t, values):
        ref[pl.ds(t * GROUP, GROUP)] = values.astype(ref.dtype).reshape(GROUP, CHUNK, width)

    def span(j):
        return slice(j * CHUNK, (j + 1) * CHUNK)

    def one_hot(t):
        index = flat(kept_index, t)
        return [
            jnp.where(index == lane16 + jnp.int16(b * width), bf16(1), bf16(0))
            for b in range(rows // width)
        ]

    def gather(t):
        base = t * GROUP
        for j in range(GROUP):
            chunk, particle = listed[0, base + j], listed[1, base + j]
            kept_edges[base + j] = edges_buf[chunk]
            row = jnp.broadcast_to(neighbour_rows[pl.ds(particle, 1), :], (CHUNK, width))
            start = (chunk & (per - 1)) * CHUNK
            index = row_sum(jnp.where(diagonal == start, row, 0.0))
            kept_index[base + j] = (
                jnp.broadcast_to(index, (CHUNK, width)).astype(i32).astype(jnp.int16)
            )
            receiver_tile[j : j + 1, :] = receiver_ref[pl.ds(particle, 1), :]
        gather_ref[rows + width : rows + width + GROUP, :] = split_pair(receiver_tile[...])

    def project(t):
        picks = jnp.concatenate(one_hot(t) + [flat(kept_edges, t), blocks_ref[0]], axis=1)
        first_tile[...] = halves(dot(picks, gather_ref[...]))

    gain_root = vector(3) * root

    def finish(t):
        base = t * GROUP
        unit, inverse = scaled_unit(last_tile[...], width)
        keep(kept_unit, t, unit)
        keep(kept_inverse, t, jnp.broadcast_to(inverse, (TILE, width)))
        change = unit * gain_root + vector(4)
        for j in range(GROUP):
            chunk = listed[0, base + j]
            alive = sublane < listed[2, base + j]
            fresh = kept_edges[base + j].astype(f32) + jnp.where(alive, change[span(j)], 0.0)
            edges_buf[chunk] = fresh.astype(bf16)
            chunk_sums[pl.ds(base + j, 1), :] = column_total(jnp.where(alive, fresh, 0.0))

    def forward(t, carry):
        gather(t + 1)
        act, slope = silu_of_half(first_tile[...])
        act = act.astype(bf16)
        keep(kept_act1, t, act)
        keep(kept_slope1, t, slope)
        finish(jnp.where(t == 0, tiles, t - 1))
        act, slope = silu_of_half(dot(act, half3) + 0.5 * vector(1))
        act = act.astype(bf16)
        keep(kept_act2, t, act)
        keep(kept_slope2, t, slope)
        project(t + 1)
        last_tile[...] = dot(act, low_ref[4]) + vector(2)
        return carry

    for ref in (kept_act1, kept_edges):
        keep(ref, tiles, jnp.zeros((TILE, width), f32))
    last_tile[...] = jnp.zeros(last_tile.shape, f32)
    gather(0)
    project(0)
    lax.fori_loop(0, tiles, forward, 0)
    finish(jnp.where(tiles == 0, tiles, tiles - 1))

    stores = [
        pltpu.make_async_copy(
            edges_buf.at[pl.ds(p * piece, piece)],
            edges_out_hbm.at[pl.ds(p * piece, piece)],
            out_sems.at[p],
        )
        for p in range(PIECES)
    ]
    for copy in stores:
        copy.start()

    aggregate = halves(dot(segment_ref[...], split_pair(chunk_sums[0:chunks, :]))).astype(bf16)
    half1 = 0.5 * (dot(latents, low_ref[5]) + dot(aggregate, low_ref[6]) + vector(5))
    act1, slope1 = silu_of_half(half1)
    act1 = act1.astype(bf16)
    act2, slope2 = silu_of_half(0.5 * (dot(act1, low_ref[7]) + vector(6)))
    act2 = act2.astype(bf16)
    unit, inverse = scaled_unit(dot(act2, low_ref[8]) + vector(7), width)
    alive = (iota((particles, width), 0) < count_ref[0]).astype(f32)
    upstream = upstream_ref[...].astype(f32)
    nodes_out_ref[...] = (
        latents.astype(f32) + alive * (unit * (vector(8) * root) + vector(9))
    ).astype(bf16)
    held = alive * upstream
    third = scaled_unit_back(held * (vector(8) * root), unit, inverse, width).astype(bf16)
    second = (0.5 * slope2 * dot_nt(third, low_ref[8])).astype(bf16)
    first = (0.5 * slope1 * dot_nt(second, low_ref[7])).astype(bf16)
    descent_ref[0:particles, :] = dot_nt(first, low_ref[6])
    node_part_ref[...] = upstream + dot_nt(first, low_ref[5])

    def put_block(block, values):
        grads[block * width : (block + 1) * width, :] = values

    put_block(5, dot_tn(latents, first))
    put_block(6, dot_tn(aggregate, first))
    put_block(7, dot_tn(act1, second))
    put_block(8, dot_tn(act2, third))
    for row, values in enumerate(
        (first.astype(f32), second.astype(f32), third.astype(f32), held * unit * root, held)
    ):
        grads[tail + 5 + row : tail + 6 + row, :] = column_total(values)

    for copy in loads:
        copy.wait()

    def add_columns(row, values):
        vec_acc[8 * row : 8 * row + 8, :] += jnp.sum(values.reshape(TILE // 8, 8, width), axis=0)

    def accept(t):
        base = t * GROUP
        parts = []
        for j in range(GROUP):
            chunk, particle = listed[0, base + j], listed[1, base + j]
            alive = sublane < listed[2, base + j]
            passed = cotangent_buf[chunk].astype(f32) + jnp.where(
                alive, descent_ref[pl.ds(particle, 1), :], 0.0
            )
            passed_tile[t & 3, span(j), :] = passed
            parts.append(jnp.where(alive, passed, 0.0))
        return jnp.concatenate(parts, axis=0)

    def descend(t, held):
        unit = flat(kept_unit, t).astype(f32)
        third = scaled_unit_back(held * gain_root, unit, flat(kept_inverse, t), width)
        third_tile[...] = third.astype(bf16)
        add_columns(2, third)
        add_columns(3, held * unit)
        add_columns(4, held)

    def settle(t, slot):
        base = t * GROUP
        first = first_back[...]
        result = passed_tile[slot] + dot_nt(first, low_ref[0])
        for j in range(GROUP):
            cotangent_buf[listed[0, base + j]] = result[span(j)].astype(bf16)
        picks = jnp.concatenate(one_hot(t) + [flat(kept_edges, t), blocks_ref[t & 3]], axis=1)
        index_acc[...] += dot_tn(first, picks[:, 0 : rows + width])
        chunk_grads[t >> 2] += dot_tn(first, picks[:, rows + width :])
        mat_acc[0] += dot_tn(flat(kept_act1, t), second_back[...])

    def backward(t, carry):
        third = third_tile[...]
        second = dot_nt(third, half4)
        held = accept(t + 1)
        settle(jnp.where(t == 0, tiles, t - 1), (t + 3) & 3)
        second = flat(kept_slope2, t).astype(f32) * second
        add_columns(1, second)
        second = second.astype(bf16)
        descend(t + 1, held)
        first = flat(kept_slope1, t).astype(f32) * dot_nt(second, half3)
        mat_acc[1] += dot_tn(flat(kept_act2, t), third)
        first_back[...] = first.astype(bf16)
        second_back[...] = second
        return carry

    first_back[...] = jnp.zeros(first_back.shape, bf16)
    second_back[...] = jnp.zeros(second_back.shape, bf16)
    passed_tile[3] = jnp.zeros((TILE, width), f32)
    descend(0, accept(0))
    def send_piece(p):
        pltpu.make_async_copy(
            cotangent_buf.at[pl.ds(p * piece, piece)],
            edges_grad_hbm.at[pl.ds(p * piece, piece)],
            out_sems.at[PIECES + p],
        ).start()

    def last_tile(p):
        return (listed[4, (p + 1) * (piece // per) - 1] + (GROUP - 1)) >> 5

    def backward_piece(p, t):
        upto = last_tile(p) + 1
        stop = jnp.minimum(upto, tiles)
        lax.fori_loop(t, stop, backward, 0)

        @pl.when(upto <= tiles)
        def _():
            send_piece(p)

        return jnp.maximum(t, stop)

    lax.fori_loop(0, PIECES, backward_piece, jnp.int32(0))
    settle(jnp.where(tiles == 0, tiles, tiles - 1), (tiles + 3) & 3)

    @pl.loop(0, PIECES)
    def _(p):
        @pl.when(last_tile(p) + 1 > tiles)
        def _():
            send_piece(p)

    stacked = split_pair(
        jnp.concatenate([chunk_grads[g] for g in range(chunks // LANES)], axis=1), axis=0
    )
    receiver_grad = halves(dot_nt(segment_ref[...], stacked)).astype(bf16)
    grads[tail : tail + 1, :] = halves(dot_nt(jnp.ones((8, chunks), bf16), stacked))[0:1, :]
    for row in range(1, 5):
        values = column_total(vec_acc[8 * row : 8 * row + 8, :])
        grads[tail + row : tail + row + 1, :] = values * root if row == 3 else values
    sent = index_acc[:, 0:rows].astype(bf16)
    put_block(0, index_acc[:, rows:].T)
    put_block(1, dot_tn(latents, receiver_grad))
    put_block(2, dot(sent, table_ref[...]).T)
    put_block(3, mat_acc[0])
    put_block(4, mat_acc[1])
    table_grad = lax.dot_general(
        sent, low_ref[2], (((0,), (1,)), ((), ())), preferred_element_type=f32
    )
    node_part_ref[...] += dot_nt(receiver_grad, low_ref[1]) + table_grad[0:particles, :]
    halo_grad[...] = table_grad[particles:, :].astype(bf16)
    low_x = halo_grad[0 : 3 * halo, :]
    high_x = halo_grad[5 * halo : 8 * halo, :]
    halo_own_ref[0:halo, :] = halo_grad[3 * halo : 4 * halo, :]
    halo_own_ref[halo : 2 * halo, :] = jnp.zeros((halo, width), bf16)
    halo_own_ref[2 * halo :, :] = halo_grad[4 * halo : 5 * halo, :]
    quarter = grads.shape[0] // 8
    relay = 2 * quarter
    send_ref[relay : relay + 3 * halo, :] = jnp.where(odd_x == 0, low_x, high_x)
    send_ref[4 * quarter + 3 * halo :, :] = jnp.where(odd_x == 0, high_x, low_x)
    keep_ref[relay : relay + 3 * halo, :] = jnp.zeros((3 * halo, width), f32)
    for slot, spot in enumerate(slot_rows(quarter, halo)):
        kept_rows = part_rows(relayed, odd_x, slot, quarter)
        sent_rows = part_rows(relayed, 1 - odd_x, slot, quarter)
        keep_ref[spot : spot + quarter, :] = grads[kept_rows, :]
        send_ref[spot : spot + quarter, :] = grads[sent_rows, :].astype(bf16)

    for copy in stores:
        copy.wait()
    for p in range(PIECES):
        pltpu.make_async_copy(
            cotangent_buf.at[pl.ds(p * piece, piece)],
            edges_grad_hbm.at[pl.ds(p * piece, piece)],
            out_sems.at[PIECES + p],
        ).wait()


def pinned(values):
    return pltpu.with_memory_space_constraint(values, pltpu.VMEM)


def outer(values):
    return pltpu.with_memory_space_constraint(values, pltpu.HBM)


def plan_call(halo, neighbours, edge_mask, latents, vectors, weights, edges):
    f32, bf16, i32 = jnp.float32, jnp.bfloat16, jnp.int32
    particles, slots = neighbours.shape
    width = latents.shape[1]
    chunks = particles * slots // CHUNK
    whole = pl.BlockSpec(memory_space=pltpu.VMEM)
    outside = pl.BlockSpec(memory_space=pl.ANY)
    buffer = pltpu.VMEM((chunks + 1, CHUNK, width), bf16)
    return pl.pallas_call(
        functools.partial(plan_kernel, halo),
        out_shape=(
            buffer,
            pltpu.VMEM((8, chunks + LANES), i32),
            pltpu.VMEM((particles, chunks), bf16),
            pltpu.VMEM((particles + 8, width), f32),
            pltpu.VMEM((particles + 8, width), f32),
            pltpu.VMEM((weights.shape[0] + 2, width, width), bf16),
            pltpu.VMEM((particles + 8 * halo + width + LANES, 2 * width), bf16),
            pltpu.VMEM((LANES // GROUP, TILE, LANES), bf16),
        ),
        in_specs=[whole] * 4 + [outside] * 2,
        out_specs=(whole,) * 8,
        scratch_shapes=[
            pltpu.VMEM(weights.shape, f32),
            pltpu.SemaphoreType.DMA((1 + PIECES,)),
        ],
        compiler_params=pltpu.CompilerParams(vmem_limit_bytes=16 * 1024 * 1024),
        cost_estimate=pl.CostEstimate(
            flops=10**9, bytes_accessed=12 * 10**6, transcendentals=0
        ),
        name="plan",
    )(
        outer(neighbours.T),
        outer(edge_mask.T),
        outer(latents),
        outer(vectors),
        outer(weights),
        outer(edges),
    )


def layer_call(halo, relayed, grad_rows, counts, latents, ring, ring_far, ring_near, upstream,
               vectors, cotangents, plan):
    f32, bf16, i32 = jnp.float32, jnp.bfloat16, jnp.int32
    edges, listing, segment, neighbour_rows, receiver, low, gather, blocks = plan
    particles, chunks = segment.shape
    width = latents.shape[1]
    rows = particles + 8 * halo
    whole = pl.BlockSpec(memory_space=pltpu.VMEM)
    outside = pl.BlockSpec(memory_space=pl.ANY)
    edge_shape = (chunks, CHUNK, width)
    kept_shape = (chunks + GROUP, CHUNK, width)
    kept = pltpu.VMEM(kept_shape, bf16)
    half = grad_rows // 2
    return pl.pallas_call(
        functools.partial(layer_kernel, halo, relayed),
        out_shape=(
            jax.ShapeDtypeStruct((particles, width), bf16),
            jax.ShapeDtypeStruct(edge_shape, bf16),
            jax.ShapeDtypeStruct(edge_shape, bf16),
            jax.ShapeDtypeStruct((particles, width), f32),
            pltpu.VMEM((3 * halo, width), bf16),
            pltpu.VMEM((half + 6 * halo, width), bf16),
            pltpu.VMEM((half + 3 * halo, width), f32),
            pltpu.VMEM(edges.shape, bf16),
            pltpu.VMEM(gather.shape, bf16),
        ),
        in_specs=[pl.BlockSpec(memory_space=pltpu.SMEM)] + [whole] * 14 + [outside],
        out_specs=(whole, outside, outside) + (whole,) * 6,
        input_output_aliases={13: 7, 14: 8},
        scratch_shapes=[
            pltpu.VMEM(edges.shape, bf16),
            kept,
            pltpu.VMEM(kept_shape, jnp.int16),
            kept,
            kept,
            kept,
            kept,
            kept,
            pltpu.VMEM(kept_shape, f32),
            pltpu.VMEM((rows, width), bf16),
            pltpu.VMEM((particles + 8, width), f32),
            pltpu.VMEM((GROUP, width), f32),
            pltpu.VMEM((chunks + GROUP, width), f32),
            pltpu.VMEM((chunks // LANES + 1, width, LANES), f32),
            pltpu.VMEM((width, rows + width), f32),
            pltpu.VMEM((2, width, width), f32),
            pltpu.VMEM((40, width), f32),
            pltpu.VMEM((TILE, width), f32),
            pltpu.VMEM((TILE, width), f32),
            pltpu.VMEM((TILE, width), bf16),
            pltpu.VMEM((TILE, width), bf16),
            pltpu.VMEM((TILE, width), bf16),
            pltpu.VMEM((4, TILE, width), f32),
            pltpu.VMEM((8 * halo, width), bf16),
            pltpu.VMEM((grad_rows, width), f32),
            pltpu.SMEM((8, chunks + LANES), i32),
            pltpu.SemaphoreType.DMA((PIECES,)),
            pltpu.SemaphoreType.DMA((2 * PIECES,)),
            pltpu.SemaphoreType.DMA,
        ],
        compiler_params=pltpu.CompilerParams(vmem_limit_bytes=52 * 1024 * 1024),
        name="edge_layer",
    )(
        counts,
        outer(latents),
        pinned(ring),
        pinned(ring_far),
        pinned(ring_near),
        outer(upstream),
        outer(vectors),
        pinned(listing),
        pinned(segment),
        pinned(neighbour_rows),
        pinned(receiver),
        pinned(low),
        pinned(blocks),
        pinned(edges),
        pinned(gather),
        outer(cotangents),
    )[:7]


def update_kernel(
    relayed,
    mine_ref,
    other_ref,
    weights_ref,
    vectors_ref,
    weights_m_ref,
    vectors_m_ref,
    weights_v_ref,
    vectors_v_ref,
    weights_ema_ref,
    vectors_ema_ref,
    norm_ref,
    weights_m_out,
    vectors_m_out,
    weights_v_out,
    vectors_v_out,
    weights_out,
    vectors_out,
    weights_copy_out,
    vectors_copy_out,
    weights_ema_out,
    vectors_ema_out,
    grads,
):
    f32 = jnp.float32
    odd = lax.axis_index("gx") & 1
    half_rows, width = mine_ref.shape
    quarter = half_rows // 4
    squares = jnp.zeros((8, width), f32)
    for side, part_ref in ((odd, mine_ref), (1 - odd, other_ref)):
        for slot in range(4):
            values = part_ref[slot * quarter : (slot + 1) * quarter, :].astype(f32)
            grads[part_rows(relayed, side, slot, quarter), :] = values
            squares = squares + jnp.sum((values * values).reshape(quarter // 8, 8, width), axis=0)
    norm = jnp.sqrt(jnp.sum(jnp.sum(squares, axis=1, keepdims=True), axis=0, keepdims=True))
    norm_ref[...] = norm
    scale = clip_norm / jnp.maximum(norm, clip_norm)
    for block in range(weights_ref.shape[0]):
        moment, second, param, average = adamw(
            weights_ref[block],
            grads[block * width : (block + 1) * width, :],
            weights_m_ref[block],
            weights_v_ref[block],
            weights_ema_ref[block],
            scale,
            matrix_rate,
        )
        weights_m_out[block] = moment
        weights_v_out[block] = second
        weights_out[block] = param
        weights_copy_out[block] = param.astype(jnp.bfloat16)
        weights_ema_out[block] = average
    tail = weights_ref.shape[0] * width
    moment, second, param, average = adamw(
        vectors_ref[...],
        grads[tail : tail + vectors_ref.shape[0], :],
        vectors_m_ref[...],
        vectors_v_ref[...],
        vectors_ema_ref[...],
        scale,
        vector_rate,
    )
    vectors_m_out[...] = moment
    vectors_v_out[...] = second
    vectors_out[...] = param
    vectors_copy_out[...] = param.astype(jnp.bfloat16)
    vectors_ema_out[...] = average


def update_call(relayed, mine, other, weights, vectors, weights_m, vectors_m, weights_v, vectors_v,
                weights_ema, vectors_ema):
    f32, bf16 = jnp.float32, jnp.bfloat16
    mat, vec = weights.shape, vectors.shape
    kinds = (
        ((1, 1), f32), (mat, f32), (vec, f32), (mat, f32), (vec, f32), (mat, f32), (vec, f32),
        (mat, bf16), (vec, bf16), (mat, f32), (vec, f32),
    )
    whole = pl.BlockSpec(memory_space=pltpu.VMEM)
    return pl.pallas_call(
        functools.partial(update_kernel, relayed),
        out_shape=tuple(jax.ShapeDtypeStruct(*kind) for kind in kinds),
        in_specs=[whole] * 10,
        out_specs=(whole,) * 11,
        scratch_shapes=[pltpu.VMEM((2 * mine.shape[0], mine.shape[1]), f32)],
        compiler_params=pltpu.CompilerParams(vmem_limit_bytes=24 * 1024 * 1024),
        name="update",
    )(mine, other, weights, vectors, weights_m, vectors_m, weights_v, vectors_v, weights_ema,
      vectors_ema)


def pair_exchange(to_far, to_near, axis):
    near, far = neighbour_pairs(lax.axis_size(axis))
    return lax.ppermute(to_far, axis, far), lax.ppermute(to_near, axis, near)


def partners(axis, stride, mask):
    return [(i, i ^ (mask * stride)) for i in range(lax.axis_size(axis))]


def even_pick(axis, even, odd):
    return jnp.where(lax.axis_index(axis) % 2 == 0, even, odd)


def swap(values, axis, stride, mask):
    return lax.ppermute(values, axis, partners(axis, stride, mask))


def tree_sum(terms):
    while len(terms) > 1:
        terms = [terms[i] + terms[i + 1] for i in range(0, len(terms), 2)]
    return terms[0]


def first_sum_kernel(quarter, halo, keep_ref, got_ref, own_ref, ahead_ref, across_ref, behind_ref):
    rows = 4 * quarter + 3 * halo
    total = keep_ref[...] + got_ref[0:rows, :].astype(jnp.float32)
    spots = slot_rows(quarter, halo)
    own_ref[...] = total[:quarter]
    ahead_ref[...] = total[quarter : 2 * quarter + 3 * halo].astype(jnp.bfloat16)
    across_ref[...] = total[spots[2] : spots[2] + quarter].astype(jnp.bfloat16)
    behind_ref[...] = total[spots[3] : spots[3] + quarter].astype(jnp.bfloat16)


def second_sum_kernel(
    quarter,
    halo,
    own_ref,
    from_behind_ref,
    from_across_ref,
    from_ahead_ref,
    got_ref,
    halo_own_ref,
    mine_ref,
    along1_ref,
    along3_ref,
    middle_ref,
):
    f32, bf16 = jnp.float32, jnp.bfloat16
    index, odd_y = lax.axis_index("gx"), lax.axis_index("gy") & 1
    mine = (own_ref[...] + from_behind_ref[0:quarter, :].astype(f32)) + (
        from_across_ref[...].astype(f32) + from_ahead_ref[...].astype(f32)
    )
    mine = mine.astype(bf16)
    mine_ref[...] = mine
    far = from_behind_ref[quarter:, :].astype(f32)
    far = jnp.where((index == 0) | (index == 7), 0.0, far)
    strips = halo_own_ref[...].astype(f32) + got_ref[4 * quarter + 3 * halo :, :].astype(f32) + far
    low, high = strips[:halo].astype(bf16), strips[2 * halo :].astype(bf16)
    middle_ref[...] = strips[halo : 2 * halo]
    along3_ref[0:halo, :] = jnp.where(odd_y == 0, low, high)
    along3_ref[halo:, :] = mine
    along1_ref[0:halo, :] = jnp.where(odd_y == 0, high, low)
    along1_ref[halo:, :] = mine


def in_vmem(kernel, name, shapes, *operands):
    whole = pl.BlockSpec(memory_space=pltpu.VMEM)
    return pl.pallas_call(
        kernel,
        out_shape=tuple(pltpu.VMEM(shape, dtype) for shape, dtype in shapes),
        in_specs=[whole] * len(operands),
        out_specs=(whole,) * len(shapes),
        compiler_params=pltpu.CompilerParams(vmem_limit_bytes=8 * 1024 * 1024),
        name=name,
    )(*[pinned(operand) for operand in operands])


def sum_relayed(send, keep, halo_own, halo):
    f32, bf16 = jnp.float32, jnp.bfloat16
    width = send.shape[1]
    quarter = (send.shape[0] - 6 * halo) // 4
    index, row = lax.axis_index("gx"), lax.axis_index("gy")

    def turned(values, step):
        pairs = [(i, ((i >> 1) + step * (1 - 2 * (i & 1))) % 4 * 2 + (i & 1)) for i in range(8)]
        return lax.ppermute(values, "gx", pairs)

    got = swap(send, "gx", 1, 1)
    own, ahead, across, behind = in_vmem(
        functools.partial(first_sum_kernel, quarter, halo),
        "first_sum",
        (
            ((quarter, width), f32),
            ((quarter + 3 * halo, width), bf16),
            ((quarter, width), bf16),
            ((quarter, width), bf16),
        ),
        keep,
        got,
    )
    from_behind = turned(ahead, 1)
    from_ahead = turned(behind, 3)
    from_across = turned(across, 2)
    mine, to1, to3, middle = in_vmem(
        functools.partial(second_sum_kernel, quarter, halo),
        "second_sum",
        (
            ((quarter, width), bf16),
            ((quarter + halo, width), bf16),
            ((quarter + halo, width), bf16),
            ((halo, width), f32),
        ),
        own,
        from_behind,
        from_across,
        from_ahead,
        got,
        halo_own,
    )
    along3 = swap(to3, "gy", 1, 3)
    along2 = swap(mine, "gy", 1, 2)
    along1 = swap(to1, "gy", 1, 1)
    mine = tree_sum(
        [
            mine.astype(f32),
            along1[halo:].astype(f32),
            along2.astype(f32),
            along3[halo:].astype(f32),
        ]
    ).astype(bf16)
    last_far = jnp.where((row == 0) | (row == 3), bf16(0), along3[:halo])
    part3, part2, part1 = (swap(mine, "gx", 2, mask) for mask in (3, 2, 1))
    onward = ((index >> 1) & 1) == (index & 1)
    mine = jnp.concatenate(
        [mine, jnp.where(onward, part1, part3), part2, jnp.where(onward, part3, part1)]
    )
    return mine, swap(mine, "gx", 1, 1), middle, last_far, along1[:halo]


def sum_staged(send, keep, halo_own, halo):
    f32, bf16 = jnp.float32, jnp.bfloat16
    width = send.shape[1]
    quarter = (send.shape[0] - 6 * halo) // 4
    slots = slot_rows(quarter, halo)

    def joined_slots(values):
        return jnp.concatenate([values[spot : spot + quarter] for spot in slots])

    far = send[2 * quarter : 2 * quarter + 3 * halo]
    near = send[4 * quarter + 3 * halo :]
    back_far, back_near = pair_exchange(far, near, "gx")
    strips = halo_own.astype(f32) + back_far.astype(f32) + back_near.astype(f32)
    low, high = strips[:halo].astype(bf16), strips[2 * halo :].astype(bf16)
    last_far, last_near = pair_exchange(
        even_pick("gy", low, high), even_pick("gy", high, low), "gy"
    )
    index = lax.axis_index("gx")
    got = swap(joined_slots(send), "gx", 1, 1)
    total = (joined_slots(keep) + got.astype(f32)).astype(bf16)
    split = stages(lax.axis_size("gx"))[1:]
    for stride, factor in split:
        part = (index // stride) % factor
        height = total.shape[0] // factor
        mine = lax.dynamic_slice_in_dim(total, part * height, height, 0).astype(f32)
        for mask in range(factor - 1, 0, -1):
            piece = lax.dynamic_slice_in_dim(total, (part ^ mask) * height, height, 0)
            mine = mine + swap(piece, "gx", stride, mask).astype(f32)
        total = mine.astype(bf16)
    total = tree_sum(
        [total.astype(f32)]
        + [swap(total, "gy", 1, mask).astype(f32) for mask in range(1, lax.axis_size("gy"))]
    ).astype(bf16)
    for stride, factor in reversed(split):
        part = (index // stride) % factor
        height = total.shape[0]
        joined = jnp.zeros((factor * height, width), bf16)
        joined = lax.dynamic_update_slice_in_dim(joined, total, part * height, 0)
        for mask in range(factor - 1, 0, -1):
            piece = swap(total, "gx", stride, mask)
            joined = lax.dynamic_update_slice_in_dim(joined, piece, (part ^ mask) * height, 0)
        total = joined
    return total, swap(total, "gx", 1, 1), strips[halo : 2 * halo], last_far, last_near


def per_device(
    node_latents,
    edge_latents,
    node_cotangent,
    edge_cotangent,
    neighbours,
    edge_mask,
    send_table,
    counts,
    weights,
    vectors,
    weights_m,
    vectors_m,
    weights_v,
    vectors_v,
    weights_ema,
    vectors_ema,
):
    f32, bf16 = jnp.float32, jnp.bfloat16
    tok_rows, width = node_latents.shape
    halo = send_table.shape[1]
    boundary_pick = selector(send_table[0], tok_rows, bf16)
    boundary = jnp.dot(boundary_pick, node_latents, preferred_element_type=f32).astype(bf16)
    from_far, from_near = pair_exchange(boundary, boundary, "gx")
    ring = jnp.concatenate([from_far, from_near, boundary], axis=0)
    ring_far, ring_near = pair_exchange(ring, ring, "gy")
    unit = 16 * lax.axis_size("gx")
    grad_rows = -(-(weights.shape[0] * width + vectors.shape[0]) // unit) * unit
    relayed = lax.axis_size("gx") == 8 and lax.axis_size("gy") == 4
    edge_shape = (tok_rows * neighbours.shape[1] // CHUNK, CHUNK, width)
    plan = plan_call(
        halo, neighbours, edge_mask, node_latents, vectors, weights,
        edge_latents.reshape(edge_shape),
    )
    nodes_out, edges_out, edges_in_grad, node_part, halo_own, send, keep = layer_call(
        halo, relayed, grad_rows, counts, node_latents, ring, ring_far, ring_near,
        node_cotangent, vectors, edge_cotangent.reshape(edge_shape), plan,
    )
    sums = sum_relayed if relayed else sum_staged
    mine, other, middle, last_far, last_near = sums(send, keep, halo_own, halo)
    boundary_grad = middle + last_far.astype(f32) + last_near.astype(f32)
    returned = lax.dot_general(
        boundary_pick.astype(f32),
        boundary_grad,
        (((0,), (0,)), ((), ())),
        precision=lax.Precision.HIGHEST,
        preferred_element_type=f32,
    )
    nodes_in_grad = (node_part + returned).astype(bf16)
    updated = update_call(
        relayed, mine, other, weights, vectors, weights_m, vectors_m, weights_v, vectors_v, weights_ema,
        vectors_ema,
    )
    return (
        nodes_out,
        edges_out.reshape(edge_latents.shape),
        nodes_in_grad,
        edges_in_grad.reshape(edge_latents.shape),
        updated[0].reshape(()),
    ) + tuple(updated[1:])


def solution(mesh):
    in_specs = (
        P(("gx", "gy"), None),
        P(("gx", "gy"), None, None),
        P(("gx", "gy"), None),
        P(("gx", "gy"), None, None),
        P(("gx", "gy"), None),
        P(("gx", "gy"), None),
        P(("gx", "gy"), None),
        P(("gx", "gy")),
        P(),
        P(),
        P(),
        P(),
        P(),
        P(),
        P(),
        P(),
    )
    out_specs = (
        P(("gx", "gy"), None),
        P(("gx", "gy"), None, None),
        P(("gx", "gy"), None),
        P(("gx", "gy"), None, None),
        P(),
        P(),
        P(),
        P(),
        P(),
        P(),
        P(),
        P(),
        P(),
        P(),
        P(),
    )
    return jax.shard_map(
        per_device, mesh=mesh, in_specs=in_specs, out_specs=out_specs, check_vma=False
    )
```

```python
import functools

import jax
import jax.numpy as jnp
from jax import lax
from jax.experimental import pallas as pl
from jax.experimental.pallas import tpu as pltpu
from jax.sharding import PartitionSpec as P

STEP = 10


first_decay = 0.5
second_decay = 0.5
adam_epsilon = 1e-08
weight_decay = 0.01
matrix_rate = 0.05
vector_rate = 0.2
average_decay = 0.9
clip_norm = 1.0
norm_epsilon = 1e-05


def neighbour_pairs(count):
    near = [(i, i ^ 1) for i in range(count) if (i ^ 1) < count]
    far = [(i, i + 1) for i in range(1, count - 1, 2)]
    return near, far + [(target, source) for source, target in far]


def stages(count):
    result, stride = [], 1
    while stride < count:
        factor = 2 if stride == 1 else min(4, count // stride)
        result.append((stride, factor))
        stride *= factor
    return result


def selector(indices, width, dtype):
    columns = lax.broadcasted_iota(jnp.int32, (indices.shape[0], width), 1)
    return (indices[:, None] == columns).astype(dtype)


def adamw(param, grad, moment, second, average, scale, rate):
    clipped = grad * scale
    moment_new = first_decay * moment + (1.0 - first_decay) * clipped
    second_new = second_decay * second + (1.0 - second_decay) * clipped * clipped
    corrected = moment_new / (1.0 - first_decay**STEP)
    denom = jnp.sqrt(second_new / (1.0 - second_decay**STEP)) + adam_epsilon
    param_new = param - rate * (corrected / denom + weight_decay * param)
    average_new = average_decay * average + (1.0 - average_decay) * param_new
    return (moment_new, second_new, param_new, average_new)


CHUNK = 16
GROUP = 32
UPDATE_ROWS = 32
TILE = CHUNK * GROUP
LANES = 128
PIECES = 8


def dot(left, right):
    return jnp.dot(left, right, preferred_element_type=jnp.float32)


def dot_nt(left, right):
    return lax.dot_general(
        left, right, (((1,), (1,)), ((), ())), preferred_element_type=jnp.float32
    )


def dot_tn(left, right):
    return lax.dot_general(
        left, right, (((0,), (0,)), ((), ())), preferred_element_type=jnp.float32
    )


def split_pair(values, axis=1):
    high = values.astype(jnp.bfloat16)
    low = (values - high.astype(jnp.float32)).astype(jnp.bfloat16)
    return jnp.concatenate([high, low], axis=axis)


def halves(pair):
    width = pair.shape[1] // 2
    return pair[:, :width] + pair[:, width:]


def silu_of_half(half):
    turn = jnp.tanh(half)
    lift = 1.0 + turn
    act = half * lift
    return act, lift + act * (1.0 - turn)


def row_sum(values):
    return jnp.sum(values, axis=-1, keepdims=True)


def scaled_unit(values, width):
    center = values - row_sum(values) * (1.0 / width)
    inverse = lax.rsqrt(row_sum(center * center) + width * norm_epsilon)
    return center * inverse, inverse


def scaled_unit_back(scaled, unit, inverse, width):
    shift = row_sum(scaled) * (1.0 / width)
    return inverse * (scaled - shift - unit * row_sum(scaled * unit))


def column_total(values):
    return jnp.sum(values, axis=0, keepdims=True)


def iota(shape, dim):
    return lax.broadcasted_iota(jnp.int32, shape, dim)


def slot_rows(quarter, halo):
    return (0, quarter, 2 * quarter + 3 * halo, 3 * quarter + 3 * halo)


def part_rows(relayed, side, slot, quarter):
    chip = lax.axis_index("gx") >> 1
    part = (chip + slot * (1 - 2 * side)) & 3 if relayed else slot
    return pl.ds(pl.multiple_of((side * 4 + part) * quarter, 16), quarter)


def plan_kernel(
    halo,
    count_ref,
    mask_hbm,
    neighbour_hbm,
    latents_hbm,
    vectors_hbm,
    upstream_hbm,
    weights_hbm,
    edges_hbm,
    latents_ref,
    vectors_ref,
    upstream_ref,
    edges_buf,
    list_rows,
    segment_ref,
    neighbour_rows,
    receiver_ref,
    low_ref,
    gather_ref,
    blocks_ref,
    mask_ref,
    neighbour_ref,
    weights_ref,
    sems,
):
    f32, bf16, i32 = jnp.float32, jnp.bfloat16, jnp.int32
    slots, particles = neighbour_ref.shape
    per = slots // CHUNK
    chunks = particles * per
    width = latents_ref.shape[1]
    rows = particles + 8 * halo
    fetches = [
        pltpu.make_async_copy(source, target, sems.at[order])
        for order, (source, target) in enumerate(
            (
                (mask_hbm, mask_ref),
                (neighbour_hbm, neighbour_ref),
                (latents_hbm, latents_ref),
                (vectors_hbm, vectors_ref),
                (weights_hbm, weights_ref),
                (upstream_hbm, upstream_ref),
            )
        )
    ]
    for copy in fetches:
        copy.start()
    piece = chunks // PIECES
    loads = [
        pltpu.make_async_copy(
            edges_hbm.at[pl.ds(p * piece, piece)],
            edges_buf.at[pl.ds(p * piece, piece)],
            sems.at[len(fetches) + p],
        )
        for p in range(PIECES)
    ]
    for copy in loads:
        copy.start()
    edges_buf[chunks] = jnp.zeros((CHUNK, width), bf16)
    fetches[0].wait()

    mask = mask_ref[...].astype(f32)
    degree = jnp.sum(mask, axis=0, keepdims=True)
    taken = ((degree.astype(i32) + (CHUNK - 1)) >> 4).astype(f32)
    earlier = iota((particles, particles), 0) < iota((particles, particles), 1)
    begin = dot(jnp.broadcast_to(taken, (16, particles)).astype(bf16), earlier.astype(bf16))
    degree_col = dot_tn(mask.astype(bf16), jnp.ones((slots, width), bf16))
    taken_col = ((degree_col.astype(i32) + (CHUNK - 1)) >> 4).astype(f32)
    later = iota((particles, particles), 1) < iota((particles, particles), 0)
    begin_col = dot(later.astype(bf16), taken_col.astype(bf16))
    end_col = begin_col + taken_col
    for block in range(chunks // width):
        lane = iota((particles, width), 1).astype(f32) + block * width
        segment_ref[:, block * width : (block + 1) * width] = (
            (lane >= begin_col) & (lane < end_col)
        ).astype(bf16)
    total = row_sum(taken)
    who = iota((16, particles), 1).astype(f32)
    offset = per * who - begin
    coarse = jnp.floor(offset * 0.125) * 8.0
    line = iota((16, particles), 0)
    facts = jnp.where(
        line == 0,
        who,
        jnp.where(line == 1, coarse, jnp.where(line == 2, offset - coarse, degree)),
    )
    listing = dot(facts.astype(bf16), segment_ref[...])
    place = iota((1, chunks), 1).astype(f32)
    particle = listing[0:1, :]
    chunk = listing[1:2, :] + listing[2:3, :] + place
    rest = listing[3:4, :] - CHUNK * (chunk - per * particle)
    used = place < total
    list_rows[...] = jnp.zeros(list_rows.shape, i32)
    list_rows[0:1, 0:chunks] = jnp.where(used, chunk, float(chunks)).astype(i32)
    list_rows[0:1, chunks:] = jnp.full((1, list_rows.shape[1] - chunks), chunks, i32)
    list_rows[1:2, 0:chunks] = jnp.where(used, particle, float(particles)).astype(i32)
    list_rows[1:2, chunks:] = jnp.full((1, list_rows.shape[1] - chunks), particles, i32)
    list_rows[2:3, 0:chunks] = jnp.where(used, rest, 0.0).astype(i32)
    list_rows[3:4, 0:particles] = jnp.broadcast_to(total, (1, particles)).astype(i32)
    list_rows[4:5, 0:particles] = (begin[0:1, :] + taken).astype(i32)
    list_rows[5:6, 0:particles] = jnp.full((1, particles), count_ref[0], i32)

    fetches[1].wait()
    neighbour = neighbour_ref[...]
    neighbour = jnp.where(neighbour >= particles + 5 * halo, neighbour - halo, neighbour)
    neighbour_rows[...] = jnp.zeros(neighbour_rows.shape, f32)
    neighbour_rows[0:particles, 0:slots] = neighbour.astype(f32).T

    block_of = iota((TILE, LANES), 0) >> 4
    for quarter in range(LANES // GROUP):
        blocks_ref[quarter] = (iota((TILE, LANES), 1) == block_of + quarter * GROUP).astype(bf16)

    for copy in fetches[2:]:
        copy.wait()
    for block in range(weights_ref.shape[0]):
        low_ref[block] = weights_ref[block].astype(bf16)
    for extra, block in ((9, 3), (10, 4)):
        low_ref[extra] = (0.5 * low_ref[block].astype(f32)).astype(bf16)
    latents = latents_ref[...]
    gather_ref[0:particles, :] = split_pair(0.5 * dot(latents, low_ref[2]))
    gather_ref[particles:rows, :] = jnp.zeros((rows - particles, 2 * width), bf16)
    gather_ref[rows : rows + width, :] = jnp.concatenate(
        [(0.5 * low_ref[0].astype(f32)).astype(bf16), jnp.zeros((width, width), bf16)], axis=1
    )
    gather_ref[rows + width :, :] = jnp.zeros((LANES, 2 * width), bf16)
    receiver_ref[0:particles, :] = 0.5 * (dot(latents, low_ref[1]) + vectors_ref[0:1, :])
    receiver_ref[particles:, :] = jnp.zeros((receiver_ref.shape[0] - particles, width), f32)
    for copy in loads:
        copy.wait()


def layer_kernel(
    halo,
    relayed,
    latents_ref,
    ring_ref,
    ring_far_ref,
    ring_near_ref,
    upstream_ref,
    vectors_ref,
    list_rows,
    segment_ref,
    neighbour_rows,
    receiver_ref,
    low_ref,
    blocks_ref,
    edges_in,
    gather_in,
    cotangent_hbm,
    nodes_out_hbm,
    edges_out_hbm,
    edges_grad_hbm,
    node_part_ref,
    halo_own_ref,
    send_ref,
    keep_ref,
    edges_buf,
    gather_ref,
    nodes_out_ref,
    cotangent_buf,
    kept_edges,
    kept_index,
    kept_act1,
    kept_act2,
    kept_slope1,
    kept_slope2,
    kept_unit,
    kept_inverse,
    table_ref,
    descent_ref,
    receiver_tile,
    chunk_sums,
    chunk_grads,
    index_acc,
    mat_acc,
    vec_acc,
    first_tile,
    last_tile,
    third_tile,
    first_back,
    second_back,
    passed_tile,
    halo_grad,
    grads,
    listed,
    in_sems,
    out_sems,
    list_sem,
    nodes_sem,
):
    f32, bf16, i32 = jnp.float32, jnp.bfloat16, jnp.int32
    fetch_list = pltpu.make_async_copy(list_rows, listed, list_sem)
    fetch_list.start()
    particles, chunks = segment_ref.shape
    per = chunks // particles
    width = latents_ref.shape[1]
    rows = table_ref.shape[0]
    piece = chunks // PIECES
    root = float(width) ** 0.5
    odd_x = lax.axis_index("gx") & 1
    odd_y = lax.axis_index("gy") & 1
    loads = [
        pltpu.make_async_copy(
            cotangent_hbm.at[pl.ds(p * piece, piece)],
            cotangent_buf.at[pl.ds(p * piece, piece)],
            in_sems.at[p],
        )
        for p in range(PIECES)
    ]
    for copy in loads:
        copy.start()
    cotangent_buf[chunks] = jnp.zeros((CHUNK, width), bf16)

    table_ref[0:particles, :] = latents_ref[...]
    far, near, own = ring_far_ref[...], ring_near_ref[...], ring_ref[...]
    low_y = jnp.where(odd_y == 0, far, near)
    high_y = jnp.where(odd_y == 0, near, far)
    spot = particles
    for a in range(3):
        for b, strip in enumerate((low_y, own, high_y)):
            if a == 1 and b == 1:
                continue
            if a == 1:
                part = strip[2 * halo :]
            elif a == 0:
                part = jnp.where(odd_x == 0, strip[0:halo], strip[halo : 2 * halo])
            else:
                part = jnp.where(odd_x == 0, strip[halo : 2 * halo], strip[0:halo])
            table_ref[spot : spot + halo, :] = part
            spot += halo

    vectors = vectors_ref[...]

    def vector(row):
        return vectors[row : row + 1, :]

    latents = latents_ref[...]
    half3, half4 = low_ref[9], low_ref[10]
    gather_ref[particles:rows, :] = split_pair(0.5 * dot(table_ref[particles:, :], low_ref[2]))
    chunk_sums[...] = jnp.zeros(chunk_sums.shape, f32)
    chunk_grads[...] = jnp.zeros(chunk_grads.shape, f32)
    index_acc[...] = jnp.zeros(index_acc.shape, f32)
    mat_acc[...] = jnp.zeros(mat_acc.shape, f32)
    vec_acc[...] = jnp.zeros(vec_acc.shape, f32)
    tail = 9 * width
    grads[tail:, :] = jnp.zeros((grads.shape[0] - tail, width), f32)
    descent_ref[particles:, :] = jnp.zeros((descent_ref.shape[0] - particles, width), f32)

    fetch_list.wait()
    tiles = (listed[3, 0] + (GROUP - 1)) >> 5

    sublane = iota((CHUNK, width), 0)
    diagonal = iota((CHUNK, width), 1) - sublane
    lane16 = iota((TILE, width), 1).astype(jnp.int16)

    def flat(ref, t):
        return ref[pl.ds(t * GROUP, GROUP)].reshape(TILE, width)

    def keep(ref, t, values):
        ref[pl.ds(t * GROUP, GROUP)] = values.astype(ref.dtype).reshape(GROUP, CHUNK, width)

    def span(j):
        return slice(j * CHUNK, (j + 1) * CHUNK)

    def one_hot(t):
        index = flat(kept_index, t)
        return [
            jnp.where(index == lane16 + jnp.int16(b * width), bf16(1), bf16(0))
            for b in range(rows // width)
        ]

    def gather(t):
        base = t * GROUP
        for j in range(GROUP):
            chunk, particle = listed[0, base + j], listed[1, base + j]
            kept_edges[base + j] = edges_buf[chunk]
            row = jnp.broadcast_to(neighbour_rows[pl.ds(particle, 1), :], (CHUNK, width))
            start = (chunk & (per - 1)) * CHUNK
            index = row_sum(jnp.where(diagonal == start, row, 0.0))
            kept_index[base + j] = (
                jnp.broadcast_to(index, (CHUNK, width)).astype(i32).astype(jnp.int16)
            )
            receiver_tile[j : j + 1, :] = receiver_ref[pl.ds(particle, 1), :]
        gather_ref[rows + width : rows + width + GROUP, :] = split_pair(receiver_tile[...])

    def project(t):
        picks = jnp.concatenate(one_hot(t) + [flat(kept_edges, t), blocks_ref[0]], axis=1)
        first_tile[...] = halves(dot(picks, gather_ref[...]))

    gain_root = vector(3) * root

    def finish(t):
        base = t * GROUP
        unit, inverse = scaled_unit(last_tile[...], width)
        keep(kept_unit, t, unit)
        keep(kept_inverse, t, jnp.broadcast_to(inverse, (TILE, width)))
        change = unit * gain_root + vector(4)
        for j in range(GROUP):
            chunk = listed[0, base + j]
            alive = sublane < listed[2, base + j]
            fresh = kept_edges[base + j].astype(f32) + jnp.where(alive, change[span(j)], 0.0)
            edges_buf[chunk] = fresh.astype(bf16)
            chunk_sums[pl.ds(base + j, 1), :] = column_total(jnp.where(alive, fresh, 0.0))

    def forward(t, carry):
        gather(t + 1)
        act, slope = silu_of_half(first_tile[...])
        act = act.astype(bf16)
        keep(kept_act1, t, act)
        keep(kept_slope1, t, slope)
        finish(jnp.where(t == 0, tiles, t - 1))
        act, slope = silu_of_half(dot(act, half3) + 0.5 * vector(1))
        act = act.astype(bf16)
        keep(kept_act2, t, act)
        keep(kept_slope2, t, slope)
        project(t + 1)
        last_tile[...] = dot(act, low_ref[4]) + vector(2)
        return carry

    for ref in (kept_act1, kept_edges):
        keep(ref, tiles, jnp.zeros((TILE, width), f32))
    last_tile[...] = jnp.zeros(last_tile.shape, f32)
    gather(0)
    project(0)
    lax.fori_loop(0, tiles, forward, 0)
    finish(jnp.where(tiles == 0, tiles, tiles - 1))

    stores = [
        pltpu.make_async_copy(
            edges_buf.at[pl.ds(p * piece, piece)],
            edges_out_hbm.at[pl.ds(p * piece, piece)],
            out_sems.at[p],
        )
        for p in range(PIECES)
    ]
    for copy in stores:
        copy.start()

    aggregate = halves(dot(segment_ref[...], split_pair(chunk_sums[0:chunks, :]))).astype(bf16)
    half1 = 0.5 * (dot(latents, low_ref[5]) + dot(aggregate, low_ref[6]) + vector(5))
    act1, slope1 = silu_of_half(half1)
    act1 = act1.astype(bf16)
    act2, slope2 = silu_of_half(0.5 * (dot(act1, low_ref[7]) + vector(6)))
    act2 = act2.astype(bf16)
    unit, inverse = scaled_unit(dot(act2, low_ref[8]) + vector(7), width)
    alive = (iota((particles, width), 0) < listed[5, 0]).astype(f32)
    upstream = upstream_ref[...].astype(f32)
    nodes_out_ref[...] = (
        latents.astype(f32) + alive * (unit * (vector(8) * root) + vector(9))
    ).astype(bf16)
    send_nodes = pltpu.make_async_copy(nodes_out_ref, nodes_out_hbm, nodes_sem)
    send_nodes.start()
    held = alive * upstream
    third = scaled_unit_back(held * (vector(8) * root), unit, inverse, width).astype(bf16)
    second = (0.5 * slope2 * dot_nt(third, low_ref[8])).astype(bf16)
    first = (0.5 * slope1 * dot_nt(second, low_ref[7])).astype(bf16)
    descent_ref[0:particles, :] = dot_nt(first, low_ref[6])
    node_part_ref[...] = upstream + dot_nt(first, low_ref[5])

    def put_block(block, values):
        grads[block * width : (block + 1) * width, :] = values

    put_block(5, dot_tn(latents, first))
    put_block(6, dot_tn(aggregate, first))
    put_block(7, dot_tn(act1, second))
    put_block(8, dot_tn(act2, third))
    for row, values in enumerate(
        (first.astype(f32), second.astype(f32), third.astype(f32), held * unit * root, held)
    ):
        grads[tail + 5 + row : tail + 6 + row, :] = column_total(values)

    for copy in loads:
        copy.wait()

    def add_columns(row, values):
        vec_acc[8 * row : 8 * row + 8, :] += jnp.sum(values.reshape(TILE // 8, 8, width), axis=0)

    def accept(t):
        base = t * GROUP
        parts = []
        for j in range(GROUP):
            chunk, particle = listed[0, base + j], listed[1, base + j]
            alive = sublane < listed[2, base + j]
            passed = cotangent_buf[chunk].astype(f32) + jnp.where(
                alive, descent_ref[pl.ds(particle, 1), :], 0.0
            )
            passed_tile[t & 3, span(j), :] = passed
            parts.append(jnp.where(alive, passed, 0.0))
        return jnp.concatenate(parts, axis=0)

    def descend(t, held):
        unit = flat(kept_unit, t).astype(f32)
        third = scaled_unit_back(held * gain_root, unit, flat(kept_inverse, t), width)
        third_tile[...] = third.astype(bf16)
        add_columns(2, third)
        add_columns(3, held * unit)
        add_columns(4, held)

    def settle(t, slot):
        base = t * GROUP
        first = first_back[...]
        result = passed_tile[slot] + dot_nt(first, low_ref[0])
        for j in range(GROUP):
            cotangent_buf[listed[0, base + j]] = result[span(j)].astype(bf16)
        picks = jnp.concatenate(one_hot(t) + [flat(kept_edges, t), blocks_ref[t & 3]], axis=1)
        index_acc[...] += dot_tn(first, picks[:, 0 : rows + width])
        chunk_grads[t >> 2] += dot_tn(first, picks[:, rows + width :])
        mat_acc[0] += dot_tn(flat(kept_act1, t), second_back[...])

    def backward(t, carry):
        third = third_tile[...]
        second = dot_nt(third, half4)
        held = accept(t + 1)
        settle(jnp.where(t == 0, tiles, t - 1), (t + 3) & 3)
        second = flat(kept_slope2, t).astype(f32) * second
        add_columns(1, second)
        second = second.astype(bf16)
        descend(t + 1, held)
        first = flat(kept_slope1, t).astype(f32) * dot_nt(second, half3)
        mat_acc[1] += dot_tn(flat(kept_act2, t), third)
        first_back[...] = first.astype(bf16)
        second_back[...] = second
        return carry

    first_back[...] = jnp.zeros(first_back.shape, bf16)
    second_back[...] = jnp.zeros(second_back.shape, bf16)
    passed_tile[3] = jnp.zeros((TILE, width), f32)
    descend(0, accept(0))
    def send_piece(p):
        pltpu.make_async_copy(
            cotangent_buf.at[pl.ds(p * piece, piece)],
            edges_grad_hbm.at[pl.ds(p * piece, piece)],
            out_sems.at[PIECES + p],
        ).start()

    def last_tile(p):
        return (listed[4, (p + 1) * (piece // per) - 1] + (GROUP - 1)) >> 5

    def backward_piece(p, t):
        upto = last_tile(p) + 1
        stop = jnp.minimum(upto, tiles)
        lax.fori_loop(t, stop, backward, 0)

        @pl.when(upto <= tiles)
        def _():
            send_piece(p)

        return jnp.maximum(t, stop)

    lax.fori_loop(0, PIECES, backward_piece, jnp.int32(0))
    settle(jnp.where(tiles == 0, tiles, tiles - 1), (tiles + 3) & 3)

    @pl.loop(0, PIECES)
    def _(p):
        @pl.when(last_tile(p) + 1 > tiles)
        def _():
            send_piece(p)

    stacked = split_pair(
        jnp.concatenate([chunk_grads[g] for g in range(chunks // LANES)], axis=1), axis=0
    )
    receiver_grad = halves(dot_nt(segment_ref[...], stacked)).astype(bf16)
    grads[tail : tail + 1, :] = halves(dot_nt(jnp.ones((8, chunks), bf16), stacked))[0:1, :]
    for row in range(1, 5):
        values = column_total(vec_acc[8 * row : 8 * row + 8, :])
        grads[tail + row : tail + row + 1, :] = values * root if row == 3 else values
    sent = index_acc[:, 0:rows].astype(bf16)
    put_block(0, index_acc[:, rows:].T)
    put_block(1, dot_tn(latents, receiver_grad))
    put_block(2, dot(sent, table_ref[...]).T)
    put_block(3, mat_acc[0])
    put_block(4, mat_acc[1])
    table_grad = lax.dot_general(
        sent, low_ref[2], (((0,), (1,)), ((), ())), preferred_element_type=f32
    )
    node_part_ref[...] += dot_nt(receiver_grad, low_ref[1]) + table_grad[0:particles, :]
    halo_grad[...] = table_grad[particles:, :].astype(bf16)
    low_x = halo_grad[0 : 3 * halo, :]
    high_x = halo_grad[5 * halo : 8 * halo, :]
    halo_own_ref[0:halo, :] = halo_grad[3 * halo : 4 * halo, :]
    halo_own_ref[halo : 2 * halo, :] = jnp.zeros((halo, width), bf16)
    halo_own_ref[2 * halo :, :] = halo_grad[4 * halo : 5 * halo, :]
    quarter = grads.shape[0] // 8
    relay = 2 * quarter
    send_ref[relay : relay + 3 * halo, :] = jnp.where(odd_x == 0, low_x, high_x)
    send_ref[4 * quarter + 3 * halo :, :] = jnp.where(odd_x == 0, high_x, low_x)
    keep_ref[relay : relay + 3 * halo, :] = jnp.zeros((3 * halo, width), f32)
    for slot, spot in enumerate(slot_rows(quarter, halo)):
        kept_rows = part_rows(relayed, odd_x, slot, quarter)
        sent_rows = part_rows(relayed, 1 - odd_x, slot, quarter)
        keep_ref[spot : spot + quarter, :] = grads[kept_rows, :]
        send_ref[spot : spot + quarter, :] = grads[sent_rows, :].astype(bf16)

    for copy in stores + [send_nodes]:
        copy.wait()
    for p in range(PIECES):
        pltpu.make_async_copy(
            cotangent_buf.at[pl.ds(p * piece, piece)],
            edges_grad_hbm.at[pl.ds(p * piece, piece)],
            out_sems.at[PIECES + p],
        ).wait()


def pinned(values):
    return pltpu.with_memory_space_constraint(values, pltpu.VMEM)


def outer(values):
    return pltpu.with_memory_space_constraint(values, pltpu.HBM)


def plan_call(halo, counts, neighbours, edge_mask, latents, vectors, upstream, weights, edges):
    f32, bf16, i32 = jnp.float32, jnp.bfloat16, jnp.int32
    particles, slots = neighbours.shape
    width = latents.shape[1]
    chunks = particles * slots // CHUNK
    whole = pl.BlockSpec(memory_space=pltpu.VMEM)
    outside = pl.BlockSpec(memory_space=pl.ANY)
    return pl.pallas_call(
        functools.partial(plan_kernel, halo),
        out_shape=(
            pltpu.VMEM(latents.shape, bf16),
            pltpu.VMEM(vectors.shape, f32),
            pltpu.VMEM(upstream.shape, bf16),
            pltpu.VMEM((chunks + 1, CHUNK, width), bf16),
            pltpu.VMEM((8, chunks + LANES), i32),
            pltpu.VMEM((particles, chunks), bf16),
            pltpu.VMEM((particles + 8, width), f32),
            pltpu.VMEM((particles + 8, width), f32),
            pltpu.VMEM((weights.shape[0] + 2, width, width), bf16),
            pltpu.VMEM((particles + 8 * halo + width + LANES, 2 * width), bf16),
            pltpu.VMEM((LANES // GROUP, TILE, LANES), bf16),
        ),
        in_specs=[pl.BlockSpec(memory_space=pltpu.SMEM)] + [outside] * 7,
        out_specs=(whole,) * 11,
        scratch_shapes=[
            pltpu.VMEM((slots, particles), i32),
            pltpu.VMEM((slots, particles), i32),
            pltpu.VMEM(weights.shape, f32),
            pltpu.SemaphoreType.DMA((6 + PIECES,)),
        ],
        compiler_params=pltpu.CompilerParams(vmem_limit_bytes=16 * 1024 * 1024),
        cost_estimate=pl.CostEstimate(
            flops=10**9, bytes_accessed=12 * 10**6, transcendentals=0
        ),
        name="plan",
    )(
        counts,
        outer(edge_mask.T),
        outer(neighbours.T),
        outer(latents),
        outer(vectors),
        outer(upstream),
        outer(weights),
        outer(edges),
    )


def layer_call(halo, relayed, grad_rows, ring, ring_far, ring_near, cotangents, plan):
    f32, bf16, i32 = jnp.float32, jnp.bfloat16, jnp.int32
    latents, vectors, upstream, edges, listing, segment, *more, gather, blocks = plan
    neighbour_rows, receiver, low = more
    particles, chunks = segment.shape
    width = latents.shape[1]
    rows = particles + 8 * halo
    whole = pl.BlockSpec(memory_space=pltpu.VMEM)
    outside = pl.BlockSpec(memory_space=pl.ANY)
    edge_shape = (chunks, CHUNK, width)
    kept_shape = (chunks + GROUP, CHUNK, width)
    kept = pltpu.VMEM(kept_shape, bf16)
    half = grad_rows // 2
    return pl.pallas_call(
        functools.partial(layer_kernel, halo, relayed),
        out_shape=(
            jax.ShapeDtypeStruct((particles, width), bf16),
            jax.ShapeDtypeStruct(edge_shape, bf16),
            jax.ShapeDtypeStruct(edge_shape, bf16),
            pltpu.VMEM((particles, width), f32),
            pltpu.VMEM((3 * halo, width), bf16),
            pltpu.VMEM((half + 6 * halo, width), bf16),
            pltpu.VMEM((half + 3 * halo, width), f32),
            pltpu.VMEM(edges.shape, bf16),
            pltpu.VMEM(gather.shape, bf16),
        ),
        in_specs=[whole] * 14 + [outside],
        out_specs=(outside,) * 3 + (whole,) * 6,
        input_output_aliases={12: 7, 13: 8},
        scratch_shapes=[
            pltpu.VMEM((particles, width), bf16),
            pltpu.VMEM(edges.shape, bf16),
            kept,
            pltpu.VMEM(kept_shape, jnp.int16),
            kept,
            kept,
            kept,
            kept,
            kept,
            pltpu.VMEM(kept_shape, f32),
            pltpu.VMEM((rows, width), bf16),
            pltpu.VMEM((particles + 8, width), f32),
            pltpu.VMEM((GROUP, width), f32),
            pltpu.VMEM((chunks + GROUP, width), f32),
            pltpu.VMEM((chunks // LANES + 1, width, LANES), f32),
            pltpu.VMEM((width, rows + width), f32),
            pltpu.VMEM((2, width, width), f32),
            pltpu.VMEM((40, width), f32),
            pltpu.VMEM((TILE, width), f32),
            pltpu.VMEM((TILE, width), f32),
            pltpu.VMEM((TILE, width), bf16),
            pltpu.VMEM((TILE, width), bf16),
            pltpu.VMEM((TILE, width), bf16),
            pltpu.VMEM((4, TILE, width), f32),
            pltpu.VMEM((8 * halo, width), bf16),
            pltpu.VMEM((grad_rows, width), f32),
            pltpu.SMEM((8, chunks + LANES), i32),
            pltpu.SemaphoreType.DMA((PIECES,)),
            pltpu.SemaphoreType.DMA((2 * PIECES,)),
            pltpu.SemaphoreType.DMA,
            pltpu.SemaphoreType.DMA,
        ],
        compiler_params=pltpu.CompilerParams(vmem_limit_bytes=52 * 1024 * 1024),
        name="edge_layer",
    )(
        pinned(latents),
        pinned(ring),
        pinned(ring_far),
        pinned(ring_near),
        pinned(upstream),
        pinned(vectors),
        pinned(listing),
        pinned(segment),
        pinned(neighbour_rows),
        pinned(receiver),
        pinned(low),
        pinned(blocks),
        pinned(edges),
        pinned(gather),
        outer(cotangents),
    )[:7]


def update_kernel(
    relayed,
    mine_ref,
    other_ref,
    weights_ref,
    vectors_ref,
    weights_m_ref,
    vectors_m_ref,
    weights_v_ref,
    vectors_v_ref,
    weights_ema_ref,
    vectors_ema_ref,
    norm_ref,
    weights_m_out,
    vectors_m_out,
    weights_v_out,
    vectors_v_out,
    weights_out,
    vectors_out,
    weights_copy_out,
    vectors_copy_out,
    weights_ema_out,
    vectors_ema_out,
    grads,
):
    f32 = jnp.float32
    odd = lax.axis_index("gx") & 1
    half_rows, width = mine_ref.shape
    quarter = half_rows // 4
    squares = jnp.zeros((8, width), f32)
    for side, part_ref in ((odd, mine_ref), (1 - odd, other_ref)):
        for slot in range(4):
            values = part_ref[slot * quarter : (slot + 1) * quarter, :].astype(f32)
            grads[part_rows(relayed, side, slot, quarter), :] = values
            squares = squares + jnp.sum((values * values).reshape(quarter // 8, 8, width), axis=0)
    norm = jnp.sqrt(jnp.sum(jnp.sum(squares, axis=1, keepdims=True), axis=0, keepdims=True))
    norm_ref[...] = norm
    scale = clip_norm / jnp.maximum(norm, clip_norm)
    for block in range(weights_ref.shape[0]):
        for row in range(0, width, UPDATE_ROWS):
            part = slice(row, row + UPDATE_ROWS)
            moment, second, param, average = adamw(
                weights_ref[block, part, :],
                grads[block * width + row : block * width + row + UPDATE_ROWS, :],
                weights_m_ref[block, part, :],
                weights_v_ref[block, part, :],
                weights_ema_ref[block, part, :],
                scale,
                matrix_rate,
            )
            weights_m_out[block, part, :] = moment
            weights_v_out[block, part, :] = second
            weights_out[block, part, :] = param
            weights_copy_out[block, part, :] = param.astype(jnp.bfloat16)
            weights_ema_out[block, part, :] = average
    tail = weights_ref.shape[0] * width
    moment, second, param, average = adamw(
        vectors_ref[...],
        grads[tail : tail + vectors_ref.shape[0], :],
        vectors_m_ref[...],
        vectors_v_ref[...],
        vectors_ema_ref[...],
        scale,
        vector_rate,
    )
    vectors_m_out[...] = moment
    vectors_v_out[...] = second
    vectors_out[...] = param
    vectors_copy_out[...] = param.astype(jnp.bfloat16)
    vectors_ema_out[...] = average


def update_call(relayed, mine, other, weights, vectors, weights_m, vectors_m, weights_v, vectors_v,
                weights_ema, vectors_ema):
    f32, bf16 = jnp.float32, jnp.bfloat16
    mat, vec = weights.shape, vectors.shape
    kinds = (
        ((1, 1), f32), (mat, f32), (vec, f32), (mat, f32), (vec, f32), (mat, f32), (vec, f32),
        (mat, bf16), (vec, bf16), (mat, f32), (vec, f32),
    )
    whole = pl.BlockSpec(memory_space=pltpu.VMEM)
    return pl.pallas_call(
        functools.partial(update_kernel, relayed),
        out_shape=tuple(jax.ShapeDtypeStruct(*kind) for kind in kinds),
        in_specs=[whole] * 10,
        out_specs=(whole,) * 11,
        scratch_shapes=[pltpu.VMEM((2 * mine.shape[0], mine.shape[1]), f32)],
        compiler_params=pltpu.CompilerParams(vmem_limit_bytes=24 * 1024 * 1024),
        name="update",
    )(mine, other, weights, vectors, weights_m, vectors_m, weights_v, vectors_v, weights_ema,
      vectors_ema)


def pair_exchange(to_far, to_near, axis):
    near, far = neighbour_pairs(lax.axis_size(axis))
    return lax.ppermute(to_far, axis, far), lax.ppermute(to_near, axis, near)


def partners(axis, stride, mask):
    return [(i, i ^ (mask * stride)) for i in range(lax.axis_size(axis))]


def even_pick(axis, even, odd):
    return jnp.where(lax.axis_index(axis) % 2 == 0, even, odd)


def swap(values, axis, stride, mask):
    return lax.ppermute(values, axis, partners(axis, stride, mask))


def tree_sum(terms):
    while len(terms) > 1:
        terms = [terms[i] + terms[i + 1] for i in range(0, len(terms), 2)]
    return terms[0]


def first_sum_kernel(quarter, halo, keep_ref, got_ref, own_ref, ahead_ref, across_ref, behind_ref):
    rows = 4 * quarter + 3 * halo
    total = keep_ref[...] + got_ref[0:rows, :].astype(jnp.float32)
    spots = slot_rows(quarter, halo)
    own_ref[...] = total[:quarter]
    ahead_ref[...] = total[quarter : 2 * quarter + 3 * halo].astype(jnp.bfloat16)
    across_ref[...] = total[spots[2] : spots[2] + quarter].astype(jnp.bfloat16)
    behind_ref[...] = total[spots[3] : spots[3] + quarter].astype(jnp.bfloat16)


def second_sum_kernel(
    quarter,
    halo,
    own_ref,
    from_behind_ref,
    from_across_ref,
    from_ahead_ref,
    got_ref,
    halo_own_ref,
    mine_ref,
    along1_ref,
    along3_ref,
    middle_ref,
):
    f32, bf16 = jnp.float32, jnp.bfloat16
    index, odd_y = lax.axis_index("gx"), lax.axis_index("gy") & 1
    mine = (own_ref[...] + from_behind_ref[0:quarter, :].astype(f32)) + (
        from_across_ref[...].astype(f32) + from_ahead_ref[...].astype(f32)
    )
    mine = mine.astype(bf16)
    mine_ref[...] = mine
    far = from_behind_ref[quarter:, :].astype(f32)
    far = jnp.where((index == 0) | (index == 7), 0.0, far)
    strips = halo_own_ref[...].astype(f32) + got_ref[4 * quarter + 3 * halo :, :].astype(f32) + far
    low, high = strips[:halo].astype(bf16), strips[2 * halo :].astype(bf16)
    middle_ref[...] = strips[halo : 2 * halo]
    along3_ref[0:halo, :] = jnp.where(odd_y == 0, low, high)
    along3_ref[halo:, :] = mine
    along1_ref[0:halo, :] = jnp.where(odd_y == 0, high, low)
    along1_ref[halo:, :] = mine


def in_vmem(kernel, name, shapes, *operands):
    whole = pl.BlockSpec(memory_space=pltpu.VMEM)
    return pl.pallas_call(
        kernel,
        out_shape=tuple(pltpu.VMEM(shape, dtype) for shape, dtype in shapes),
        in_specs=[whole] * len(operands),
        out_specs=(whole,) * len(shapes),
        compiler_params=pltpu.CompilerParams(vmem_limit_bytes=8 * 1024 * 1024),
        name=name,
    )(*[pinned(operand) for operand in operands])


def sum_relayed(send, keep, halo_own, halo):
    f32, bf16 = jnp.float32, jnp.bfloat16
    width = send.shape[1]
    quarter = (send.shape[0] - 6 * halo) // 4
    index, row = lax.axis_index("gx"), lax.axis_index("gy")

    def turned(values, step):
        pairs = [(i, ((i >> 1) + step * (1 - 2 * (i & 1))) % 4 * 2 + (i & 1)) for i in range(8)]
        return lax.ppermute(values, "gx", pairs)

    got = swap(send, "gx", 1, 1)
    own, ahead, across, behind = in_vmem(
        functools.partial(first_sum_kernel, quarter, halo),
        "first_sum",
        (
            ((quarter, width), f32),
            ((quarter + 3 * halo, width), bf16),
            ((quarter, width), bf16),
            ((quarter, width), bf16),
        ),
        keep,
        got,
    )
    from_behind = turned(ahead, 1)
    from_ahead = turned(behind, 3)
    from_across = turned(across, 2)
    mine, to1, to3, middle = in_vmem(
        functools.partial(second_sum_kernel, quarter, halo),
        "second_sum",
        (
            ((quarter, width), bf16),
            ((quarter + halo, width), bf16),
            ((quarter + halo, width), bf16),
            ((halo, width), f32),
        ),
        own,
        from_behind,
        from_across,
        from_ahead,
        got,
        halo_own,
    )
    along3 = swap(to3, "gy", 1, 3)
    along2 = swap(mine, "gy", 1, 2)
    along1 = swap(to1, "gy", 1, 1)
    mine = tree_sum(
        [
            mine.astype(f32),
            along1[halo:].astype(f32),
            along2.astype(f32),
            along3[halo:].astype(f32),
        ]
    ).astype(bf16)
    last_far = jnp.where((row == 0) | (row == 3), bf16(0), along3[:halo])
    part3, part2, part1 = (swap(mine, "gx", 2, mask) for mask in (3, 2, 1))
    onward = ((index >> 1) & 1) == (index & 1)
    mine = jnp.concatenate(
        [mine, jnp.where(onward, part1, part3), part2, jnp.where(onward, part3, part1)]
    )
    return mine, swap(mine, "gx", 1, 1), middle, last_far, along1[:halo]


def sum_staged(send, keep, halo_own, halo):
    f32, bf16 = jnp.float32, jnp.bfloat16
    width = send.shape[1]
    quarter = (send.shape[0] - 6 * halo) // 4
    slots = slot_rows(quarter, halo)

    def joined_slots(values):
        return jnp.concatenate([values[spot : spot + quarter] for spot in slots])

    far = send[2 * quarter : 2 * quarter + 3 * halo]
    near = send[4 * quarter + 3 * halo :]
    back_far, back_near = pair_exchange(far, near, "gx")
    strips = halo_own.astype(f32) + back_far.astype(f32) + back_near.astype(f32)
    low, high = strips[:halo].astype(bf16), strips[2 * halo :].astype(bf16)
    last_far, last_near = pair_exchange(
        even_pick("gy", low, high), even_pick("gy", high, low), "gy"
    )
    index = lax.axis_index("gx")
    got = swap(joined_slots(send), "gx", 1, 1)
    total = (joined_slots(keep) + got.astype(f32)).astype(bf16)
    split = stages(lax.axis_size("gx"))[1:]
    for stride, factor in split:
        part = (index // stride) % factor
        height = total.shape[0] // factor
        mine = lax.dynamic_slice_in_dim(total, part * height, height, 0).astype(f32)
        for mask in range(factor - 1, 0, -1):
            piece = lax.dynamic_slice_in_dim(total, (part ^ mask) * height, height, 0)
            mine = mine + swap(piece, "gx", stride, mask).astype(f32)
        total = mine.astype(bf16)
    total = tree_sum(
        [total.astype(f32)]
        + [swap(total, "gy", 1, mask).astype(f32) for mask in range(1, lax.axis_size("gy"))]
    ).astype(bf16)
    for stride, factor in reversed(split):
        part = (index // stride) % factor
        height = total.shape[0]
        joined = jnp.zeros((factor * height, width), bf16)
        joined = lax.dynamic_update_slice_in_dim(joined, total, part * height, 0)
        for mask in range(factor - 1, 0, -1):
            piece = swap(total, "gx", stride, mask)
            joined = lax.dynamic_update_slice_in_dim(joined, piece, (part ^ mask) * height, 0)
        total = joined
    return total, swap(total, "gx", 1, 1), strips[halo : 2 * halo], last_far, last_near


def per_device(
    node_latents,
    edge_latents,
    node_cotangent,
    edge_cotangent,
    neighbours,
    edge_mask,
    send_table,
    counts,
    weights,
    vectors,
    weights_m,
    vectors_m,
    weights_v,
    vectors_v,
    weights_ema,
    vectors_ema,
):
    f32, bf16 = jnp.float32, jnp.bfloat16
    tok_rows, width = node_latents.shape
    halo = send_table.shape[1]
    boundary_pick = selector(send_table[0], tok_rows, bf16)
    boundary = jnp.dot(boundary_pick, node_latents, preferred_element_type=f32).astype(bf16)
    from_far, from_near = pair_exchange(boundary, boundary, "gx")
    ring = jnp.concatenate([from_far, from_near, boundary], axis=0)
    ring_far, ring_near = pair_exchange(ring, ring, "gy")
    unit = 16 * lax.axis_size("gx")
    grad_rows = -(-(weights.shape[0] * width + vectors.shape[0]) // unit) * unit
    relayed = lax.axis_size("gx") == 8 and lax.axis_size("gy") == 4
    edge_shape = (tok_rows * neighbours.shape[1] // CHUNK, CHUNK, width)
    plan = plan_call(
        halo, counts, neighbours, edge_mask, node_latents, vectors, node_cotangent, weights,
        edge_latents.reshape(edge_shape),
    )
    nodes_out, edges_out, edges_in_grad, node_part, halo_own, send, keep = layer_call(
        halo, relayed, grad_rows, ring, ring_far, ring_near, edge_cotangent.reshape(edge_shape),
        plan,
    )
    sums = sum_relayed if relayed else sum_staged
    mine, other, middle, last_far, last_near = sums(send, keep, halo_own, halo)
    boundary_grad = middle + last_far.astype(f32) + last_near.astype(f32)
    returned = lax.dot_general(
        boundary_pick.astype(f32),
        boundary_grad,
        (((0,), (0,)), ((), ())),
        precision=lax.Precision.HIGHEST,
        preferred_element_type=f32,
    )
    nodes_in_grad = (node_part + returned).astype(bf16)
    updated = update_call(
        relayed, mine, other, weights, vectors, weights_m, vectors_m, weights_v, vectors_v, weights_ema,
        vectors_ema,
    )
    return (
        nodes_out,
        edges_out.reshape(edge_latents.shape),
        nodes_in_grad,
        edges_in_grad.reshape(edge_latents.shape),
        updated[0].reshape(()),
    ) + tuple(updated[1:])


def solution(mesh):
    in_specs = (
        P(("gx", "gy"), None),
        P(("gx", "gy"), None, None),
        P(("gx", "gy"), None),
        P(("gx", "gy"), None, None),
        P(("gx", "gy"), None),
        P(("gx", "gy"), None),
        P(("gx", "gy"), None),
        P(("gx", "gy")),
        P(),
        P(),
        P(),
        P(),
        P(),
        P(),
        P(),
        P(),
    )
    out_specs = (
        P(("gx", "gy"), None),
        P(("gx", "gy"), None, None),
        P(("gx", "gy"), None),
        P(("gx", "gy"), None, None),
        P(),
        P(),
        P(),
        P(),
        P(),
        P(),
        P(),
        P(),
        P(),
        P(),
        P(),
    )
    return jax.shard_map(
        per_device, mesh=mesh, in_specs=in_specs, out_specs=out_specs, check_vma=False
    )
```

```python
import functools

import jax
import jax.numpy as jnp
from jax import lax
from jax.experimental import pallas as pl
from jax.experimental.pallas import tpu as pltpu
from jax.sharding import PartitionSpec as P

STEP = 10


first_decay = 0.5
second_decay = 0.5
adam_epsilon = 1e-08
weight_decay = 0.01
matrix_rate = 0.05
vector_rate = 0.2
average_decay = 0.9
clip_norm = 1.0
norm_epsilon = 1e-05


def neighbour_pairs(count):
    near = [(i, i ^ 1) for i in range(count) if (i ^ 1) < count]
    far = [(i, i + 1) for i in range(1, count - 1, 2)]
    return near, far + [(target, source) for source, target in far]


def stages(count):
    result, stride = [], 1
    while stride < count:
        factor = 2 if stride == 1 else min(4, count // stride)
        result.append((stride, factor))
        stride *= factor
    return result


def selector(indices, width, dtype):
    columns = lax.broadcasted_iota(jnp.int32, (indices.shape[0], width), 1)
    return (indices[:, None] == columns).astype(dtype)


def adamw(param, grad, moment, second, average, scale, rate):
    clipped = grad * scale
    moment_new = first_decay * moment + (1.0 - first_decay) * clipped
    second_new = second_decay * second + (1.0 - second_decay) * clipped * clipped
    corrected = moment_new / (1.0 - first_decay**STEP)
    denom = jnp.sqrt(second_new / (1.0 - second_decay**STEP)) + adam_epsilon
    param_new = param - rate * (corrected / denom + weight_decay * param)
    average_new = average_decay * average + (1.0 - average_decay) * param_new
    return (moment_new, second_new, param_new, average_new)


CHUNK = 16
GROUP = 32
UPDATE_ROWS = 32
TILE = CHUNK * GROUP
LANES = 128
PIECES = 8


def dot(left, right):
    return jnp.dot(left, right, preferred_element_type=jnp.float32)


def dot_nt(left, right):
    return lax.dot_general(
        left, right, (((1,), (1,)), ((), ())), preferred_element_type=jnp.float32
    )


def dot_tn(left, right):
    return lax.dot_general(
        left, right, (((0,), (0,)), ((), ())), preferred_element_type=jnp.float32
    )


def split_pair(values, axis=1):
    high = values.astype(jnp.bfloat16)
    low = (values - high.astype(jnp.float32)).astype(jnp.bfloat16)
    return jnp.concatenate([high, low], axis=axis)


def halves(pair):
    width = pair.shape[1] // 2
    return pair[:, :width] + pair[:, width:]


def silu_of_half(half):
    turn = jnp.tanh(half)
    lift = 1.0 + turn
    act = half * lift
    return act, lift + act * (1.0 - turn)


def row_sum(values):
    return jnp.sum(values, axis=-1, keepdims=True)


def scaled_unit(values, width):
    center = values - row_sum(values) * (1.0 / width)
    inverse = lax.rsqrt(row_sum(center * center) + width * norm_epsilon)
    return center * inverse, inverse


def scaled_unit_back(scaled, unit, inverse, width):
    shift = row_sum(scaled) * (1.0 / width)
    return inverse * (scaled - shift - unit * row_sum(scaled * unit))


def column_total(values):
    return jnp.sum(values, axis=0, keepdims=True)


def iota(shape, dim):
    return lax.broadcasted_iota(jnp.int32, shape, dim)


def slot_rows(quarter, halo):
    return (0, quarter, 2 * quarter + 3 * halo, 3 * quarter + 3 * halo)


def part_rows(relayed, side, slot, quarter):
    chip = lax.axis_index("gx") >> 1
    part = (chip + slot * (1 - 2 * side)) & 3 if relayed else slot
    return pl.ds(pl.multiple_of((side * 4 + part) * quarter, 16), quarter)


def plan_kernel(
    halo,
    count_ref,
    mask_hbm,
    neighbour_hbm,
    latents_hbm,
    vectors_hbm,
    upstream_hbm,
    weights_hbm,
    edges_hbm,
    latents_ref,
    vectors_ref,
    upstream_ref,
    edges_buf,
    list_rows,
    segment_ref,
    neighbour_rows,
    receiver_ref,
    low_ref,
    gather_ref,
    blocks_ref,
    mask_ref,
    neighbour_ref,
    weights_ref,
    sems,
):
    f32, bf16, i32 = jnp.float32, jnp.bfloat16, jnp.int32
    slots, particles = neighbour_ref.shape
    per = slots // CHUNK
    chunks = particles * per
    width = latents_ref.shape[1]
    rows = particles + 8 * halo
    fetches = [
        pltpu.make_async_copy(source, target, sems.at[order])
        for order, (source, target) in enumerate(
            (
                (mask_hbm, mask_ref),
                (neighbour_hbm, neighbour_ref),
                (latents_hbm, latents_ref),
                (vectors_hbm, vectors_ref),
                (weights_hbm, weights_ref),
                (upstream_hbm, upstream_ref),
            )
        )
    ]
    for copy in fetches:
        copy.start()
    piece = chunks // PIECES
    loads = [
        pltpu.make_async_copy(
            edges_hbm.at[pl.ds(p * piece, piece)],
            edges_buf.at[pl.ds(p * piece, piece)],
            sems.at[len(fetches) + p],
        )
        for p in range(PIECES)
    ]
    for copy in loads:
        copy.start()
    edges_buf[chunks] = jnp.zeros((CHUNK, width), bf16)
    fetches[0].wait()

    mask = mask_ref[...].astype(f32)
    degree = jnp.sum(mask, axis=0, keepdims=True)
    taken = ((degree.astype(i32) + (CHUNK - 1)) >> 4).astype(f32)
    earlier = iota((particles, particles), 0) < iota((particles, particles), 1)
    begin = dot(jnp.broadcast_to(taken, (16, particles)).astype(bf16), earlier.astype(bf16))
    degree_col = dot_tn(mask.astype(bf16), jnp.ones((slots, width), bf16))
    taken_col = ((degree_col.astype(i32) + (CHUNK - 1)) >> 4).astype(f32)
    later = iota((particles, particles), 1) < iota((particles, particles), 0)
    begin_col = dot(later.astype(bf16), taken_col.astype(bf16))
    end_col = begin_col + taken_col
    for block in range(chunks // width):
        lane = iota((particles, width), 1).astype(f32) + block * width
        segment_ref[:, block * width : (block + 1) * width] = (
            (lane >= begin_col) & (lane < end_col)
        ).astype(bf16)
    total = row_sum(taken)
    who = iota((16, particles), 1).astype(f32)
    offset = per * who - begin
    coarse = jnp.floor(offset * 0.125) * 8.0
    line = iota((16, particles), 0)
    facts = jnp.where(
        line == 0,
        who,
        jnp.where(line == 1, coarse, jnp.where(line == 2, offset - coarse, degree)),
    )
    listing = dot(facts.astype(bf16), segment_ref[...])
    place = iota((1, chunks), 1).astype(f32)
    particle = listing[0:1, :]
    chunk = listing[1:2, :] + listing[2:3, :] + place
    rest = listing[3:4, :] - CHUNK * (chunk - per * particle)
    used = place < total
    list_rows[...] = jnp.zeros(list_rows.shape, i32)
    list_rows[0:1, 0:chunks] = jnp.where(used, chunk, float(chunks)).astype(i32)
    list_rows[0:1, chunks:] = jnp.full((1, list_rows.shape[1] - chunks), chunks, i32)
    list_rows[1:2, 0:chunks] = jnp.where(used, particle, float(particles)).astype(i32)
    list_rows[1:2, chunks:] = jnp.full((1, list_rows.shape[1] - chunks), particles, i32)
    list_rows[2:3, 0:chunks] = jnp.where(used, rest, 0.0).astype(i32)
    list_rows[3:4, 0:particles] = jnp.broadcast_to(total, (1, particles)).astype(i32)
    list_rows[4:5, 0:particles] = (begin[0:1, :] + taken).astype(i32)
    list_rows[5:6, 0:particles] = jnp.full((1, particles), count_ref[0], i32)

    fetches[1].wait()
    neighbour = neighbour_ref[...]
    neighbour = jnp.where(neighbour >= particles + 5 * halo, neighbour - halo, neighbour)
    neighbour_rows[...] = jnp.zeros(neighbour_rows.shape, f32)
    neighbour_rows[0:particles, 0:slots] = neighbour.astype(f32).T

    block_of = iota((TILE, LANES), 0) >> 4
    for quarter in range(LANES // GROUP):
        blocks_ref[quarter] = (iota((TILE, LANES), 1) == block_of + quarter * GROUP).astype(bf16)

    for copy in fetches[2:]:
        copy.wait()
    for block in range(weights_ref.shape[0]):
        low_ref[block] = weights_ref[block].astype(bf16)
    for extra, block in ((9, 3), (10, 4)):
        low_ref[extra] = (0.5 * low_ref[block].astype(f32)).astype(bf16)
    latents = latents_ref[...]
    gather_ref[0:particles, :] = split_pair(0.5 * dot(latents, low_ref[2]))
    gather_ref[particles:rows, :] = jnp.zeros((rows - particles, 2 * width), bf16)
    gather_ref[rows : rows + width, :] = jnp.concatenate(
        [(0.5 * low_ref[0].astype(f32)).astype(bf16), jnp.zeros((width, width), bf16)], axis=1
    )
    gather_ref[rows + width :, :] = jnp.zeros((LANES, 2 * width), bf16)
    receiver_ref[0:particles, :] = 0.5 * (dot(latents, low_ref[1]) + vectors_ref[0:1, :])
    receiver_ref[particles:, :] = jnp.zeros((receiver_ref.shape[0] - particles, width), f32)
    for copy in loads:
        copy.wait()


def layer_kernel(
    halo,
    relayed,
    latents_ref,
    ring_ref,
    ring_far_ref,
    ring_near_ref,
    upstream_ref,
    vectors_ref,
    list_rows,
    segment_ref,
    neighbour_rows,
    receiver_ref,
    low_ref,
    blocks_ref,
    edges_in,
    gather_in,
    cotangent_hbm,
    nodes_out_hbm,
    edges_out_hbm,
    edges_grad_hbm,
    node_part_ref,
    halo_own_ref,
    send_ref,
    keep_ref,
    edges_buf,
    gather_ref,
    nodes_out_ref,
    cotangent_buf,
    kept_edges,
    kept_index,
    kept_act1,
    kept_act2,
    kept_slope1,
    kept_slope2,
    kept_unit,
    kept_inverse,
    table_ref,
    descent_ref,
    receiver_tile,
    chunk_sums,
    chunk_grads,
    segment_acc,
    index_acc,
    mat_acc,
    vec_acc,
    first_tile,
    last_tile,
    third_tile,
    first_back,
    second_back,
    passed_tile,
    halo_grad,
    grads,
    listed,
    in_sems,
    out_sems,
    list_sem,
    nodes_sem,
):
    f32, bf16, i32 = jnp.float32, jnp.bfloat16, jnp.int32
    fetch_list = pltpu.make_async_copy(list_rows, listed, list_sem)
    fetch_list.start()
    particles, chunks = segment_ref.shape
    per = chunks // particles
    width = latents_ref.shape[1]
    rows = table_ref.shape[0]
    piece = chunks // PIECES
    root = float(width) ** 0.5
    odd_x = lax.axis_index("gx") & 1
    odd_y = lax.axis_index("gy") & 1
    loads = [
        pltpu.make_async_copy(
            cotangent_hbm.at[pl.ds(p * piece, piece)],
            cotangent_buf.at[pl.ds(p * piece, piece)],
            in_sems.at[p],
        )
        for p in range(PIECES)
    ]
    for copy in loads:
        copy.start()
    cotangent_buf[chunks] = jnp.zeros((CHUNK, width), bf16)

    table_ref[0:particles, :] = latents_ref[...]
    far, near, own = ring_far_ref[...], ring_near_ref[...], ring_ref[...]
    low_y = jnp.where(odd_y == 0, far, near)
    high_y = jnp.where(odd_y == 0, near, far)
    spot = particles
    for a in range(3):
        for b, strip in enumerate((low_y, own, high_y)):
            if a == 1 and b == 1:
                continue
            if a == 1:
                part = strip[2 * halo :]
            elif a == 0:
                part = jnp.where(odd_x == 0, strip[0:halo], strip[halo : 2 * halo])
            else:
                part = jnp.where(odd_x == 0, strip[halo : 2 * halo], strip[0:halo])
            table_ref[spot : spot + halo, :] = part
            spot += halo

    vectors = vectors_ref[...]

    def vector(row):
        return vectors[row : row + 1, :]

    latents = latents_ref[...]
    half3, half4 = low_ref[9], low_ref[10]
    gather_ref[particles:rows, :] = split_pair(0.5 * dot(table_ref[particles:, :], low_ref[2]))
    chunk_sums[...] = jnp.zeros(chunk_sums.shape, f32)
    chunk_grads[...] = jnp.zeros(chunk_grads.shape, f32)
    index_acc[...] = jnp.zeros(index_acc.shape, f32)
    mat_acc[...] = jnp.zeros(mat_acc.shape, f32)
    vec_acc[...] = jnp.zeros(vec_acc.shape, f32)
    tail = 9 * width
    grads[tail:, :] = jnp.zeros((grads.shape[0] - tail, width), f32)
    descent_ref[particles:, :] = jnp.zeros((descent_ref.shape[0] - particles, width), f32)

    fetch_list.wait()
    tiles = (listed[3, 0] + (GROUP - 1)) >> 5

    sublane = iota((CHUNK, width), 0)
    diagonal = iota((CHUNK, width), 1) - sublane
    lane16 = iota((TILE, width), 1).astype(jnp.int16)

    def flat(ref, t):
        return ref[pl.ds(t * GROUP, GROUP)].reshape(TILE, width)

    def keep(ref, t, values):
        ref[pl.ds(t * GROUP, GROUP)] = values.astype(ref.dtype).reshape(GROUP, CHUNK, width)

    def span(j):
        return slice(j * CHUNK, (j + 1) * CHUNK)

    def one_hot(t):
        index = flat(kept_index, t)
        return [
            jnp.where(index == lane16 + jnp.int16(b * width), bf16(1), bf16(0))
            for b in range(rows // width)
        ]

    def gather(t):
        base = t * GROUP
        for j in range(GROUP):
            chunk, particle = listed[0, base + j], listed[1, base + j]
            kept_edges[base + j] = edges_buf[chunk]
            row = jnp.broadcast_to(neighbour_rows[pl.ds(particle, 1), :], (CHUNK, width))
            start = (chunk & (per - 1)) * CHUNK
            index = row_sum(jnp.where(diagonal == start, row, 0.0))
            kept_index[base + j] = (
                jnp.broadcast_to(index, (CHUNK, width)).astype(i32).astype(jnp.int16)
            )
            receiver_tile[j : j + 1, :] = receiver_ref[pl.ds(particle, 1), :]
        gather_ref[rows + width : rows + width + GROUP, :] = split_pair(receiver_tile[...])

    def project(t):
        picks = jnp.concatenate(one_hot(t) + [flat(kept_edges, t), blocks_ref[0]], axis=1)
        first_tile[...] = halves(dot(picks, gather_ref[...]))

    gain_root = vector(3) * root

    def finish(t):
        base = t * GROUP
        unit, inverse = scaled_unit(last_tile[...], width)
        keep(kept_unit, t, unit)
        keep(kept_inverse, t, jnp.broadcast_to(inverse, (TILE, width)))
        change = unit * gain_root + vector(4)
        for j in range(GROUP):
            chunk = listed[0, base + j]
            alive = sublane < listed[2, base + j]
            fresh = kept_edges[base + j].astype(f32) + jnp.where(alive, change[span(j)], 0.0)
            edges_buf[chunk] = fresh.astype(bf16)
            chunk_sums[pl.ds(base + j, 1), :] = column_total(jnp.where(alive, fresh, 0.0))

    def forward(t, carry):
        gather(t + 1)
        act, slope = silu_of_half(first_tile[...])
        act = act.astype(bf16)
        keep(kept_act1, t, act)
        keep(kept_slope1, t, slope)
        finish(jnp.where(t == 0, tiles, t - 1))
        act, slope = silu_of_half(dot(act, half3) + 0.5 * vector(1))
        act = act.astype(bf16)
        keep(kept_act2, t, act)
        keep(kept_slope2, t, slope)
        project(t + 1)
        last_tile[...] = dot(act, low_ref[4]) + vector(2)
        return carry

    for ref in (kept_act1, kept_edges):
        keep(ref, tiles, jnp.zeros((TILE, width), f32))
    last_tile[...] = jnp.zeros(last_tile.shape, f32)
    gather(0)
    project(0)
    lax.fori_loop(0, tiles, forward, 0)
    finish(jnp.where(tiles == 0, tiles, tiles - 1))

    stores = [
        pltpu.make_async_copy(
            edges_buf.at[pl.ds(p * piece, piece)],
            edges_out_hbm.at[pl.ds(p * piece, piece)],
            out_sems.at[p],
        )
        for p in range(PIECES)
    ]
    for copy in stores:
        copy.start()

    def segment_sum(part):
        half, most = chunks // 2, 3 * chunks // 4
        segment_acc[...] = part(0, half)
        for low, high in ((half, most), (most, chunks)):

            @pl.when(listed[3, 0] > low)
            def _():
                segment_acc[...] += part(low, high)

        return halves(segment_acc[...])

    def forward_part(low, high):
        return dot(segment_ref[:, low:high], split_pair(chunk_sums[low:high, :]))

    aggregate = segment_sum(forward_part).astype(bf16)
    half1 = 0.5 * (dot(latents, low_ref[5]) + dot(aggregate, low_ref[6]) + vector(5))
    act1, slope1 = silu_of_half(half1)
    act1 = act1.astype(bf16)
    act2, slope2 = silu_of_half(0.5 * (dot(act1, low_ref[7]) + vector(6)))
    act2 = act2.astype(bf16)
    unit, inverse = scaled_unit(dot(act2, low_ref[8]) + vector(7), width)
    alive = (iota((particles, width), 0) < listed[5, 0]).astype(f32)
    upstream = upstream_ref[...].astype(f32)
    nodes_out_ref[...] = (
        latents.astype(f32) + alive * (unit * (vector(8) * root) + vector(9))
    ).astype(bf16)
    send_nodes = pltpu.make_async_copy(nodes_out_ref, nodes_out_hbm, nodes_sem)
    send_nodes.start()
    held = alive * upstream
    third = scaled_unit_back(held * (vector(8) * root), unit, inverse, width).astype(bf16)
    second = (0.5 * slope2 * dot_nt(third, low_ref[8])).astype(bf16)
    first = (0.5 * slope1 * dot_nt(second, low_ref[7])).astype(bf16)
    descent_ref[0:particles, :] = dot_nt(first, low_ref[6])
    node_part_ref[...] = upstream + dot_nt(first, low_ref[5])

    def put_block(block, values):
        grads[block * width : (block + 1) * width, :] = values

    put_block(5, dot_tn(latents, first))
    put_block(6, dot_tn(aggregate, first))
    put_block(7, dot_tn(act1, second))
    put_block(8, dot_tn(act2, third))
    for row, values in enumerate(
        (first.astype(f32), second.astype(f32), third.astype(f32), held * unit * root, held)
    ):
        grads[tail + 5 + row : tail + 6 + row, :] = column_total(values)

    for copy in loads:
        copy.wait()

    def add_columns(row, values):
        vec_acc[8 * row : 8 * row + 8, :] += jnp.sum(values.reshape(TILE // 8, 8, width), axis=0)

    def accept(t):
        base = t * GROUP
        parts = []
        for j in range(GROUP):
            chunk, particle = listed[0, base + j], listed[1, base + j]
            alive = sublane < listed[2, base + j]
            passed = cotangent_buf[chunk].astype(f32) + jnp.where(
                alive, descent_ref[pl.ds(particle, 1), :], 0.0
            )
            passed_tile[t & 3, span(j), :] = passed
            parts.append(jnp.where(alive, passed, 0.0))
        return jnp.concatenate(parts, axis=0)

    def descend(t, held):
        unit = flat(kept_unit, t).astype(f32)
        third = scaled_unit_back(held * gain_root, unit, flat(kept_inverse, t), width)
        third_tile[...] = third.astype(bf16)
        add_columns(2, third)
        add_columns(3, held * unit)
        add_columns(4, held)

    def settle(t, slot):
        base = t * GROUP
        first = first_back[...]
        result = passed_tile[slot] + dot_nt(first, low_ref[0])
        for j in range(GROUP):
            cotangent_buf[listed[0, base + j]] = result[span(j)].astype(bf16)
        picks = jnp.concatenate(one_hot(t) + [flat(kept_edges, t), blocks_ref[t & 3]], axis=1)
        index_acc[...] += dot_tn(first, picks[:, 0 : rows + width])
        chunk_grads[t >> 2] += dot_tn(first, picks[:, rows + width :])
        mat_acc[0] += dot_tn(flat(kept_act1, t), second_back[...])

    def backward(t, carry):
        third = third_tile[...]
        second = dot_nt(third, half4)
        held = accept(t + 1)
        settle(jnp.where(t == 0, tiles, t - 1), (t + 3) & 3)
        second = flat(kept_slope2, t).astype(f32) * second
        add_columns(1, second)
        second = second.astype(bf16)
        descend(t + 1, held)
        first = flat(kept_slope1, t).astype(f32) * dot_nt(second, half3)
        mat_acc[1] += dot_tn(flat(kept_act2, t), third)
        first_back[...] = first.astype(bf16)
        second_back[...] = second
        return carry

    first_back[...] = jnp.zeros(first_back.shape, bf16)
    second_back[...] = jnp.zeros(second_back.shape, bf16)
    passed_tile[3] = jnp.zeros((TILE, width), f32)
    descend(0, accept(0))
    def send_piece(p):
        pltpu.make_async_copy(
            cotangent_buf.at[pl.ds(p * piece, piece)],
            edges_grad_hbm.at[pl.ds(p * piece, piece)],
            out_sems.at[PIECES + p],
        ).start()

    def last_tile(p):
        return (listed[4, (p + 1) * (piece // per) - 1] + (GROUP - 1)) >> 5

    def has_live(p):
        before = listed[4, jnp.maximum(p * (piece // per) - 1, 0)]
        return jnp.where(p == 0, 0, before) < listed[3, 0]

    @pl.loop(0, PIECES)
    def _(p):
        @pl.when(jnp.logical_not(has_live(p)))
        def _():
            send_piece(p)

    def backward_piece(p, t):
        upto = last_tile(p) + 1
        stop = jnp.minimum(upto, tiles)
        lax.fori_loop(t, stop, backward, 0)

        @pl.when((upto <= tiles) & has_live(p))
        def _():
            send_piece(p)

        return jnp.maximum(t, stop)

    lax.fori_loop(0, PIECES, backward_piece, jnp.int32(0))
    settle(jnp.where(tiles == 0, tiles, tiles - 1), (tiles + 3) & 3)

    @pl.loop(0, PIECES)
    def _(p):
        @pl.when((last_tile(p) + 1 > tiles) & has_live(p))
        def _():
            send_piece(p)

    def backward_part(low, high):
        groups = [chunk_grads[g] for g in range(low // LANES, high // LANES)]
        return dot_nt(segment_ref[:, low:high], split_pair(jnp.concatenate(groups, axis=1), axis=0))

    receiver_grad = segment_sum(backward_part)
    grads[tail : tail + 1, :] = column_total(receiver_grad)
    receiver_grad = receiver_grad.astype(bf16)
    for row in range(1, 5):
        values = column_total(vec_acc[8 * row : 8 * row + 8, :])
        grads[tail + row : tail + row + 1, :] = values * root if row == 3 else values
    sent = index_acc[:, 0:rows].astype(bf16)
    put_block(0, index_acc[:, rows:].T)
    put_block(1, dot_tn(latents, receiver_grad))
    put_block(2, dot(sent, table_ref[...]).T)
    put_block(3, mat_acc[0])
    put_block(4, mat_acc[1])
    table_grad = lax.dot_general(
        sent, low_ref[2], (((0,), (1,)), ((), ())), preferred_element_type=f32
    )
    node_part_ref[...] += dot_nt(receiver_grad, low_ref[1]) + table_grad[0:particles, :]
    halo_grad[...] = table_grad[particles:, :].astype(bf16)
    low_x = halo_grad[0 : 3 * halo, :]
    high_x = halo_grad[5 * halo : 8 * halo, :]
    halo_own_ref[0:halo, :] = halo_grad[3 * halo : 4 * halo, :]
    halo_own_ref[halo : 2 * halo, :] = jnp.zeros((halo, width), bf16)
    halo_own_ref[2 * halo :, :] = halo_grad[4 * halo : 5 * halo, :]
    quarter = grads.shape[0] // 8
    relay = 2 * quarter
    send_ref[relay : relay + 3 * halo, :] = jnp.where(odd_x == 0, low_x, high_x)
    send_ref[4 * quarter + 3 * halo :, :] = jnp.where(odd_x == 0, high_x, low_x)
    keep_ref[relay : relay + 3 * halo, :] = jnp.zeros((3 * halo, width), f32)
    for slot, spot in enumerate(slot_rows(quarter, halo)):
        kept_rows = part_rows(relayed, odd_x, slot, quarter)
        sent_rows = part_rows(relayed, 1 - odd_x, slot, quarter)
        keep_ref[spot : spot + quarter, :] = grads[kept_rows, :]
        send_ref[spot : spot + quarter, :] = grads[sent_rows, :].astype(bf16)

    for copy in stores + [send_nodes]:
        copy.wait()
    for p in range(PIECES):
        pltpu.make_async_copy(
            cotangent_buf.at[pl.ds(p * piece, piece)],
            edges_grad_hbm.at[pl.ds(p * piece, piece)],
            out_sems.at[PIECES + p],
        ).wait()


def pinned(values):
    return pltpu.with_memory_space_constraint(values, pltpu.VMEM)


def outer(values):
    return pltpu.with_memory_space_constraint(values, pltpu.HBM)


def plan_call(halo, counts, neighbours, edge_mask, latents, vectors, upstream, weights, edges):
    f32, bf16, i32 = jnp.float32, jnp.bfloat16, jnp.int32
    particles, slots = neighbours.shape
    width = latents.shape[1]
    chunks = particles * slots // CHUNK
    whole = pl.BlockSpec(memory_space=pltpu.VMEM)
    outside = pl.BlockSpec(memory_space=pl.ANY)
    return pl.pallas_call(
        functools.partial(plan_kernel, halo),
        out_shape=(
            pltpu.VMEM(latents.shape, bf16),
            pltpu.VMEM(vectors.shape, f32),
            pltpu.VMEM(upstream.shape, bf16),
            pltpu.VMEM((chunks + 1, CHUNK, width), bf16),
            pltpu.VMEM((8, chunks + LANES), i32),
            pltpu.VMEM((particles, chunks), bf16),
            pltpu.VMEM((particles + 8, width), f32),
            pltpu.VMEM((particles + 8, width), f32),
            pltpu.VMEM((weights.shape[0] + 2, width, width), bf16),
            pltpu.VMEM((particles + 8 * halo + width + LANES, 2 * width), bf16),
            pltpu.VMEM((LANES // GROUP, TILE, LANES), bf16),
        ),
        in_specs=[pl.BlockSpec(memory_space=pltpu.SMEM)] + [outside] * 7,
        out_specs=(whole,) * 11,
        scratch_shapes=[
            pltpu.VMEM((slots, particles), i32),
            pltpu.VMEM((slots, particles), i32),
            pltpu.VMEM(weights.shape, f32),
            pltpu.SemaphoreType.DMA((6 + PIECES,)),
        ],
        compiler_params=pltpu.CompilerParams(vmem_limit_bytes=16 * 1024 * 1024),
        cost_estimate=pl.CostEstimate(
            flops=10**9, bytes_accessed=12 * 10**6, transcendentals=0
        ),
        name="plan",
    )(
        counts,
        outer(edge_mask.T),
        outer(neighbours.T),
        outer(latents),
        outer(vectors),
        outer(upstream),
        outer(weights),
        outer(edges),
    )


def layer_call(halo, relayed, grad_rows, ring, ring_far, ring_near, cotangents, plan):
    f32, bf16, i32 = jnp.float32, jnp.bfloat16, jnp.int32
    latents, vectors, upstream, edges, listing, segment, *more, gather, blocks = plan
    neighbour_rows, receiver, low = more
    particles, chunks = segment.shape
    width = latents.shape[1]
    rows = particles + 8 * halo
    whole = pl.BlockSpec(memory_space=pltpu.VMEM)
    outside = pl.BlockSpec(memory_space=pl.ANY)
    edge_shape = (chunks, CHUNK, width)
    kept_shape = (chunks + GROUP, CHUNK, width)
    kept = pltpu.VMEM(kept_shape, bf16)
    half = grad_rows // 2
    return pl.pallas_call(
        functools.partial(layer_kernel, halo, relayed),
        out_shape=(
            jax.ShapeDtypeStruct((particles, width), bf16),
            jax.ShapeDtypeStruct(edge_shape, bf16),
            jax.ShapeDtypeStruct(edge_shape, bf16),
            pltpu.VMEM((particles, width), f32),
            pltpu.VMEM((3 * halo, width), bf16),
            pltpu.VMEM((half + 6 * halo, width), bf16),
            pltpu.VMEM((half + 3 * halo, width), f32),
            pltpu.VMEM(edges.shape, bf16),
            pltpu.VMEM(gather.shape, bf16),
        ),
        in_specs=[whole] * 14 + [outside],
        out_specs=(outside,) * 3 + (whole,) * 6,
        input_output_aliases={12: 7, 13: 8},
        scratch_shapes=[
            pltpu.VMEM((particles, width), bf16),
            pltpu.VMEM(edges.shape, bf16),
            kept,
            pltpu.VMEM(kept_shape, jnp.int16),
            kept,
            kept,
            kept,
            kept,
            kept,
            pltpu.VMEM(kept_shape, f32),
            pltpu.VMEM((rows, width), bf16),
            pltpu.VMEM((particles + 8, width), f32),
            pltpu.VMEM((GROUP, width), f32),
            pltpu.VMEM((chunks + GROUP, width), f32),
            pltpu.VMEM((chunks // LANES + 1, width, LANES), f32),
            pltpu.VMEM((particles, 2 * width), f32),
            pltpu.VMEM((width, rows + width), f32),
            pltpu.VMEM((2, width, width), f32),
            pltpu.VMEM((40, width), f32),
            pltpu.VMEM((TILE, width), f32),
            pltpu.VMEM((TILE, width), f32),
            pltpu.VMEM((TILE, width), bf16),
            pltpu.VMEM((TILE, width), bf16),
            pltpu.VMEM((TILE, width), bf16),
            pltpu.VMEM((4, TILE, width), f32),
            pltpu.VMEM((8 * halo, width), bf16),
            pltpu.VMEM((grad_rows, width), f32),
            pltpu.SMEM((8, chunks + LANES), i32),
            pltpu.SemaphoreType.DMA((PIECES,)),
            pltpu.SemaphoreType.DMA((2 * PIECES,)),
            pltpu.SemaphoreType.DMA,
            pltpu.SemaphoreType.DMA,
        ],
        compiler_params=pltpu.CompilerParams(vmem_limit_bytes=52 * 1024 * 1024),
        name="edge_layer",
    )(
        pinned(latents),
        pinned(ring),
        pinned(ring_far),
        pinned(ring_near),
        pinned(upstream),
        pinned(vectors),
        pinned(listing),
        pinned(segment),
        pinned(neighbour_rows),
        pinned(receiver),
        pinned(low),
        pinned(blocks),
        pinned(edges),
        pinned(gather),
        outer(cotangents),
    )[:7]


def update_kernel(
    relayed,
    mine_ref,
    other_ref,
    weights_ref,
    vectors_ref,
    weights_m_ref,
    vectors_m_ref,
    weights_v_ref,
    vectors_v_ref,
    weights_ema_ref,
    vectors_ema_ref,
    norm_ref,
    weights_m_out,
    vectors_m_out,
    weights_v_out,
    vectors_v_out,
    weights_out,
    vectors_out,
    weights_copy_out,
    vectors_copy_out,
    weights_ema_out,
    vectors_ema_out,
    grads,
):
    f32 = jnp.float32
    odd = lax.axis_index("gx") & 1
    half_rows, width = mine_ref.shape
    quarter = half_rows // 4
    squares = jnp.zeros((8, width), f32)
    for side, part_ref in ((odd, mine_ref), (1 - odd, other_ref)):
        for slot in range(4):
            values = part_ref[slot * quarter : (slot + 1) * quarter, :].astype(f32)
            grads[part_rows(relayed, side, slot, quarter), :] = values
            squares = squares + jnp.sum((values * values).reshape(quarter // 8, 8, width), axis=0)
    norm = jnp.sqrt(jnp.sum(jnp.sum(squares, axis=1, keepdims=True), axis=0, keepdims=True))
    norm_ref[...] = norm
    scale = clip_norm / jnp.maximum(norm, clip_norm)
    for block in range(weights_ref.shape[0]):
        for row in range(0, width, UPDATE_ROWS):
            part = slice(row, row + UPDATE_ROWS)
            moment, second, param, average = adamw(
                weights_ref[block, part, :],
                grads[block * width + row : block * width + row + UPDATE_ROWS, :],
                weights_m_ref[block, part, :],
                weights_v_ref[block, part, :],
                weights_ema_ref[block, part, :],
                scale,
                matrix_rate,
            )
            weights_m_out[block, part, :] = moment
            weights_v_out[block, part, :] = second
            weights_out[block, part, :] = param
            weights_copy_out[block, part, :] = param.astype(jnp.bfloat16)
            weights_ema_out[block, part, :] = average
    tail = weights_ref.shape[0] * width
    moment, second, param, average = adamw(
        vectors_ref[...],
        grads[tail : tail + vectors_ref.shape[0], :],
        vectors_m_ref[...],
        vectors_v_ref[...],
        vectors_ema_ref[...],
        scale,
        vector_rate,
    )
    vectors_m_out[...] = moment
    vectors_v_out[...] = second
    vectors_out[...] = param
    vectors_copy_out[...] = param.astype(jnp.bfloat16)
    vectors_ema_out[...] = average


def update_call(relayed, mine, other, weights, vectors, weights_m, vectors_m, weights_v, vectors_v,
                weights_ema, vectors_ema):
    f32, bf16 = jnp.float32, jnp.bfloat16
    mat, vec = weights.shape, vectors.shape
    kinds = (
        ((1, 1), f32), (mat, f32), (vec, f32), (mat, f32), (vec, f32), (mat, f32), (vec, f32),
        (mat, bf16), (vec, bf16), (mat, f32), (vec, f32),
    )
    whole = pl.BlockSpec(memory_space=pltpu.VMEM)
    return pl.pallas_call(
        functools.partial(update_kernel, relayed),
        out_shape=tuple(jax.ShapeDtypeStruct(*kind) for kind in kinds),
        in_specs=[whole] * 10,
        out_specs=(whole,) * 11,
        scratch_shapes=[pltpu.VMEM((2 * mine.shape[0], mine.shape[1]), f32)],
        compiler_params=pltpu.CompilerParams(vmem_limit_bytes=24 * 1024 * 1024),
        name="update",
    )(mine, other, weights, vectors, weights_m, vectors_m, weights_v, vectors_v, weights_ema,
      vectors_ema)


def pair_exchange(to_far, to_near, axis):
    near, far = neighbour_pairs(lax.axis_size(axis))
    return lax.ppermute(to_far, axis, far), lax.ppermute(to_near, axis, near)


def partners(axis, stride, mask):
    return [(i, i ^ (mask * stride)) for i in range(lax.axis_size(axis))]


def even_pick(axis, even, odd):
    return jnp.where(lax.axis_index(axis) % 2 == 0, even, odd)


def swap(values, axis, stride, mask):
    return lax.ppermute(values, axis, partners(axis, stride, mask))


def tree_sum(terms):
    while len(terms) > 1:
        terms = [terms[i] + terms[i + 1] for i in range(0, len(terms), 2)]
    return terms[0]


def first_sum_kernel(quarter, halo, keep_ref, got_ref, own_ref, ahead_ref, across_ref, behind_ref):
    rows = 4 * quarter + 3 * halo
    total = keep_ref[...] + got_ref[0:rows, :].astype(jnp.float32)
    spots = slot_rows(quarter, halo)
    own_ref[...] = total[:quarter]
    ahead_ref[...] = total[quarter : 2 * quarter + 3 * halo].astype(jnp.bfloat16)
    across_ref[...] = total[spots[2] : spots[2] + quarter].astype(jnp.bfloat16)
    behind_ref[...] = total[spots[3] : spots[3] + quarter].astype(jnp.bfloat16)


def second_sum_kernel(
    quarter,
    halo,
    own_ref,
    from_behind_ref,
    from_across_ref,
    from_ahead_ref,
    got_ref,
    halo_own_ref,
    mine_ref,
    along1_ref,
    along3_ref,
    middle_ref,
):
    f32, bf16 = jnp.float32, jnp.bfloat16
    index, odd_y = lax.axis_index("gx"), lax.axis_index("gy") & 1
    mine = (own_ref[...] + from_behind_ref[0:quarter, :].astype(f32)) + (
        from_across_ref[...].astype(f32) + from_ahead_ref[...].astype(f32)
    )
    mine = mine.astype(bf16)
    mine_ref[...] = mine
    far = from_behind_ref[quarter:, :].astype(f32)
    far = jnp.where((index == 0) | (index == 7), 0.0, far)
    strips = halo_own_ref[...].astype(f32) + got_ref[4 * quarter + 3 * halo :, :].astype(f32) + far
    low, high = strips[:halo].astype(bf16), strips[2 * halo :].astype(bf16)
    middle_ref[...] = strips[halo : 2 * halo]
    along3_ref[0:halo, :] = jnp.where(odd_y == 0, low, high)
    along3_ref[halo:, :] = mine
    along1_ref[0:halo, :] = jnp.where(odd_y == 0, high, low)
    along1_ref[halo:, :] = mine


def in_vmem(kernel, name, shapes, *operands):
    whole = pl.BlockSpec(memory_space=pltpu.VMEM)
    return pl.pallas_call(
        kernel,
        out_shape=tuple(pltpu.VMEM(shape, dtype) for shape, dtype in shapes),
        in_specs=[whole] * len(operands),
        out_specs=(whole,) * len(shapes),
        compiler_params=pltpu.CompilerParams(vmem_limit_bytes=8 * 1024 * 1024),
        name=name,
    )(*[pinned(operand) for operand in operands])


def sum_relayed(send, keep, halo_own, halo):
    f32, bf16 = jnp.float32, jnp.bfloat16
    width = send.shape[1]
    quarter = (send.shape[0] - 6 * halo) // 4
    index, row = lax.axis_index("gx"), lax.axis_index("gy")

    def turned(values, step):
        pairs = [(i, ((i >> 1) + step * (1 - 2 * (i & 1))) % 4 * 2 + (i & 1)) for i in range(8)]
        return lax.ppermute(values, "gx", pairs)

    got = swap(send, "gx", 1, 1)
    own, ahead, across, behind = in_vmem(
        functools.partial(first_sum_kernel, quarter, halo),
        "first_sum",
        (
            ((quarter, width), f32),
            ((quarter + 3 * halo, width), bf16),
            ((quarter, width), bf16),
            ((quarter, width), bf16),
        ),
        keep,
        got,
    )
    from_behind = turned(ahead, 1)
    from_ahead = turned(behind, 3)
    from_across = turned(across, 2)
    mine, to1, to3, middle = in_vmem(
        functools.partial(second_sum_kernel, quarter, halo),
        "second_sum",
        (
            ((quarter, width), bf16),
            ((quarter + halo, width), bf16),
            ((quarter + halo, width), bf16),
            ((halo, width), f32),
        ),
        own,
        from_behind,
        from_across,
        from_ahead,
        got,
        halo_own,
    )
    along3 = swap(to3, "gy", 1, 3)
    along2 = swap(mine, "gy", 1, 2)
    along1 = swap(to1, "gy", 1, 1)
    mine = tree_sum(
        [
            mine.astype(f32),
            along1[halo:].astype(f32),
            along2.astype(f32),
            along3[halo:].astype(f32),
        ]
    ).astype(bf16)
    last_far = jnp.where((row == 0) | (row == 3), bf16(0), along3[:halo])
    part3, part2, part1 = (swap(mine, "gx", 2, mask) for mask in (3, 2, 1))
    onward = ((index >> 1) & 1) == (index & 1)
    mine = jnp.concatenate(
        [mine, jnp.where(onward, part1, part3), part2, jnp.where(onward, part3, part1)]
    )
    return mine, swap(mine, "gx", 1, 1), middle, last_far, along1[:halo]


def sum_staged(send, keep, halo_own, halo):
    f32, bf16 = jnp.float32, jnp.bfloat16
    width = send.shape[1]
    quarter = (send.shape[0] - 6 * halo) // 4
    slots = slot_rows(quarter, halo)

    def joined_slots(values):
        return jnp.concatenate([values[spot : spot + quarter] for spot in slots])

    far = send[2 * quarter : 2 * quarter + 3 * halo]
    near = send[4 * quarter + 3 * halo :]
    back_far, back_near = pair_exchange(far, near, "gx")
    strips = halo_own.astype(f32) + back_far.astype(f32) + back_near.astype(f32)
    low, high = strips[:halo].astype(bf16), strips[2 * halo :].astype(bf16)
    last_far, last_near = pair_exchange(
        even_pick("gy", low, high), even_pick("gy", high, low), "gy"
    )
    index = lax.axis_index("gx")
    got = swap(joined_slots(send), "gx", 1, 1)
    total = (joined_slots(keep) + got.astype(f32)).astype(bf16)
    split = stages(lax.axis_size("gx"))[1:]
    for stride, factor in split:
        part = (index // stride) % factor
        height = total.shape[0] // factor
        mine = lax.dynamic_slice_in_dim(total, part * height, height, 0).astype(f32)
        for mask in range(factor - 1, 0, -1):
            piece = lax.dynamic_slice_in_dim(total, (part ^ mask) * height, height, 0)
            mine = mine + swap(piece, "gx", stride, mask).astype(f32)
        total = mine.astype(bf16)
    total = tree_sum(
        [total.astype(f32)]
        + [swap(total, "gy", 1, mask).astype(f32) for mask in range(1, lax.axis_size("gy"))]
    ).astype(bf16)
    for stride, factor in reversed(split):
        part = (index // stride) % factor
        height = total.shape[0]
        joined = jnp.zeros((factor * height, width), bf16)
        joined = lax.dynamic_update_slice_in_dim(joined, total, part * height, 0)
        for mask in range(factor - 1, 0, -1):
            piece = swap(total, "gx", stride, mask)
            joined = lax.dynamic_update_slice_in_dim(joined, piece, (part ^ mask) * height, 0)
        total = joined
    return total, swap(total, "gx", 1, 1), strips[halo : 2 * halo], last_far, last_near


def per_device(
    node_latents,
    edge_latents,
    node_cotangent,
    edge_cotangent,
    neighbours,
    edge_mask,
    send_table,
    counts,
    weights,
    vectors,
    weights_m,
    vectors_m,
    weights_v,
    vectors_v,
    weights_ema,
    vectors_ema,
):
    f32, bf16 = jnp.float32, jnp.bfloat16
    tok_rows, width = node_latents.shape
    halo = send_table.shape[1]
    boundary_pick = selector(send_table[0], tok_rows, bf16)
    boundary = jnp.dot(boundary_pick, node_latents, preferred_element_type=f32).astype(bf16)
    from_far, from_near = pair_exchange(boundary, boundary, "gx")
    ring = jnp.concatenate([from_far, from_near, boundary], axis=0)
    ring_far, ring_near = pair_exchange(ring, ring, "gy")
    unit = 16 * lax.axis_size("gx")
    grad_rows = -(-(weights.shape[0] * width + vectors.shape[0]) // unit) * unit
    relayed = lax.axis_size("gx") == 8 and lax.axis_size("gy") == 4
    edge_shape = (tok_rows * neighbours.shape[1] // CHUNK, CHUNK, width)
    plan = plan_call(
        halo, counts, neighbours, edge_mask, node_latents, vectors, node_cotangent, weights,
        edge_latents.reshape(edge_shape),
    )
    nodes_out, edges_out, edges_in_grad, node_part, halo_own, send, keep = layer_call(
        halo, relayed, grad_rows, ring, ring_far, ring_near, edge_cotangent.reshape(edge_shape),
        plan,
    )
    sums = sum_relayed if relayed else sum_staged
    mine, other, middle, last_far, last_near = sums(send, keep, halo_own, halo)
    boundary_grad = middle + last_far.astype(f32) + last_near.astype(f32)
    returned = lax.dot_general(
        boundary_pick.astype(f32),
        boundary_grad,
        (((0,), (0,)), ((), ())),
        precision=lax.Precision.HIGHEST,
        preferred_element_type=f32,
    )
    nodes_in_grad = (node_part + returned).astype(bf16)
    updated = update_call(
        relayed, mine, other, weights, vectors, weights_m, vectors_m, weights_v, vectors_v, weights_ema,
        vectors_ema,
    )
    return (
        nodes_out,
        edges_out.reshape(edge_latents.shape),
        nodes_in_grad,
        edges_in_grad.reshape(edge_latents.shape),
        updated[0].reshape(()),
    ) + tuple(updated[1:])


def solution(mesh):
    in_specs = (
        P(("gx", "gy"), None),
        P(("gx", "gy"), None, None),
        P(("gx", "gy"), None),
        P(("gx", "gy"), None, None),
        P(("gx", "gy"), None),
        P(("gx", "gy"), None),
        P(("gx", "gy"), None),
        P(("gx", "gy")),
        P(),
        P(),
        P(),
        P(),
        P(),
        P(),
        P(),
        P(),
    )
    out_specs = (
        P(("gx", "gy"), None),
        P(("gx", "gy"), None, None),
        P(("gx", "gy"), None),
        P(("gx", "gy"), None, None),
        P(),
        P(),
        P(),
        P(),
        P(),
        P(),
        P(),
        P(),
        P(),
        P(),
        P(),
    )
    return jax.shard_map(
        per_device, mesh=mesh, in_specs=in_specs, out_specs=out_specs, check_vma=False
    )
```

```python
import functools

import jax
import jax.numpy as jnp
from jax import lax
from jax.experimental import pallas as pl
from jax.experimental.pallas import tpu as pltpu
from jax.sharding import PartitionSpec as P

STEP = 10


first_decay = 0.5
second_decay = 0.5
adam_epsilon = 1e-08
weight_decay = 0.01
matrix_rate = 0.05
vector_rate = 0.2
average_decay = 0.9
clip_norm = 1.0
norm_epsilon = 1e-05


def neighbour_pairs(count):
    near = [(i, i ^ 1) for i in range(count) if (i ^ 1) < count]
    far = [(i, i + 1) for i in range(1, count - 1, 2)]
    return near, far + [(target, source) for source, target in far]


def stages(count):
    result, stride = [], 1
    while stride < count:
        factor = 2 if stride == 1 else min(4, count // stride)
        result.append((stride, factor))
        stride *= factor
    return result


def selector(indices, width, dtype):
    columns = lax.broadcasted_iota(jnp.int32, (indices.shape[0], width), 1)
    return (indices[:, None] == columns).astype(dtype)


def adamw(param, grad, moment, second, average, scale, rate):
    clipped = grad * scale
    moment_new = first_decay * moment + (1.0 - first_decay) * clipped
    second_new = second_decay * second + (1.0 - second_decay) * clipped * clipped
    corrected = moment_new / (1.0 - first_decay**STEP)
    denom = jnp.sqrt(second_new / (1.0 - second_decay**STEP)) + adam_epsilon
    param_new = param - rate * (corrected / denom + weight_decay * param)
    average_new = average_decay * average + (1.0 - average_decay) * param_new
    return (moment_new, second_new, param_new, average_new)


CHUNK = 16
GROUP = 32
UPDATE_ROWS = 32
TILE = CHUNK * GROUP
LANES = 128
PIECES = 8


def dot(left, right):
    return jnp.dot(left, right, preferred_element_type=jnp.float32)


def dot_nt(left, right):
    return lax.dot_general(
        left, right, (((1,), (1,)), ((), ())), preferred_element_type=jnp.float32
    )


def dot_tn(left, right):
    return lax.dot_general(
        left, right, (((0,), (0,)), ((), ())), preferred_element_type=jnp.float32
    )


def split_pair(values, axis=1):
    high = values.astype(jnp.bfloat16)
    low = (values - high.astype(jnp.float32)).astype(jnp.bfloat16)
    return jnp.concatenate([high, low], axis=axis)


def halves(pair):
    width = pair.shape[1] // 2
    return pair[:, :width] + pair[:, width:]


def silu_of_half(half):
    turn = jnp.tanh(half)
    lift = 1.0 + turn
    act = half * lift
    return act, lift + act * (1.0 - turn)


def row_sum(values):
    return jnp.sum(values, axis=-1, keepdims=True)


def scaled_unit(values, width):
    center = values - row_sum(values) * (1.0 / width)
    inverse = lax.rsqrt(row_sum(center * center) + width * norm_epsilon)
    return center * inverse, inverse


def scaled_unit_back(scaled, unit, inverse, width):
    shift = row_sum(scaled) * (1.0 / width)
    return inverse * (scaled - shift - unit * row_sum(scaled * unit))


def column_total(values):
    return jnp.sum(values, axis=0, keepdims=True)


def iota(shape, dim):
    return lax.broadcasted_iota(jnp.int32, shape, dim)


def slot_rows(quarter, halo):
    return (0, quarter, 2 * quarter + 3 * halo, 3 * quarter + 3 * halo)


def part_rows(relayed, side, slot, quarter):
    chip = lax.axis_index("gx") >> 1
    part = (chip + slot * (1 - 2 * side)) & 3 if relayed else slot
    return pl.ds(pl.multiple_of((side * 4 + part) * quarter, 16), quarter)


def plan_kernel(
    halo,
    count_ref,
    mask_hbm,
    neighbour_hbm,
    latents_hbm,
    vectors_hbm,
    upstream_hbm,
    weights_hbm,
    edges_hbm,
    latents_ref,
    vectors_ref,
    upstream_ref,
    edges_buf,
    list_rows,
    segment_ref,
    neighbour_rows,
    receiver_ref,
    low_ref,
    gather_ref,
    blocks_ref,
    mask_ref,
    neighbour_ref,
    weights_ref,
    sems,
):
    f32, bf16, i32 = jnp.float32, jnp.bfloat16, jnp.int32
    slots, particles = neighbour_ref.shape
    per = slots // CHUNK
    chunks = particles * per
    width = latents_ref.shape[1]
    rows = particles + 8 * halo
    fetches = [
        pltpu.make_async_copy(source, target, sems.at[order])
        for order, (source, target) in enumerate(
            (
                (mask_hbm, mask_ref),
                (neighbour_hbm, neighbour_ref),
                (latents_hbm, latents_ref),
                (vectors_hbm, vectors_ref),
                (weights_hbm, weights_ref),
                (upstream_hbm, upstream_ref),
            )
        )
    ]
    for copy in fetches:
        copy.start()
    piece = chunks // PIECES
    loads = [
        pltpu.make_async_copy(
            edges_hbm.at[pl.ds(p * piece, piece)],
            edges_buf.at[pl.ds(p * piece, piece)],
            sems.at[len(fetches) + p],
        )
        for p in range(PIECES)
    ]
    for copy in loads:
        copy.start()
    edges_buf[chunks] = jnp.zeros((CHUNK, width), bf16)
    fetches[0].wait()

    mask = mask_ref[...].astype(f32)
    degree = jnp.sum(mask, axis=0, keepdims=True)
    taken = ((degree.astype(i32) + (CHUNK - 1)) >> 4).astype(f32)
    earlier = iota((particles, particles), 0) < iota((particles, particles), 1)
    begin = dot(jnp.broadcast_to(taken, (16, particles)).astype(bf16), earlier.astype(bf16))
    degree_col = dot_tn(mask.astype(bf16), jnp.ones((slots, width), bf16))
    taken_col = ((degree_col.astype(i32) + (CHUNK - 1)) >> 4).astype(f32)
    later = iota((particles, particles), 1) < iota((particles, particles), 0)
    begin_col = dot(later.astype(bf16), taken_col.astype(bf16))
    end_col = begin_col + taken_col
    for block in range(chunks // width):
        lane = iota((particles, width), 1).astype(f32) + block * width
        segment_ref[:, block * width : (block + 1) * width] = (
            (lane >= begin_col) & (lane < end_col)
        ).astype(bf16)
    total = row_sum(taken)
    who = iota((16, particles), 1).astype(f32)
    offset = per * who - begin
    coarse = jnp.floor(offset * 0.125) * 8.0
    line = iota((16, particles), 0)
    facts = jnp.where(
        line == 0,
        who,
        jnp.where(line == 1, coarse, jnp.where(line == 2, offset - coarse, degree)),
    )
    listing = dot(facts.astype(bf16), segment_ref[...])
    place = iota((1, chunks), 1).astype(f32)
    particle = listing[0:1, :]
    chunk = listing[1:2, :] + listing[2:3, :] + place
    rest = listing[3:4, :] - CHUNK * (chunk - per * particle)
    used = place < total
    list_rows[...] = jnp.zeros(list_rows.shape, i32)
    list_rows[0:1, 0:chunks] = jnp.where(used, chunk, float(chunks)).astype(i32)
    list_rows[0:1, chunks:] = jnp.full((1, list_rows.shape[1] - chunks), chunks, i32)
    list_rows[1:2, 0:chunks] = jnp.where(used, particle, float(particles)).astype(i32)
    list_rows[1:2, chunks:] = jnp.full((1, list_rows.shape[1] - chunks), particles, i32)
    list_rows[2:3, 0:chunks] = jnp.where(used, rest, 0.0).astype(i32)
    list_rows[3:4, 0:particles] = jnp.broadcast_to(total, (1, particles)).astype(i32)
    list_rows[4:5, 0:particles] = (begin[0:1, :] + taken).astype(i32)
    list_rows[5:6, 0:particles] = jnp.full((1, particles), count_ref[0], i32)

    fetches[1].wait()
    neighbour = neighbour_ref[...]
    neighbour = jnp.where(neighbour >= particles + 5 * halo, neighbour - halo, neighbour)
    neighbour_rows[...] = jnp.zeros(neighbour_rows.shape, f32)
    neighbour_rows[0:particles, 0:slots] = neighbour.astype(f32).T

    block_of = iota((TILE, LANES), 0) >> 4
    for quarter in range(LANES // GROUP):
        blocks_ref[quarter] = (iota((TILE, LANES), 1) == block_of + quarter * GROUP).astype(bf16)

    for copy in fetches[2:]:
        copy.wait()
    for block in range(weights_ref.shape[0]):
        low_ref[block] = weights_ref[block].astype(bf16)
    for extra, block in ((9, 3), (10, 4)):
        low_ref[extra] = (0.5 * low_ref[block].astype(f32)).astype(bf16)
    latents = latents_ref[...]
    gather_ref[0:particles, :] = split_pair(0.5 * dot(latents, low_ref[2]))
    gather_ref[particles:rows, :] = jnp.zeros((rows - particles, 2 * width), bf16)
    gather_ref[rows : rows + width, :] = jnp.concatenate(
        [(0.5 * low_ref[0].astype(f32)).astype(bf16), jnp.zeros((width, width), bf16)], axis=1
    )
    gather_ref[rows + width :, :] = jnp.zeros((LANES, 2 * width), bf16)
    receiver_ref[0:particles, :] = 0.5 * (dot(latents, low_ref[1]) + vectors_ref[0:1, :])
    receiver_ref[particles:, :] = jnp.zeros((receiver_ref.shape[0] - particles, width), f32)
    for copy in loads:
        copy.wait()


def layer_kernel(
    halo,
    relayed,
    latents_ref,
    ring_ref,
    ring_far_ref,
    ring_near_ref,
    upstream_ref,
    vectors_ref,
    list_rows,
    segment_ref,
    neighbour_rows,
    receiver_ref,
    low_ref,
    blocks_ref,
    edges_in,
    gather_in,
    cotangent_hbm,
    nodes_out_hbm,
    edges_out_hbm,
    edges_grad_hbm,
    node_part_ref,
    halo_own_ref,
    send_ref,
    keep_ref,
    edges_buf,
    gather_ref,
    nodes_out_ref,
    cotangent_buf,
    kept_edges,
    kept_index,
    kept_act1,
    kept_act2,
    kept_slope1,
    kept_slope2,
    kept_unit,
    kept_inverse,
    table_ref,
    descent_ref,
    receiver_tile,
    chunk_sums,
    chunk_grads,
    index_acc,
    mat_acc,
    vec_acc,
    first_tile,
    last_tile,
    third_tile,
    first_back,
    second_back,
    passed_tile,
    halo_grad,
    grads,
    listed,
    in_sems,
    out_sems,
    list_sem,
    nodes_sem,
):
    f32, bf16, i32 = jnp.float32, jnp.bfloat16, jnp.int32
    fetch_list = pltpu.make_async_copy(list_rows, listed, list_sem)
    fetch_list.start()
    particles, chunks = segment_ref.shape
    per = chunks // particles
    width = latents_ref.shape[1]
    rows = table_ref.shape[0]
    piece = chunks // PIECES
    root = float(width) ** 0.5
    odd_x = lax.axis_index("gx") & 1
    odd_y = lax.axis_index("gy") & 1
    loads = [
        pltpu.make_async_copy(
            cotangent_hbm.at[pl.ds(p * piece, piece)],
            cotangent_buf.at[pl.ds(p * piece, piece)],
            in_sems.at[p],
        )
        for p in range(PIECES)
    ]
    for copy in loads:
        copy.start()
    cotangent_buf[chunks] = jnp.zeros((CHUNK, width), bf16)

    table_ref[0:particles, :] = latents_ref[...]
    far, near, own = ring_far_ref[...], ring_near_ref[...], ring_ref[...]
    low_y = jnp.where(odd_y == 0, far, near)
    high_y = jnp.where(odd_y == 0, near, far)
    spot = particles
    for a in range(3):
        for b, strip in enumerate((low_y, own, high_y)):
            if a == 1 and b == 1:
                continue
            if a == 1:
                part = strip[2 * halo :]
            elif a == 0:
                part = jnp.where(odd_x == 0, strip[0:halo], strip[halo : 2 * halo])
            else:
                part = jnp.where(odd_x == 0, strip[halo : 2 * halo], strip[0:halo])
            table_ref[spot : spot + halo, :] = part
            spot += halo

    vectors = vectors_ref[...]

    def vector(row):
        return vectors[row : row + 1, :]

    latents = latents_ref[...]
    half3, half4 = low_ref[9], low_ref[10]
    gather_ref[particles:rows, :] = split_pair(0.5 * dot(table_ref[particles:, :], low_ref[2]))
    chunk_sums[...] = jnp.zeros(chunk_sums.shape, f32)
    chunk_grads[...] = jnp.zeros(chunk_grads.shape, f32)
    index_acc[...] = jnp.zeros(index_acc.shape, f32)
    mat_acc[...] = jnp.zeros(mat_acc.shape, f32)
    vec_acc[...] = jnp.zeros(vec_acc.shape, f32)
    tail = 9 * width
    grads[tail:, :] = jnp.zeros((grads.shape[0] - tail, width), f32)
    descent_ref[particles:, :] = jnp.zeros((descent_ref.shape[0] - particles, width), f32)

    fetch_list.wait()
    tiles = (listed[3, 0] + (GROUP - 1)) >> 5

    sublane = iota((CHUNK, width), 0)
    diagonal = iota((CHUNK, width), 1) - sublane
    lane16 = iota((TILE, width), 1).astype(jnp.int16)

    def flat(ref, t):
        return ref[pl.ds(t * GROUP, GROUP)].reshape(TILE, width)

    def keep(ref, t, values):
        ref[pl.ds(t * GROUP, GROUP)] = values.astype(ref.dtype).reshape(GROUP, CHUNK, width)

    def span(j):
        return slice(j * CHUNK, (j + 1) * CHUNK)

    def one_hot(t):
        index = flat(kept_index, t)
        return [
            jnp.where(index == lane16 + jnp.int16(b * width), bf16(1), bf16(0))
            for b in range(rows // width)
        ]

    def gather(t):
        base = t * GROUP
        for j in range(GROUP):
            chunk, particle = listed[0, base + j], listed[1, base + j]
            kept_edges[base + j] = edges_buf[chunk]
            row = jnp.broadcast_to(neighbour_rows[pl.ds(particle, 1), :], (CHUNK, width))
            start = (chunk & (per - 1)) * CHUNK
            index = row_sum(jnp.where(diagonal == start, row, 0.0))
            kept_index[base + j] = (
                jnp.broadcast_to(index, (CHUNK, width)).astype(i32).astype(jnp.int16)
            )
            receiver_tile[j : j + 1, :] = receiver_ref[pl.ds(particle, 1), :]
        gather_ref[rows + width : rows + width + GROUP, :] = split_pair(receiver_tile[...])

    def project(t):
        picks = jnp.concatenate(one_hot(t) + [flat(kept_edges, t), blocks_ref[0]], axis=1)
        first_tile[...] = halves(dot(picks, gather_ref[...]))

    gain_root = vector(3) * root

    def finish(t):
        base = t * GROUP
        unit, inverse = scaled_unit(last_tile[...], width)
        keep(kept_unit, t, unit)
        keep(kept_inverse, t, jnp.broadcast_to(inverse, (TILE, width)))
        change = unit * gain_root + vector(4)
        for j in range(GROUP):
            chunk = listed[0, base + j]
            alive = sublane < listed[2, base + j]
            fresh = kept_edges[base + j].astype(f32) + jnp.where(alive, change[span(j)], 0.0)
            edges_buf[chunk] = fresh.astype(bf16)
            chunk_sums[pl.ds(base + j, 1), :] = column_total(jnp.where(alive, fresh, 0.0))

    def forward(t, carry):
        gather(t + 1)
        act, slope = silu_of_half(first_tile[...])
        act = act.astype(bf16)
        keep(kept_act1, t, act)
        keep(kept_slope1, t, slope)
        finish(jnp.where(t == 0, tiles, t - 1))
        act, slope = silu_of_half(dot(act, half3) + 0.5 * vector(1))
        act = act.astype(bf16)
        keep(kept_act2, t, act)
        keep(kept_slope2, t, slope)
        project(t + 1)
        last_tile[...] = dot(act, low_ref[4]) + vector(2)
        return carry

    for ref in (kept_act1, kept_edges):
        keep(ref, tiles, jnp.zeros((TILE, width), f32))
    last_tile[...] = jnp.zeros(last_tile.shape, f32)
    gather(0)
    project(0)
    lax.fori_loop(0, tiles, forward, 0)
    finish(jnp.where(tiles == 0, tiles, tiles - 1))

    stores = [
        pltpu.make_async_copy(
            edges_buf.at[pl.ds(p * piece, piece)],
            edges_out_hbm.at[pl.ds(p * piece, piece)],
            out_sems.at[p],
        )
        for p in range(PIECES)
    ]
    for copy in stores:
        copy.start()

    aggregate = halves(dot(segment_ref[...], split_pair(chunk_sums[0:chunks, :]))).astype(bf16)
    half1 = 0.5 * (dot(latents, low_ref[5]) + dot(aggregate, low_ref[6]) + vector(5))
    act1, slope1 = silu_of_half(half1)
    act1 = act1.astype(bf16)
    act2, slope2 = silu_of_half(0.5 * (dot(act1, low_ref[7]) + vector(6)))
    act2 = act2.astype(bf16)
    unit, inverse = scaled_unit(dot(act2, low_ref[8]) + vector(7), width)
    alive = (iota((particles, width), 0) < listed[5, 0]).astype(f32)
    upstream = upstream_ref[...].astype(f32)
    nodes_out_ref[...] = (
        latents.astype(f32) + alive * (unit * (vector(8) * root) + vector(9))
    ).astype(bf16)
    send_nodes = pltpu.make_async_copy(nodes_out_ref, nodes_out_hbm, nodes_sem)
    send_nodes.start()
    held = alive * upstream
    third = scaled_unit_back(held * (vector(8) * root), unit, inverse, width).astype(bf16)
    second = (0.5 * slope2 * dot_nt(third, low_ref[8])).astype(bf16)
    first = (0.5 * slope1 * dot_nt(second, low_ref[7])).astype(bf16)
    descent_ref[0:particles, :] = dot_nt(first, low_ref[6])
    node_part_ref[...] = upstream + dot_nt(first, low_ref[5])

    def put_block(block, values):
        grads[block * width : (block + 1) * width, :] = values

    put_block(5, dot_tn(latents, first))
    put_block(6, dot_tn(aggregate, first))
    put_block(7, dot_tn(act1, second))
    put_block(8, dot_tn(act2, third))
    for row, values in enumerate(
        (first.astype(f32), second.astype(f32), third.astype(f32), held * unit * root, held)
    ):
        grads[tail + 5 + row : tail + 6 + row, :] = column_total(values)

    for copy in loads:
        copy.wait()

    def add_columns(row, values):
        vec_acc[8 * row : 8 * row + 8, :] += jnp.sum(values.reshape(TILE // 8, 8, width), axis=0)

    def accept(t):
        base = t * GROUP
        parts = []
        for j in range(GROUP):
            chunk, particle = listed[0, base + j], listed[1, base + j]
            alive = sublane < listed[2, base + j]
            passed = cotangent_buf[chunk].astype(f32) + jnp.where(
                alive, descent_ref[pl.ds(particle, 1), :], 0.0
            )
            passed_tile[t & 3, span(j), :] = passed
            parts.append(jnp.where(alive, passed, 0.0))
        return jnp.concatenate(parts, axis=0)

    def descend(t, held):
        unit = flat(kept_unit, t).astype(f32)
        third = scaled_unit_back(held * gain_root, unit, flat(kept_inverse, t), width)
        third_tile[...] = third.astype(bf16)
        add_columns(2, third)
        add_columns(3, held * unit)
        add_columns(4, held)

    def settle(t, slot):
        base = t * GROUP
        first = first_back[...]
        result = passed_tile[slot] + dot_nt(first, low_ref[0])
        for j in range(GROUP):
            cotangent_buf[listed[0, base + j]] = result[span(j)].astype(bf16)
        picks = jnp.concatenate(one_hot(t) + [flat(kept_edges, t), blocks_ref[t & 3]], axis=1)
        index_acc[...] += dot_tn(first, picks[:, 0 : rows + width])
        chunk_grads[t >> 2] += dot_tn(first, picks[:, rows + width :])
        mat_acc[0] += dot_tn(flat(kept_act1, t), second_back[...])

    def backward(t, carry):
        third = third_tile[...]
        second = dot_nt(third, half4)
        held = accept(t + 1)
        settle(jnp.where(t == 0, tiles, t - 1), (t + 3) & 3)
        second = flat(kept_slope2, t).astype(f32) * second
        add_columns(1, second)
        second = second.astype(bf16)
        descend(t + 1, held)
        first = flat(kept_slope1, t).astype(f32) * dot_nt(second, half3)
        mat_acc[1] += dot_tn(flat(kept_act2, t), third)
        first_back[...] = first.astype(bf16)
        second_back[...] = second
        return carry

    first_back[...] = jnp.zeros(first_back.shape, bf16)
    second_back[...] = jnp.zeros(second_back.shape, bf16)
    passed_tile[3] = jnp.zeros((TILE, width), f32)
    descend(0, accept(0))
    def send_piece(p):
        pltpu.make_async_copy(
            cotangent_buf.at[pl.ds(p * piece, piece)],
            edges_grad_hbm.at[pl.ds(p * piece, piece)],
            out_sems.at[PIECES + p],
        ).start()

    def last_tile(p):
        return (listed[4, (p + 1) * (piece // per) - 1] + (GROUP - 1)) >> 5

    def backward_piece(p, t):
        upto = last_tile(p) + 1
        stop = jnp.minimum(upto, tiles)
        lax.fori_loop(t, stop, backward, 0)

        @pl.when(upto <= tiles)
        def _():
            send_piece(p)

        return jnp.maximum(t, stop)

    lax.fori_loop(0, PIECES, backward_piece, jnp.int32(0))
    settle(jnp.where(tiles == 0, tiles, tiles - 1), (tiles + 3) & 3)

    @pl.loop(0, PIECES)
    def _(p):
        @pl.when(last_tile(p) + 1 > tiles)
        def _():
            send_piece(p)

    stacked = split_pair(
        jnp.concatenate([chunk_grads[g] for g in range(chunks // LANES)], axis=1), axis=0
    )
    receiver_grad = halves(dot_nt(segment_ref[...], stacked)).astype(bf16)
    grads[tail : tail + 1, :] = halves(dot_nt(jnp.ones((8, chunks), bf16), stacked))[0:1, :]
    for row in range(1, 5):
        values = column_total(vec_acc[8 * row : 8 * row + 8, :])
        grads[tail + row : tail + row + 1, :] = values * root if row == 3 else values
    sent = index_acc[:, 0:rows].astype(bf16)
    put_block(0, index_acc[:, rows:].T)
    put_block(1, dot_tn(latents, receiver_grad))
    put_block(2, dot(sent, table_ref[...]).T)
    put_block(3, mat_acc[0])
    put_block(4, mat_acc[1])
    table_grad = lax.dot_general(
        sent, low_ref[2], (((0,), (1,)), ((), ())), preferred_element_type=f32
    )
    node_part_ref[...] += dot_nt(receiver_grad, low_ref[1]) + table_grad[0:particles, :]
    halo_grad[...] = table_grad[particles:, :].astype(bf16)
    low_x = halo_grad[0 : 3 * halo, :]
    high_x = halo_grad[5 * halo : 8 * halo, :]
    halo_own_ref[0:halo, :] = halo_grad[3 * halo : 4 * halo, :]
    halo_own_ref[halo : 2 * halo, :] = jnp.zeros((halo, width), bf16)
    halo_own_ref[2 * halo :, :] = halo_grad[4 * halo : 5 * halo, :]
    quarter = grads.shape[0] // 8
    relay = 2 * quarter
    send_ref[relay : relay + 3 * halo, :] = jnp.where(odd_x == 0, low_x, high_x)
    send_ref[4 * quarter + 3 * halo :, :] = jnp.where(odd_x == 0, high_x, low_x)
    keep_ref[relay : relay + 3 * halo, :] = jnp.zeros((3 * halo, width), f32)
    for slot, spot in enumerate(slot_rows(quarter, halo)):
        kept_rows = part_rows(relayed, odd_x, slot, quarter)
        sent_rows = part_rows(relayed, 1 - odd_x, slot, quarter)
        keep_ref[spot : spot + quarter, :] = grads[kept_rows, :]
        send_ref[spot : spot + quarter, :] = grads[sent_rows, :].astype(bf16)

    for copy in stores + [send_nodes]:
        copy.wait()
    for p in range(PIECES):
        pltpu.make_async_copy(
            cotangent_buf.at[pl.ds(p * piece, piece)],
            edges_grad_hbm.at[pl.ds(p * piece, piece)],
            out_sems.at[PIECES + p],
        ).wait()


def pinned(values):
    return pltpu.with_memory_space_constraint(values, pltpu.VMEM)


def outer(values):
    return pltpu.with_memory_space_constraint(values, pltpu.HBM)


def plan_call(halo, counts, neighbours, edge_mask, latents, vectors, upstream, weights, edges):
    f32, bf16, i32 = jnp.float32, jnp.bfloat16, jnp.int32
    particles, slots = neighbours.shape
    width = latents.shape[1]
    chunks = particles * slots // CHUNK
    whole = pl.BlockSpec(memory_space=pltpu.VMEM)
    outside = pl.BlockSpec(memory_space=pl.ANY)
    return pl.pallas_call(
        functools.partial(plan_kernel, halo),
        out_shape=(
            pltpu.VMEM(latents.shape, bf16),
            pltpu.VMEM(vectors.shape, f32),
            pltpu.VMEM(upstream.shape, bf16),
            pltpu.VMEM((chunks + 1, CHUNK, width), bf16),
            pltpu.VMEM((8, chunks + LANES), i32),
            pltpu.VMEM((particles, chunks), bf16),
            pltpu.VMEM((particles + 8, width), f32),
            pltpu.VMEM((particles + 8, width), f32),
            pltpu.VMEM((weights.shape[0] + 2, width, width), bf16),
            pltpu.VMEM((particles + 8 * halo + width + LANES, 2 * width), bf16),
            pltpu.VMEM((LANES // GROUP, TILE, LANES), bf16),
        ),
        in_specs=[pl.BlockSpec(memory_space=pltpu.SMEM)] + [outside] * 7,
        out_specs=(whole,) * 11,
        scratch_shapes=[
            pltpu.VMEM((slots, particles), i32),
            pltpu.VMEM((slots, particles), i32),
            pltpu.VMEM(weights.shape, f32),
            pltpu.SemaphoreType.DMA((6 + PIECES,)),
        ],
        compiler_params=pltpu.CompilerParams(vmem_limit_bytes=16 * 1024 * 1024),
        cost_estimate=pl.CostEstimate(
            flops=10**9, bytes_accessed=12 * 10**6, transcendentals=0
        ),
        name="plan",
    )(
        counts,
        outer(edge_mask.T),
        outer(neighbours.T),
        outer(latents),
        outer(vectors),
        outer(upstream),
        outer(weights),
        outer(edges),
    )


def layer_call(halo, relayed, grad_rows, ring, ring_far, ring_near, cotangents, plan):
    f32, bf16, i32 = jnp.float32, jnp.bfloat16, jnp.int32
    latents, vectors, upstream, edges, listing, segment, *more, gather, blocks = plan
    neighbour_rows, receiver, low = more
    particles, chunks = segment.shape
    width = latents.shape[1]
    rows = particles + 8 * halo
    whole = pl.BlockSpec(memory_space=pltpu.VMEM)
    outside = pl.BlockSpec(memory_space=pl.ANY)
    edge_shape = (chunks, CHUNK, width)
    kept_shape = (chunks + GROUP, CHUNK, width)
    kept = pltpu.VMEM(kept_shape, bf16)
    half = grad_rows // 2
    return pl.pallas_call(
        functools.partial(layer_kernel, halo, relayed),
        out_shape=(
            jax.ShapeDtypeStruct((particles, width), bf16),
            jax.ShapeDtypeStruct(edge_shape, bf16),
            jax.ShapeDtypeStruct(edge_shape, bf16),
            pltpu.VMEM((particles, width), f32),
            pltpu.VMEM((3 * halo, width), bf16),
            pltpu.VMEM((half + 6 * halo, width), bf16),
            pltpu.VMEM((half + 3 * halo, width), f32),
            pltpu.VMEM(edges.shape, bf16),
            pltpu.VMEM(gather.shape, bf16),
        ),
        in_specs=[whole] * 14 + [outside],
        out_specs=(outside,) * 3 + (whole,) * 6,
        input_output_aliases={12: 7, 13: 8},
        scratch_shapes=[
            pltpu.VMEM((particles, width), bf16),
            pltpu.VMEM(edges.shape, bf16),
            kept,
            pltpu.VMEM(kept_shape, jnp.int16),
            kept,
            kept,
            kept,
            kept,
            kept,
            pltpu.VMEM(kept_shape, f32),
            pltpu.VMEM((rows, width), bf16),
            pltpu.VMEM((particles + 8, width), f32),
            pltpu.VMEM((GROUP, width), f32),
            pltpu.VMEM((chunks + GROUP, width), f32),
            pltpu.VMEM((chunks // LANES + 1, width, LANES), f32),
            pltpu.VMEM((width, rows + width), f32),
            pltpu.VMEM((2, width, width), f32),
            pltpu.VMEM((40, width), f32),
            pltpu.VMEM((TILE, width), f32),
            pltpu.VMEM((TILE, width), f32),
            pltpu.VMEM((TILE, width), bf16),
            pltpu.VMEM((TILE, width), bf16),
            pltpu.VMEM((TILE, width), bf16),
            pltpu.VMEM((4, TILE, width), f32),
            pltpu.VMEM((8 * halo, width), bf16),
            pltpu.VMEM((grad_rows, width), f32),
            pltpu.SMEM((8, chunks + LANES), i32),
            pltpu.SemaphoreType.DMA((PIECES,)),
            pltpu.SemaphoreType.DMA((2 * PIECES,)),
            pltpu.SemaphoreType.DMA,
            pltpu.SemaphoreType.DMA,
        ],
        compiler_params=pltpu.CompilerParams(vmem_limit_bytes=52 * 1024 * 1024),
        name="edge_layer",
    )(
        pinned(latents),
        pinned(ring),
        pinned(ring_far),
        pinned(ring_near),
        pinned(upstream),
        pinned(vectors),
        pinned(listing),
        pinned(segment),
        pinned(neighbour_rows),
        pinned(receiver),
        pinned(low),
        pinned(blocks),
        pinned(edges),
        pinned(gather),
        outer(cotangents),
    )[:7]


def update_kernel(
    relayed,
    *refs,
):
    parts, rest = refs[:8], refs[8:]
    update_rows(relayed, parts, *rest)


def update_rows(
    relayed,
    parts,
    weights_ref,
    vectors_ref,
    weights_m_ref,
    vectors_m_ref,
    weights_v_ref,
    vectors_v_ref,
    weights_ema_ref,
    vectors_ema_ref,
    norm_ref,
    weights_m_out,
    vectors_m_out,
    weights_v_out,
    vectors_v_out,
    weights_out,
    vectors_out,
    weights_copy_out,
    vectors_copy_out,
    weights_ema_out,
    vectors_ema_out,
    grads,
):
    f32 = jnp.float32
    odd = lax.axis_index("gx") & 1
    quarter, width = parts[0].shape
    chip = (lax.axis_index("gx") >> 1) & 3 if relayed else 0
    squares = jnp.zeros((8, width), f32)
    for order, part_ref in enumerate(parts):
        side = odd if order < 4 else 1 - odd
        values = part_ref[...].astype(f32)
        spot = (side * 4 + ((order & 3) ^ chip)) * quarter
        grads[pl.ds(pl.multiple_of(spot, 16), quarter), :] = values
        squares = squares + jnp.sum((values * values).reshape(quarter // 8, 8, width), axis=0)
    norm = jnp.sqrt(jnp.sum(jnp.sum(squares, axis=1, keepdims=True), axis=0, keepdims=True))
    norm_ref[...] = norm
    scale = clip_norm / jnp.maximum(norm, clip_norm)
    for block in range(weights_ref.shape[0]):
        for row in range(0, width, UPDATE_ROWS):
            part = slice(row, row + UPDATE_ROWS)
            moment, second, param, average = adamw(
                weights_ref[block, part, :],
                grads[block * width + row : block * width + row + UPDATE_ROWS, :],
                weights_m_ref[block, part, :],
                weights_v_ref[block, part, :],
                weights_ema_ref[block, part, :],
                scale,
                matrix_rate,
            )
            weights_m_out[block, part, :] = moment
            weights_v_out[block, part, :] = second
            weights_out[block, part, :] = param
            weights_copy_out[block, part, :] = param.astype(jnp.bfloat16)
            weights_ema_out[block, part, :] = average
    tail = weights_ref.shape[0] * width
    moment, second, param, average = adamw(
        vectors_ref[...],
        grads[tail : tail + vectors_ref.shape[0], :],
        vectors_m_ref[...],
        vectors_v_ref[...],
        vectors_ema_ref[...],
        scale,
        vector_rate,
    )
    vectors_m_out[...] = moment
    vectors_v_out[...] = second
    vectors_out[...] = param
    vectors_copy_out[...] = param.astype(jnp.bfloat16)
    vectors_ema_out[...] = average


def update_call(relayed, parts, weights, vectors, weights_m, vectors_m, weights_v, vectors_v,
                weights_ema, vectors_ema):
    f32, bf16 = jnp.float32, jnp.bfloat16
    mat, vec = weights.shape, vectors.shape
    kinds = (
        ((1, 1), f32), (mat, f32), (vec, f32), (mat, f32), (vec, f32), (mat, f32), (vec, f32),
        (mat, bf16), (vec, bf16), (mat, f32), (vec, f32),
    )
    whole = pl.BlockSpec(memory_space=pltpu.VMEM)
    return pl.pallas_call(
        functools.partial(update_kernel, relayed),
        out_shape=tuple(jax.ShapeDtypeStruct(*kind) for kind in kinds),
        in_specs=[whole] * 16,
        out_specs=(whole,) * 11,
        scratch_shapes=[pltpu.VMEM((8 * parts[0].shape[0], parts[0].shape[1]), f32)],
        compiler_params=pltpu.CompilerParams(vmem_limit_bytes=24 * 1024 * 1024),
        name="update",
    )(*[pinned(part) for part in parts], weights, vectors, weights_m, vectors_m, weights_v, vectors_v, weights_ema,
      vectors_ema)


def pair_exchange(to_far, to_near, axis):
    near, far = neighbour_pairs(lax.axis_size(axis))
    return lax.ppermute(to_far, axis, far), lax.ppermute(to_near, axis, near)


def partners(axis, stride, mask):
    return [(i, i ^ (mask * stride)) for i in range(lax.axis_size(axis))]


def even_pick(axis, even, odd):
    return jnp.where(lax.axis_index(axis) % 2 == 0, even, odd)


def swap(values, axis, stride, mask):
    return lax.ppermute(values, axis, partners(axis, stride, mask))


def tree_sum(terms):
    while len(terms) > 1:
        terms = [terms[i] + terms[i + 1] for i in range(0, len(terms), 2)]
    return terms[0]


def first_sum_kernel(quarter, halo, keep_ref, got_ref, own_ref, ahead_ref, across_ref, behind_ref):
    rows = 4 * quarter + 3 * halo
    total = keep_ref[...] + got_ref[0:rows, :].astype(jnp.float32)
    spots = slot_rows(quarter, halo)
    own_ref[...] = total[:quarter]
    ahead_ref[...] = total[quarter : 2 * quarter + 3 * halo].astype(jnp.bfloat16)
    across_ref[...] = total[spots[2] : spots[2] + quarter].astype(jnp.bfloat16)
    behind_ref[...] = total[spots[3] : spots[3] + quarter].astype(jnp.bfloat16)


def second_sum_kernel(
    quarter,
    halo,
    own_ref,
    from_behind_ref,
    from_across_ref,
    from_ahead_ref,
    got_ref,
    halo_own_ref,
    mine_ref,
    along1_ref,
    along3_ref,
    middle_ref,
):
    f32, bf16 = jnp.float32, jnp.bfloat16
    index, odd_y = lax.axis_index("gx"), lax.axis_index("gy") & 1
    mine = (own_ref[...] + from_behind_ref[0:quarter, :].astype(f32)) + (
        from_across_ref[...].astype(f32) + from_ahead_ref[...].astype(f32)
    )
    mine = mine.astype(bf16)
    mine_ref[...] = mine
    far = from_behind_ref[quarter:, :].astype(f32)
    far = jnp.where((index == 0) | (index == 7), 0.0, far)
    strips = halo_own_ref[...].astype(f32) + got_ref[4 * quarter + 3 * halo :, :].astype(f32) + far
    low, high = strips[:halo].astype(bf16), strips[2 * halo :].astype(bf16)
    middle_ref[...] = strips[halo : 2 * halo]
    along3_ref[0:halo, :] = jnp.where(odd_y == 0, low, high)
    along3_ref[halo:, :] = mine
    along1_ref[0:halo, :] = jnp.where(odd_y == 0, high, low)
    along1_ref[halo:, :] = mine


def in_vmem(kernel, name, shapes, *operands):
    whole = pl.BlockSpec(memory_space=pltpu.VMEM)
    return pl.pallas_call(
        kernel,
        out_shape=tuple(pltpu.VMEM(shape, dtype) for shape, dtype in shapes),
        in_specs=[whole] * len(operands),
        out_specs=(whole,) * len(shapes),
        compiler_params=pltpu.CompilerParams(vmem_limit_bytes=8 * 1024 * 1024),
        name=name,
    )(*[pinned(operand) for operand in operands])


def sum_relayed(send, keep, halo_own, halo):
    f32, bf16 = jnp.float32, jnp.bfloat16
    width = send.shape[1]
    quarter = (send.shape[0] - 6 * halo) // 4
    index, row = lax.axis_index("gx"), lax.axis_index("gy")

    def turned(values, step):
        pairs = [(i, ((i >> 1) + step * (1 - 2 * (i & 1))) % 4 * 2 + (i & 1)) for i in range(8)]
        return lax.ppermute(values, "gx", pairs)

    got = swap(send, "gx", 1, 1)
    own, ahead, across, behind = in_vmem(
        functools.partial(first_sum_kernel, quarter, halo),
        "first_sum",
        (
            ((quarter, width), f32),
            ((quarter + 3 * halo, width), bf16),
            ((quarter, width), bf16),
            ((quarter, width), bf16),
        ),
        keep,
        got,
    )
    from_behind = turned(ahead, 1)
    from_ahead = turned(behind, 3)
    from_across = turned(across, 2)
    mine, to1, to3, middle = in_vmem(
        functools.partial(second_sum_kernel, quarter, halo),
        "second_sum",
        (
            ((quarter, width), bf16),
            ((quarter + halo, width), bf16),
            ((quarter + halo, width), bf16),
            ((halo, width), f32),
        ),
        own,
        from_behind,
        from_across,
        from_ahead,
        got,
        halo_own,
    )
    along3 = swap(to3, "gy", 1, 3)
    along2 = swap(mine, "gy", 1, 2)
    along1 = swap(to1, "gy", 1, 1)
    mine = tree_sum(
        [
            mine.astype(f32),
            along1[halo:].astype(f32),
            along2.astype(f32),
            along3[halo:].astype(f32),
        ]
    ).astype(bf16)
    last_far = jnp.where((row == 0) | (row == 3), bf16(0), along3[:halo])
    part3, part2, part1 = (swap(mine, "gx", 2, mask) for mask in (3, 2, 1))
    mine, part3 = lax.optimization_barrier((mine, part3))
    parts = [mine, part1, part2, part3]
    others = [swap(part, "gx", 1, 1) for part in parts]
    return parts + others, middle, last_far, along1[:halo]


def sum_staged(send, keep, halo_own, halo):
    f32, bf16 = jnp.float32, jnp.bfloat16
    width = send.shape[1]
    quarter = (send.shape[0] - 6 * halo) // 4
    slots = slot_rows(quarter, halo)

    def joined_slots(values):
        return jnp.concatenate([values[spot : spot + quarter] for spot in slots])

    far = send[2 * quarter : 2 * quarter + 3 * halo]
    near = send[4 * quarter + 3 * halo :]
    back_far, back_near = pair_exchange(far, near, "gx")
    strips = halo_own.astype(f32) + back_far.astype(f32) + back_near.astype(f32)
    low, high = strips[:halo].astype(bf16), strips[2 * halo :].astype(bf16)
    last_far, last_near = pair_exchange(
        even_pick("gy", low, high), even_pick("gy", high, low), "gy"
    )
    index = lax.axis_index("gx")
    got = swap(joined_slots(send), "gx", 1, 1)
    total = (joined_slots(keep) + got.astype(f32)).astype(bf16)
    split = stages(lax.axis_size("gx"))[1:]
    for stride, factor in split:
        part = (index // stride) % factor
        height = total.shape[0] // factor
        mine = lax.dynamic_slice_in_dim(total, part * height, height, 0).astype(f32)
        for mask in range(factor - 1, 0, -1):
            piece = lax.dynamic_slice_in_dim(total, (part ^ mask) * height, height, 0)
            mine = mine + swap(piece, "gx", stride, mask).astype(f32)
        total = mine.astype(bf16)
    total = tree_sum(
        [total.astype(f32)]
        + [swap(total, "gy", 1, mask).astype(f32) for mask in range(1, lax.axis_size("gy"))]
    ).astype(bf16)
    for stride, factor in reversed(split):
        part = (index // stride) % factor
        height = total.shape[0]
        joined = jnp.zeros((factor * height, width), bf16)
        joined = lax.dynamic_update_slice_in_dim(joined, total, part * height, 0)
        for mask in range(factor - 1, 0, -1):
            piece = swap(total, "gx", stride, mask)
            joined = lax.dynamic_update_slice_in_dim(joined, piece, (part ^ mask) * height, 0)
        total = joined
    other = swap(total, "gx", 1, 1)
    parts = [
        half[part * quarter : (part + 1) * quarter] for half in (total, other) for part in range(4)
    ]
    return parts, strips[halo : 2 * halo], last_far, last_near


def per_device(
    node_latents,
    edge_latents,
    node_cotangent,
    edge_cotangent,
    neighbours,
    edge_mask,
    send_table,
    counts,
    weights,
    vectors,
    weights_m,
    vectors_m,
    weights_v,
    vectors_v,
    weights_ema,
    vectors_ema,
):
    f32, bf16 = jnp.float32, jnp.bfloat16
    tok_rows, width = node_latents.shape
    halo = send_table.shape[1]
    boundary_pick = selector(send_table[0], tok_rows, bf16)
    boundary = jnp.dot(boundary_pick, node_latents, preferred_element_type=f32).astype(bf16)
    from_far, from_near = pair_exchange(boundary, boundary, "gx")
    ring = jnp.concatenate([from_far, from_near, boundary], axis=0)
    ring_far, ring_near = pair_exchange(ring, ring, "gy")
    unit = 16 * lax.axis_size("gx")
    grad_rows = -(-(weights.shape[0] * width + vectors.shape[0]) // unit) * unit
    relayed = lax.axis_size("gx") == 8 and lax.axis_size("gy") == 4
    edge_shape = (tok_rows * neighbours.shape[1] // CHUNK, CHUNK, width)
    plan = plan_call(
        halo, counts, neighbours, edge_mask, node_latents, vectors, node_cotangent, weights,
        edge_latents.reshape(edge_shape),
    )
    nodes_out, edges_out, edges_in_grad, node_part, halo_own, send, keep = layer_call(
        halo, relayed, grad_rows, ring, ring_far, ring_near, edge_cotangent.reshape(edge_shape),
        plan,
    )
    sums = sum_relayed if relayed else sum_staged
    parts, middle, last_far, last_near = sums(send, keep, halo_own, halo)
    boundary_grad = middle + last_far.astype(f32) + last_near.astype(f32)
    returned = lax.dot_general(
        boundary_pick.astype(f32),
        boundary_grad,
        (((0,), (0,)), ((), ())),
        precision=lax.Precision.HIGHEST,
        preferred_element_type=f32,
    )
    nodes_in_grad = (node_part + returned).astype(bf16)
    updated = update_call(
        relayed, parts, weights, vectors, weights_m, vectors_m, weights_v, vectors_v, weights_ema,
        vectors_ema,
    )
    return (
        nodes_out,
        edges_out.reshape(edge_latents.shape),
        nodes_in_grad,
        edges_in_grad.reshape(edge_latents.shape),
        updated[0].reshape(()),
    ) + tuple(updated[1:])


def solution(mesh):
    in_specs = (
        P(("gx", "gy"), None),
        P(("gx", "gy"), None, None),
        P(("gx", "gy"), None),
        P(("gx", "gy"), None, None),
        P(("gx", "gy"), None),
        P(("gx", "gy"), None),
        P(("gx", "gy"), None),
        P(("gx", "gy")),
        P(),
        P(),
        P(),
        P(),
        P(),
        P(),
        P(),
        P(),
    )
    out_specs = (
        P(("gx", "gy"), None),
        P(("gx", "gy"), None, None),
        P(("gx", "gy"), None),
        P(("gx", "gy"), None, None),
        P(),
        P(),
        P(),
        P(),
        P(),
        P(),
        P(),
        P(),
        P(),
        P(),
        P(),
    )
    return jax.shard_map(
        per_device, mesh=mesh, in_specs=in_specs, out_specs=out_specs, check_vma=False
    )
```
